32 devices in a mesh: gx: 4 (over x, core), bulk: 8 (over z, y).
Axes of the slice: x: 2, y: 2, z: 4, core: 2. Of those that a mesh axis runs over, the one named last changes fastest.
Arguments:
- basis: bfloat16 [8, 64, 131072], P(None, None, ('gx', 'bulk')), may hold values from -6 to 6
- near_blocks: bfloat16 [512, 8, 256, 256], P(('gx', 'bulk')), may hold values from -0.125 to 0.125
- near_src: int32 [512, 8], P(('gx', 'bulk')), may hold values from 0 to 47
- near_count: int32 [512], P(('gx', 'bulk')), may hold values from 1 to 8
- p2m: bfloat16 [512, 256, 128], P(('gx', 'bulk')), may hold values from -0.375 to 0.375
- m2l: bfloat16 [16, 128, 128], replicated, may hold values from -0.25 to 0.25
- send_list: int32 [32, 32, 4], P(('gx', 'bulk')), may hold values from 0 to 15
- send_count: int32 [32, 32], P(('gx', 'bulk')), may hold values from 0 to 4
- far_src: int32 [512, 32], P(('gx', 'bulk')), may hold values from 0 to 127
- far_class: int32 [512, 32], P(('gx', 'bulk')), may hold values from 0 to 15
Outputs:
- next_block: bfloat16 [64, 131072], P(None, ('gx', 'bulk'))
- projections: float32 [8, 64, 64], replicated
- factor: float32 [64, 64], replicated
The draws below stay inside these ranges and needn't reach their ends.
All inputs are finite; a program needn't handle non-finite values.
Results may differ from the reference program's by a relative error of at most 0.012.
Values may be sent and summed in bfloat16 or wider, within the bound.
No kernel may reach another device: no remote copies, remote signals or barrier semaphores. Data moves between devices by JAX's collectives and lax.ppermute only.
A program may use at most 128 MiB of HBM per device.

```python
import jax
import jax.numpy as jnp
from jax import lax

P_SIZE = 256
RHS = 64
Q = 128
KB = 8
CLS = 16
NB = 8
FL = 32
SLOT = 4
LDEV = 16
LEAVES = 512
ROWS = 131072
N_GX = 4
N_BULK = 8


def plant(result, rng, least, top_value):
    shape = result.shape
    place = [jax.random.randint(jax.random.fold_in(rng, axis), (), 0, shape[axis]) for axis in range(len(shape))]
    result = result.at[tuple(place)].set(least)
    longest = shape.index(max(shape))
    place[longest] = (place[longest] + 1) % shape[longest]
    return result.at[tuple(place)].set(top_value)


def levels(rng, shape, split, low, high):
    def one(position, shards_of):
        heights = jax.random.uniform(jax.random.fold_in(jax.random.fold_in(rng, 6), position), (shards_of,), jnp.float32, low / len(split), high / len(split))
        return jnp.repeat(jnp.exp(heights), shape[position] // shards_of).reshape((-1,) + (1,) * (len(shape) - position - 1))

    gain = one(*split[0])
    for cut in split[1:]:
        gain = gain * one(*cut)
    return gain


def centred(own_key, extent, spread, most, shards=(), held_as=jnp.bfloat16):
    array = jax.random.normal(own_key, extent, jnp.float32) * spread
    if len(shards) > 0:
        array = levels(own_key, extent, shards, -0.22, 0.18) * array
    return jnp.clip(array, min=-most, max=most).astype(held_as)


def setup_inputs(seed: int = 0) -> dict:
    splits = jax.random.split(jax.random.key(seed), 11)
    basis = centred(splits[0], (KB, RHS, ROWS), 1.0, 6.0, ((2, 32),))
    near_blocks = centred(splits[1], (LEAVES, NB, P_SIZE, P_SIZE), (P_SIZE * NB) ** -0.5, 0.125, ((0, 32),))
    near_src = plant(jax.random.randint(splits[2], (LEAVES, NB), 0, 3 * LDEV), jax.random.fold_in(splits[2], 1), 0, (3 * LDEV) - 1).astype(jnp.int32)
    near_count = plant(jax.random.randint(splits[3], (LEAVES,), 1, NB + 1), jax.random.fold_in(splits[3], 1), 1, NB).astype(jnp.int32)
    p2m = centred(splits[4], (LEAVES, P_SIZE, Q), P_SIZE ** -0.5, 0.375, ((0, 32),))
    m2l = centred(splits[5], (CLS, Q, Q), (4 * Q) ** -0.5, 0.25)
    send_list = plant(jax.random.randint(splits[6], (N_GX * N_BULK, N_GX * N_BULK, SLOT), 0, LDEV), jax.random.fold_in(splits[6], 1), 0, LDEV - 1).astype(jnp.int32)
    send_count = plant(jax.random.randint(splits[7], (N_GX * N_BULK, N_GX * N_BULK), 0, SLOT + 1), jax.random.fold_in(splits[7], 1), 0, SLOT).astype(jnp.int32)
    far_src = plant(jax.random.randint(splits[8], (LEAVES, FL), 0, N_GX * N_BULK * SLOT), jax.random.fold_in(splits[8], 1), 0, (N_GX * N_BULK * SLOT) - 1).astype(jnp.int32)
    far_class = plant(jax.random.randint(splits[9], (LEAVES, FL), 0, CLS), jax.random.fold_in(splits[9], 1), 0, CLS - 1).astype(jnp.int32)
    return dict(basis=basis, near_blocks=near_blocks, near_src=near_src, near_count=near_count, p2m=p2m, m2l=m2l, send_list=send_list, send_count=send_count, far_src=far_src, far_class=far_class)


def reference(basis, near_blocks, near_src, near_count, p2m, m2l, send_list, send_count, far_src, far_class):
    ndev = N_GX * N_BULK
    x = basis[KB - 1].reshape(RHS, ndev, LDEV, P_SIZE)
    xpad = jnp.pad(x, ((0, 0), (N_BULK, N_BULK), (0, 0), (0, 0)))
    blocks_dev = near_blocks.reshape(ndev, LDEV, NB, P_SIZE, P_SIZE)
    nsrc_dev = near_src.reshape(ndev, LDEV, NB)
    ncount_dev = near_count.reshape(ndev, LDEV)
    p2m_dev = p2m.reshape(ndev, LDEV, P_SIZE, Q)
    fsrc_dev = far_src.reshape(ndev, LDEV, FL)
    fcls_dev = far_class.reshape(ndev, LDEV, FL)

    def multipoles(dev):
        return jnp.einsum('rlp,lpq->lrq', x[:, dev].astype(jnp.float32), p2m_dev[dev].astype(jnp.float32)).astype(jnp.bfloat16)
    mult = lax.map(multipoles, jnp.arange(ndev, dtype=jnp.int32))

    def per_device(dev):
        window = lax.dynamic_slice_in_dim(xpad, dev, 2 * N_BULK + 1, 1)
        three = jnp.concatenate([window[:, 0], window[:, N_BULK], window[:, 2 * N_BULK]], axis=1)
        picked = jnp.take(three, nsrc_dev[dev].reshape(-1), axis=1).reshape(RHS, LDEV, NB, P_SIZE)
        live = (jnp.arange(NB, dtype=jnp.int32)[None, :] < ncount_dev[dev][:, None]).astype(jnp.float32)
        picked = picked.astype(jnp.float32) * live[None, :, :, None]
        near = jnp.einsum('rlkq,lkpq->rlp', picked, blocks_dev[dev].astype(jnp.float32))
        sender = fsrc_dev[dev] // SLOT
        slot = fsrc_dev[dev] % SLOT
        leaf = send_list[sender, dev, slot]
        valid = (slot < send_count[sender, dev]).astype(jnp.float32)
        sources = mult[sender, leaf].astype(jnp.float32) * valid[:, :, None, None]
        onehot = (fcls_dev[dev][:, :, None] == jnp.arange(CLS, dtype=jnp.int32)[None, None, :]).astype(jnp.float32)
        gathered = jnp.einsum('lec,lerq->clrq', onehot, sources).astype(jnp.bfloat16)
        local = jnp.einsum('clrq,cqs->lrs', gathered.astype(jnp.float32), m2l.astype(jnp.float32)).astype(jnp.bfloat16)
        far = jnp.einsum('lrq,lpq->rlp', local.astype(jnp.float32), p2m_dev[dev].astype(jnp.float32))
        return x[:, dev].astype(jnp.float32) + near + far
    image = lax.map(per_device, jnp.arange(ndev, dtype=jnp.int32))
    image = jnp.transpose(image, (1, 0, 2, 3)).reshape(RHS, ROWS)
    vecs = basis.astype(jnp.float32)
    hi = lax.Precision.HIGHEST
    projections = jnp.einsum('krn,sn->krs', vecs, image, precision=hi) / ROWS
    resid = image - jnp.einsum('krs,krn->sn', projections, vecs, precision=hi)
    gram = jnp.dot(resid, resid.T, precision=hi) / ROWS
    factor = jnp.linalg.cholesky(gram)
    next_block = lax.linalg.triangular_solve(factor, resid, left_side=True, lower=True).astype(jnp.bfloat16)
    return (next_block, projections, factor)
```

```python
import functools

import jax
import jax.numpy as jnp
from jax import lax
from jax.experimental import pallas as pl
from jax.experimental.pallas import tpu as pltpu
from jax.sharding import PartitionSpec as P

F32 = jnp.float32
BF16 = jnp.bfloat16
AXES = ("gx", "bulk")
HIGHEST = lax.Precision.HIGHEST
VMEM_LIMIT = 48 * 1024 * 1024


def dot(a, b, dims=((1,), (0,)), precision=None):
    return lax.dot_general(a, b, (dims, ((), ())), precision=precision, preferred_element_type=F32)


def dot_nt(a, b, precision=None):
    return dot(a, b, ((1,), (1,)), precision)


def split_parts(values):
    upper = values.astype(BF16)
    lower = (values - upper.astype(F32)).astype(BF16)
    return (upper, lower)


def params(**kwargs):
    return pltpu.CompilerParams(vmem_limit_bytes=VMEM_LIMIT, **kwargs)


def whole(shape):
    return pl.BlockSpec(shape, lambda *_: (0,) * len(shape))


def send_kernel(halves, x_ref, p2m_ref, list_ref, count_ref, out_ref, copy_ref, scratch):
    leaves, panels, terms = p2m_ref.shape
    rhs = x_ref.shape[1]
    peers, slots = list_ref.shape
    part = rhs // halves
    rows = peers * slots * halves
    copy_ref[...] = x_ref[0]
    for g in range(leaves):
        mult = dot(x_ref[0, :, g * panels : (g + 1) * panels], p2m_ref[g])
        for h in range(halves):
            scratch[:, g * halves + h, :] = mult[h * part : (h + 1) * part]
    row = lax.broadcasted_iota(jnp.int32, (rows, peers), 0) // (slots * halves)
    peer_hot = row == lax.broadcasted_iota(jnp.int32, (rows, peers), 1)
    listed = dot(peer_hot.astype(BF16), list_ref[...].astype(F32).astype(BF16))
    row_s = lax.broadcasted_iota(jnp.int32, (rows, slots), 0) // halves % slots
    lane_s = lax.broadcasted_iota(jnp.int32, (rows, slots), 1)
    leaf = jnp.sum(jnp.where(row_s == lane_s, listed, 0.0), axis=1, keepdims=True)
    counts = jnp.broadcast_to(count_ref[...].astype(F32), (rows, peers))
    live = jnp.sum(jnp.where(peer_hot, counts, 0.0), axis=1, keepdims=True)
    row_k = lax.broadcasted_iota(jnp.int32, (rows, leaves * halves), 0)
    lane_k = lax.broadcasted_iota(jnp.int32, (rows, leaves * halves), 1)
    half = row_k % halves
    slot = (row_k // halves % slots).astype(F32)
    wanted = leaf * halves + half.astype(F32)
    chosen = ((lane_k.astype(F32) == wanted) & (slot < live)).astype(F32).astype(BF16)
    for j in range(part // 2):
        pair = jnp.concatenate([scratch[2 * j], scratch[2 * j + 1]], axis=1).astype(BF16)
        out_ref[:, j * 2 * terms : (j + 1) * 2 * terms] = dot(chosen, pair).astype(BF16)


def sent_multipoles(basis, p2m, send_list, send_count, halves):
    blocks, rhs, columns = basis.shape
    leaves, panels, terms = p2m.shape
    peers, slots = send_list.shape
    rows, width = peers * slots * halves, rhs // halves * terms
    return pl.pallas_call(
        functools.partial(send_kernel, halves),
        grid=(1,),
        out_shape=(
            jax.ShapeDtypeStruct((rows, width), BF16),
            jax.ShapeDtypeStruct((rhs, columns), BF16),
        ),
        in_specs=[
            pl.BlockSpec((1, rhs, columns), lambda i: (blocks - 1, 0, 0)),
            whole(p2m.shape),
            whole(send_list.shape),
            whole(send_count.shape),
        ],
        out_specs=(whole((rows, width)), whole((rhs, columns))),
        scratch_shapes=[pltpu.VMEM((rhs // halves, leaves * halves, terms), F32)],
        compiler_params=params(),
        name="send",
    )(basis, p2m, send_list, send_count)


def basis_gram_kernel(v_ref, out_ref):
    blocks, rhs, width = v_ref.shape
    half = blocks * rhs // 2
    v = v_ref[...].reshape(2 * half, width)
    top, bottom = v[:half], v[half:]

    @pl.when(pl.program_id(0) == 0)
    def _():
        out_ref[...] = jnp.zeros_like(out_ref)

    out_ref[0] += dot_nt(top, top)
    out_ref[1] += dot_nt(top, bottom)
    out_ref[2] += dot_nt(bottom, bottom)


def basis_grams(basis, steps):
    blocks, rhs, columns = basis.shape
    half = blocks * rhs // 2
    return pl.pallas_call(
        basis_gram_kernel,
        grid=(steps,),
        out_shape=jax.ShapeDtypeStruct((3, half, half), F32),
        in_specs=[pl.BlockSpec((blocks, rhs, columns // steps), lambda i: (0, 0, i))],
        out_specs=whole((3, half, half)),
        compiler_params=params(),
        cost_estimate=pl.CostEstimate(
            flops=6 * half * half * columns,
            bytes_accessed=basis.size * 2 + 12 * half * half,
            transcendentals=0,
        ),
        name="basis_gram",
    )(basis)


def near_kernel(src_ref, count_ref, before, own, after, blocks_ref, out_ref, wide):
    columns = own.shape[1]
    slots, panels = blocks_ref.shape[1], blocks_ref.shape[2]
    g = pl.program_id(0)

    @pl.when(g == 0)
    def _():
        wide[:, :columns] = before[...]
        wide[:, columns : 2 * columns] = own[...]
        wide[:, 2 * columns :] = after[...]

    here = pl.ds(pl.multiple_of(columns + g * panels, panels), panels)
    total = wide[:, here].astype(F32)
    for k in range(slots):
        place = pl.multiple_of(src_ref[g, k] * panels, panels)
        source = wide[:, pl.ds(place, panels)]
        source = jnp.where(k < count_ref[g], source, jnp.zeros_like(source))
        total += dot_nt(source, blocks_ref[0, k])
    out_ref[...] = total


def near_field(near_src, near_count, before, own, after, near_blocks):
    leaves, slots, panels, _ = near_blocks.shape
    rhs, columns = own.shape
    grid_spec = pltpu.PrefetchScalarGridSpec(
        num_scalar_prefetch=2,
        grid=(leaves,),
        in_specs=[
            whole((rhs, columns)),
            whole((rhs, columns)),
            whole((rhs, columns)),
            pl.BlockSpec((1, slots, panels, panels), lambda g, *_: (g, 0, 0, 0)),
        ],
        out_specs=pl.BlockSpec((rhs, panels), lambda g, *_: (0, g)),
        scratch_shapes=[pltpu.VMEM((rhs, 3 * columns), BF16)],
    )
    return pl.pallas_call(
        near_kernel,
        grid_spec=grid_spec,
        out_shape=jax.ShapeDtypeStruct((rhs, columns), F32),
        compiler_params=params(),
        cost_estimate=pl.CostEstimate(
            flops=2 * rhs * near_blocks.size,
            bytes_accessed=near_blocks.size * 2 + 7 * rhs * columns * 2,
            transcendentals=0,
        ),
        name="near",
    )(near_src, near_count, before, own, after, near_blocks)


def far_kernel(halves, peers, recv, pick, m2l, p2m, near, basis, image_ref, sums_ref, lhs, loc):
    leaves, panels, terms = p2m.shape
    classes = m2l.shape[0]
    blocks, rhs, columns = basis.shape
    part = rhs // halves
    for h in range(halves):

        def step(j, carry, h=h):
            lanes = pl.ds(pl.multiple_of(j * 2 * terms, 2 * terms), 2 * terms)
            got = dot(pick[h], recv[:, lanes]).astype(BF16)
            base = pl.multiple_of((h * part + 2 * j) * leaves, 2 * leaves)
            for t in range(2):
                for c in range(classes):
                    lhs[pl.ds(base + t * leaves, leaves), c * terms : (c + 1) * terms] = got[
                        c * leaves : (c + 1) * leaves, t * terms : (t + 1) * terms
                    ]
            return carry

        lax.fori_loop(0, part // 2, step, 0)
    weights = m2l[...].reshape(classes * terms, terms)
    tall = 256
    for i in range(rhs * leaves // tall):
        got = dot(lhs[i * tall : (i + 1) * tall, :], weights)
        loc[i * tall // leaves : (i + 1) * tall // leaves] = got.reshape(
            tall // leaves, leaves, terms
        )
    inner = jnp.zeros((2 * rhs, blocks * rhs), F32)
    square = jnp.zeros((2 * rhs, 2 * rhs), F32)
    for g in range(leaves):
        cols = slice(g * panels, (g + 1) * panels)
        far = dot_nt(loc[:, g, :].astype(BF16), p2m[g])
        image = near[:, cols] + far
        image_ref[:, cols] = image
        both = jnp.concatenate(split_parts(image), axis=0)
        inner += dot_nt(both, basis[:, :, cols].reshape(blocks * rhs, panels))
        square += dot_nt(both, both)
    products = inner[:rhs] + inner[rhs:]
    ww = square[:rhs, :rhs] + square[:rhs, rhs:] + square[rhs:, :rhs] + square[rhs:, rhs:]
    pack(products, ww, sums_ref)


def pack_sizes(rhs, wide, peers):
    rows = rhs * wide // 128 // peers
    return rows, -(-(rows + 1) // 8) * 8


def pack(products, ww, out_ref):
    peers, _, lanes = out_ref.shape
    rhs, wide = products.shape
    rows, _ = pack_sizes(rhs, wide, peers)
    out_ref[...] = jnp.zeros_like(out_ref)
    tall = jnp.concatenate(
        [products[:, i * lanes : (i + 1) * lanes] for i in range(wide // lanes)], axis=0
    )
    for p in range(peers):
        out_ref[p, :rows, :] = tall[p * rows : (p + 1) * rows]
    half = rhs // 2
    folded = jnp.concatenate([ww[:half], ww[half:]], axis=1)
    for i in range(half):
        out_ref[i, rows : rows + 1, :] = folded[i : i + 1]


def unpack(in_ref, rhs, wide):
    peers, _, lanes = in_ref.shape
    rows, _ = pack_sizes(rhs, wide, peers)
    tall = jnp.concatenate([in_ref[p, :rows, :] for p in range(peers)], axis=0)
    products = jnp.concatenate(
        [tall[i * rhs : (i + 1) * rhs] for i in range(wide // lanes)], axis=1
    )
    half = rhs // 2
    folded = jnp.concatenate([in_ref[i, rows : rows + 1, :] for i in range(half)], axis=0)
    ww = jnp.concatenate([folded[:, :rhs], folded[:, rhs:]], axis=0)
    return products, ww


def far_field(recv, pick, m2l, p2m, near, basis, halves, peers):
    leaves, panels, terms = p2m.shape
    classes = m2l.shape[0]
    blocks, rhs, columns = basis.shape
    _, piece = pack_sizes(rhs, blocks * rhs, peers)
    args = (recv, pick, m2l, p2m, near, basis)
    return pl.pallas_call(
        functools.partial(far_kernel, halves, peers),
        grid=(1,),
        out_shape=(
            jax.ShapeDtypeStruct((rhs, columns), F32),
            jax.ShapeDtypeStruct((peers, piece, 128), F32),
        ),
        in_specs=[whole(a.shape) for a in args],
        out_specs=(whole((rhs, columns)), whole((peers, piece, 128))),
        scratch_shapes=[
            pltpu.VMEM((rhs * leaves, classes * terms), BF16),
            pltpu.VMEM((rhs, leaves, terms), F32),
        ],
        compiler_params=params(),
        name="far",
    )(*args)


def add_kernel(in_ref, out_ref):
    total = jnp.sum(in_ref[...], axis=0)
    out_ref[...] = jnp.broadcast_to(total[None], out_ref.shape)


def all_sum(pieces):
    got = lax.all_to_all(pieces, AXES, split_axis=0, concat_axis=0, tiled=True)
    added = pl.pallas_call(
        add_kernel,
        grid=(1,),
        out_shape=jax.ShapeDtypeStruct(pieces.shape, F32),
        in_specs=[whole(pieces.shape)],
        out_specs=whole(pieces.shape),
        compiler_params=params(),
        name="add",
    )(got)
    return lax.all_to_all(added, AXES, split_axis=0, concat_axis=0, tiled=True)


def factored(gram):
    size = gram.shape[0]
    rows = lax.broadcasted_iota(jnp.int32, (size, size), 0)
    cols = lax.broadcasted_iota(jnp.int32, (size, size), 1)
    eye = (rows == cols).astype(F32)
    both = jnp.concatenate([gram, eye], axis=1)
    tiles = [both[8 * i : 8 * i + 8] for i in range(size // 8)]
    sub = lax.broadcasted_iota(jnp.int32, (8, 2 * size), 0)
    for j in range(size):
        t, o = divmod(j, 8)
        row = tiles[t][o : o + 1]
        pivot = 1.0 / row[:, j : j + 1]
        scaled = row * pivot
        for i in range(t, size // 8):
            column = tiles[i][:, j : j + 1]
            change = column * scaled
            if i == t:
                change = jnp.where(sub > o, change, 0.0)
            tiles[i] = tiles[i] - change
    both = jnp.concatenate(tiles, axis=0)
    pivots = jnp.sum(both[:, :size] * eye, axis=1, keepdims=True)
    both = both * (1.0 / jnp.sqrt(pivots))
    upper = jnp.where(cols >= rows, both[:, :size], 0.0)
    return upper.T, both[:, size:]


def tail_kernel(total_rows, sums, grams, basis, image, next_ref, proj_ref, factor_ref, coef):
    blocks, rhs, width = basis.shape
    wide = blocks * rhs

    @pl.when(pl.program_id(0) == 0)
    def _():
        products, ww = unpack(sums, rhs, wide)
        proj = products * (1.0 / total_rows)
        half = wide // 2
        left, right = proj[:, :half], proj[:, half:]
        scale = 1.0 / total_rows
        g00, g01, g11 = grams[0] * scale, grams[1] * scale, grams[2] * scale
        first = dot(left, g00, precision=HIGHEST) + dot_nt(right, g01, HIGHEST) - 2.0 * left
        second = dot(left, g01, precision=HIGHEST) + dot(right, g11, precision=HIGHEST)
        second = second - 2.0 * right
        gram = ww * scale + dot_nt(first, left, HIGHEST) + dot_nt(second, right, HIGHEST)
        lower, inverse = factored(gram)
        factor_ref[...] = lower
        proj_ref[...] = proj.T
        mixed = dot(inverse, proj, precision=HIGHEST)
        coef[:rhs, :wide], coef[rhs:, :wide] = split_parts(-mixed)
        coef[:rhs, wide : wide + rhs], coef[rhs:, wide : wide + rhs] = split_parts(inverse)

    upper, lower = split_parts(image[...])
    by_basis = dot(coef[:, :wide], basis[...].reshape(wide, width))
    by_image = dot(coef[:, wide : wide + rhs], upper)
    rest = dot(coef[:rhs, wide : wide + rhs], lower)
    total = by_basis + by_image
    next_ref[...] = (total[:rhs] + total[rhs:] + rest).astype(BF16)


def tail(sums, grams, basis, image, total_rows, steps):
    blocks, rhs, columns = basis.shape
    width = columns // steps
    return pl.pallas_call(
        functools.partial(tail_kernel, total_rows),
        grid=(steps,),
        out_shape=(
            jax.ShapeDtypeStruct((rhs, columns), BF16),
            jax.ShapeDtypeStruct((blocks * rhs, rhs), F32),
            jax.ShapeDtypeStruct((rhs, rhs), F32),
        ),
        in_specs=[
            whole(sums.shape),
            whole(grams.shape),
            pl.BlockSpec((blocks, rhs, width), lambda i: (0, 0, i)),
            pl.BlockSpec((rhs, width), lambda i: (0, i)),
        ],
        out_specs=(
            pl.BlockSpec((rhs, width), lambda i: (0, i)),
            whole((blocks * rhs, rhs)),
            whole((rhs, rhs)),
        ),
        scratch_shapes=[pltpu.VMEM((2 * rhs, blocks * rhs + 128), BF16)],
        compiler_params=params(),
        name="tail",
    )(sums, grams, basis, image)


def shards(
    basis, near_blocks, near_src, near_count, p2m, m2l, send_list, send_count, far_src, far_class
):
    blocks, rhs, columns = basis.shape
    leaves = near_src.shape[0]
    classes, terms, _ = m2l.shape
    devices = lax.axis_size("gx")
    peers = devices * lax.axis_size("bulk")
    slots = send_list.shape[2]
    total_rows = columns * peers
    halves = 2

    sent, own = sent_multipoles(basis, p2m, send_list[0], send_count, halves)
    sent = sent.reshape(peers, slots * halves, sent.shape[1])
    received = lax.all_to_all(sent, AXES, split_axis=0, concat_axis=0, tiled=True)
    received = received.reshape(peers * slots * halves, received.shape[2])

    up = [(i, i + 1) for i in range(devices - 1)]
    down = [(j, i) for i, j in up]
    before = lax.ppermute(own, "gx", up)
    after = lax.ppermute(own, "gx", down)

    grams = lax.psum(basis_grams(basis, 4), AXES)
    near = near_field(near_src, near_count, before, own, after, near_blocks)

    class_hot = (far_class[:, None, :] == jnp.arange(classes)[None, :, None]).astype(BF16)
    rows = jnp.arange(peers * slots * halves)[None, None, None, :]
    wanted = far_src[None, :, :, None] * halves + jnp.arange(halves)[:, None, None, None]
    source_hot = (wanted == rows).astype(BF16)
    pick = jnp.einsum("gce,hgef->hcgf", class_hot, source_hot, preferred_element_type=F32)
    pick = pick.astype(BF16).reshape(halves, classes * leaves, -1)

    image, sums = far_field(received, pick, m2l, p2m, near, basis, halves, peers)
    sums = all_sum(sums)
    next_block, projections, factor = tail(sums, grams, basis, image, total_rows, 4)
    return (next_block, projections.reshape(blocks, rhs, rhs), factor)


def solution(mesh):
    return jax.shard_map(
        shards,
        mesh=mesh,
        in_specs=(
            P(None, None, AXES),
            P(AXES, None, None, None),
            P(AXES, None),
            P(AXES),
            P(AXES, None, None),
            P(),
            P(AXES, None, None),
            P(AXES, None),
            P(AXES, None),
            P(AXES, None),
        ),
        out_specs=(P(None, AXES), P(), P()),
        check_vma=False,
    )
```

```python
import functools

import jax
import jax.numpy as jnp
from jax import lax
from jax.experimental import pallas as pl
from jax.experimental.pallas import tpu as pltpu
from jax.sharding import PartitionSpec as P

F32 = jnp.float32
BF16 = jnp.bfloat16
AXES = ("gx", "bulk")
HIGHEST = lax.Precision.HIGHEST
VMEM_LIMIT = 36 * 1024 * 1024


def dot(a, b, dims=((1,), (0,)), precision=None):
    return lax.dot_general(a, b, (dims, ((), ())), precision=precision, preferred_element_type=F32)


def dot_nt(a, b, precision=None):
    return dot(a, b, ((1,), (1,)), precision)


def split_parts(values):
    upper = values.astype(BF16)
    lower = (values - upper.astype(F32)).astype(BF16)
    return (upper, lower)


def params(**kwargs):
    return pltpu.CompilerParams(vmem_limit_bytes=VMEM_LIMIT, **kwargs)


def whole(shape):
    return pl.BlockSpec(shape, lambda *_: (0,) * len(shape))


def send_kernel(halves, x_ref, p2m_ref, list_ref, count_ref, out_ref, copy_ref, scratch):
    leaves, panels, terms = p2m_ref.shape
    rhs = x_ref.shape[1]
    peers, slots = list_ref.shape
    part = rhs // halves
    rows = peers * slots * halves
    copy_ref[...] = x_ref[0]
    for g in range(leaves):
        mult = dot(x_ref[0, :, g * panels : (g + 1) * panels], p2m_ref[g])
        for h in range(halves):
            scratch[:, g * halves + h, :] = mult[h * part : (h + 1) * part]
    row = lax.broadcasted_iota(jnp.int32, (rows, peers), 0) // (slots * halves)
    peer_hot = row == lax.broadcasted_iota(jnp.int32, (rows, peers), 1)
    listed = dot(peer_hot.astype(BF16), list_ref[...].astype(F32).astype(BF16))
    row_s = lax.broadcasted_iota(jnp.int32, (rows, slots), 0) // halves % slots
    lane_s = lax.broadcasted_iota(jnp.int32, (rows, slots), 1)
    leaf = jnp.sum(jnp.where(row_s == lane_s, listed, 0.0), axis=1, keepdims=True)
    counts = jnp.broadcast_to(count_ref[...].astype(F32), (rows, peers))
    live = jnp.sum(jnp.where(peer_hot, counts, 0.0), axis=1, keepdims=True)
    row_k = lax.broadcasted_iota(jnp.int32, (rows, leaves * halves), 0)
    lane_k = lax.broadcasted_iota(jnp.int32, (rows, leaves * halves), 1)
    half = row_k % halves
    slot = (row_k // halves % slots).astype(F32)
    wanted = leaf * halves + half.astype(F32)
    chosen = ((lane_k.astype(F32) == wanted) & (slot < live)).astype(F32).astype(BF16)
    for j in range(part // 2):
        pair = jnp.concatenate([scratch[2 * j], scratch[2 * j + 1]], axis=1).astype(BF16)
        out_ref[:, j * 2 * terms : (j + 1) * 2 * terms] = dot(chosen, pair).astype(BF16)


def sent_multipoles(basis, p2m, send_list, send_count, halves):
    blocks, rhs, columns = basis.shape
    leaves, panels, terms = p2m.shape
    peers, slots = send_list.shape
    rows, width = peers * slots * halves, rhs // halves * terms
    return pl.pallas_call(
        functools.partial(send_kernel, halves),
        grid=(1,),
        out_shape=(
            jax.ShapeDtypeStruct((rows, width), BF16),
            jax.ShapeDtypeStruct((rhs, columns), BF16),
        ),
        in_specs=[
            pl.BlockSpec((1, rhs, columns), lambda i: (blocks - 1, 0, 0)),
            whole(p2m.shape),
            whole(send_list.shape),
            whole(send_count.shape),
        ],
        out_specs=(whole((rows, width)), whole((rhs, columns))),
        scratch_shapes=[pltpu.VMEM((rhs // halves, leaves * halves, terms), F32)],
        compiler_params=params(),
        name="send",
    )(basis, p2m, send_list, send_count)


def near_kernel(src_ref, count_ref, before, own, after, blocks_ref, out_ref, wide):
    columns = own.shape[1]
    slots, panels = blocks_ref.shape[1], blocks_ref.shape[2]
    g = pl.program_id(0)

    @pl.when(g == 0)
    def _():
        wide[:, :columns] = before[...]
        wide[:, columns : 2 * columns] = own[...]
        wide[:, 2 * columns :] = after[...]

    here = pl.ds(pl.multiple_of(columns + g * panels, panels), panels)
    total = wide[:, here].astype(F32)
    for k in range(slots):
        place = pl.multiple_of(src_ref[g, k] * panels, panels)
        source = wide[:, pl.ds(place, panels)]
        source = jnp.where(k < count_ref[g], source, jnp.zeros_like(source))
        total += dot_nt(source, blocks_ref[0, k])
    out_ref[...] = total


def near_field(near_src, near_count, before, own, after, near_blocks):
    leaves, slots, panels, _ = near_blocks.shape
    rhs, columns = own.shape
    grid_spec = pltpu.PrefetchScalarGridSpec(
        num_scalar_prefetch=2,
        grid=(leaves,),
        in_specs=[
            whole((rhs, columns)),
            whole((rhs, columns)),
            whole((rhs, columns)),
            pl.BlockSpec((1, slots, panels, panels), lambda g, *_: (g, 0, 0, 0)),
        ],
        out_specs=pl.BlockSpec((rhs, panels), lambda g, *_: (0, g)),
        scratch_shapes=[pltpu.VMEM((rhs, 3 * columns), BF16)],
    )
    return pl.pallas_call(
        near_kernel,
        grid_spec=grid_spec,
        out_shape=jax.ShapeDtypeStruct((rhs, columns), F32),
        compiler_params=params(),
        cost_estimate=pl.CostEstimate(
            flops=2 * rhs * near_blocks.size,
            bytes_accessed=near_blocks.size * 2 + 7 * rhs * columns * 2,
            transcendentals=0,
        ),
        name="near",
    )(near_src, near_count, before, own, after, near_blocks)


def far_kernel(halves, recv, pick, m2l, p2m, near, basis, image_ref, sums_ref, lhs, loc, both):
    leaves, panels, terms = p2m.shape
    classes = m2l.shape[0]
    blocks, rhs, columns = basis.shape
    part = rhs // halves
    group = 8
    for h in range(halves):
        for j in range(0, part, group):
            got = dot(pick[h], recv[:, j * terms : (j + group) * terms]).astype(BF16)
            for t in range(group):
                base = (h * part + j + t) * leaves
                for c in range(classes):
                    lhs[base : base + leaves, c * terms : (c + 1) * terms] = got[
                        c * leaves : (c + 1) * leaves, t * terms : (t + 1) * terms
                    ]
    weights = m2l[...].reshape(classes * terms, terms)
    tall = 256
    for i in range(rhs * leaves // tall):
        got = dot(lhs[i * tall : (i + 1) * tall, :], weights)
        loc[i * tall // leaves : (i + 1) * tall // leaves] = got.reshape(
            tall // leaves, leaves, terms
        )
    for g in range(leaves):
        cols = slice(g * panels, (g + 1) * panels)
        image = near[:, cols] + dot_nt(loc[:, g, :].astype(BF16), p2m[g])
        image_ref[:, cols] = image
        both[:rhs, cols], both[rhs:, cols] = split_parts(image)
    inner = dot_nt(both[...], basis[...].reshape(blocks * rhs, columns))
    pack(inner[:rhs] + inner[rhs:], sums_ref)


def pack_sizes(rhs, wide, peers):
    rows = rhs * wide // 128 // peers
    return rows, -(-rows // 8) * 8


def pack(products, out_ref):
    peers, piece, lanes = out_ref.shape
    rhs, wide = products.shape
    rows, _ = pack_sizes(rhs, wide, peers)
    if rows < piece:
        out_ref[...] = jnp.zeros_like(out_ref)
    tall = jnp.concatenate(
        [products[:, i * lanes : (i + 1) * lanes] for i in range(wide // lanes)], axis=0
    )
    for p in range(peers):
        out_ref[p, :rows, :] = tall[p * rows : (p + 1) * rows]


def unpack(in_ref, rhs, wide):
    peers, _, lanes = in_ref.shape
    rows, _ = pack_sizes(rhs, wide, peers)
    tall = jnp.concatenate([in_ref[p, :rows, :] for p in range(peers)], axis=0)
    return jnp.concatenate(
        [tall[i * rhs : (i + 1) * rhs] for i in range(wide // lanes)], axis=1
    )


def far_field(recv, pick, m2l, p2m, near, basis, halves, peers):
    leaves, panels, terms = p2m.shape
    classes = m2l.shape[0]
    blocks, rhs, columns = basis.shape
    _, piece = pack_sizes(rhs, blocks * rhs, peers)
    args = (recv, pick, m2l, p2m, near, basis)
    return pl.pallas_call(
        functools.partial(far_kernel, halves),
        grid=(1,),
        out_shape=(
            jax.ShapeDtypeStruct((rhs, columns), F32),
            jax.ShapeDtypeStruct((peers, piece, 128), F32),
        ),
        in_specs=[whole(a.shape) for a in args],
        out_specs=(whole((rhs, columns)), whole((peers, piece, 128))),
        scratch_shapes=[
            pltpu.VMEM((rhs * leaves, classes * terms), BF16),
            pltpu.VMEM((rhs, leaves, terms), F32),
            pltpu.VMEM((2 * rhs, columns), BF16),
        ],
        compiler_params=params(),
        name="far",
    )(*args)


def exchange(pieces):
    return lax.all_to_all(pieces, AXES, split_axis=0, concat_axis=0, tiled=True)


def add_kernel(in_ref, out_ref):
    total = jnp.sum(in_ref[...], axis=0)
    out_ref[...] = jnp.broadcast_to(total[None], out_ref.shape)


def all_sum(pieces):
    got = exchange(pieces)
    added = pl.pallas_call(
        add_kernel,
        grid=(1,),
        out_shape=jax.ShapeDtypeStruct(pieces.shape, F32),
        in_specs=[whole(pieces.shape)],
        out_specs=whole(pieces.shape),
        compiler_params=params(),
        name="add",
    )(got)
    return exchange(added)


def resid_kernel(total_rows, sums, basis, image, resid_ref, gram_ref, proj_ref):
    blocks, rhs, columns = basis.shape
    wide = blocks * rhs
    proj = unpack(sums, rhs, wide) * (1.0 / total_rows)
    proj_ref[...] = proj.T
    coef = jnp.concatenate(split_parts(proj), axis=0)
    step = 1024
    for i in range(columns // step):
        cols = slice(i * step, (i + 1) * step)
        by_basis = dot(coef, basis[:, :, cols].reshape(wide, step))
        resid = image[:, cols] - (by_basis[:rhs] + by_basis[rhs:])
        resid_ref[:rhs, cols], resid_ref[rhs:, cols] = split_parts(resid)
    both = resid_ref[...]
    square = dot_nt(both, both)
    gram = square[:rhs, :rhs] + square[:rhs, rhs:] + square[rhs:, :rhs] + square[rhs:, rhs:]
    half = rhs // 2
    folded = jnp.concatenate([gram[:half], gram[half:]], axis=1) * (1.0 / total_rows)
    gram_ref[...] = jnp.broadcast_to(folded[None], gram_ref.shape)


def residual(sums, basis, image, total_rows):
    blocks, rhs, columns = basis.shape
    peers = sums.shape[0]
    args = (sums, basis, image)
    shapes = (
        jax.ShapeDtypeStruct((2 * rhs, columns), BF16),
        jax.ShapeDtypeStruct((peers, rhs // 2, 2 * rhs), F32),
        jax.ShapeDtypeStruct((blocks * rhs, rhs), F32),
    )
    return pl.pallas_call(
        functools.partial(resid_kernel, total_rows),
        grid=(1,),
        out_shape=shapes,
        in_specs=[whole(a.shape) for a in args],
        out_specs=tuple(whole(s.shape) for s in shapes),
        compiler_params=params(),
        name="residual",
    )(*args)


def factored(gram):
    size = gram.shape[0]
    rows = lax.broadcasted_iota(jnp.int32, (size, size), 0)
    cols = lax.broadcasted_iota(jnp.int32, (size, size), 1)
    eye = (rows == cols).astype(F32)
    both = jnp.concatenate([gram, eye], axis=1)
    tiles = [both[8 * i : 8 * i + 8] for i in range(size // 8)]
    sub = lax.broadcasted_iota(jnp.int32, (8, 2 * size), 0)
    for j in range(size):
        t, o = divmod(j, 8)
        row = tiles[t][o : o + 1]
        pivot = 1.0 / row[:, j : j + 1]
        scaled = row * pivot
        for i in range(t, size // 8):
            column = tiles[i][:, j : j + 1]
            change = column * scaled
            if i == t:
                change = jnp.where(sub > o, change, 0.0)
            tiles[i] = tiles[i] - change
    both = jnp.concatenate(tiles, axis=0)
    pivots = jnp.sum(both[:, :size] * eye, axis=1, keepdims=True)
    both = both * (1.0 / jnp.sqrt(pivots))
    upper = jnp.where(cols >= rows, both[:, :size], 0.0)
    return upper.T, both[:, size:]


def tail_kernel(grams, resid, next_ref, factor_ref):
    rhs = factor_ref.shape[0]
    columns = resid.shape[1]
    folded = jnp.sum(grams[...], axis=0)
    gram = jnp.concatenate([folded[:, :rhs], folded[:, rhs:]], axis=0)
    lower, inverse = factored(gram)
    factor_ref[...] = lower
    coef = jnp.concatenate(split_parts(inverse), axis=0)
    step = 1024
    for i in range(columns // step):
        cols = slice(i * step, (i + 1) * step)
        first = dot(coef, resid[:rhs, cols])
        second = dot(coef[:rhs], resid[rhs:, cols])
        next_ref[:, cols] = (first[:rhs] + first[rhs:] + second).astype(BF16)


def tail(grams, resid):
    rhs, columns = resid.shape[0] // 2, resid.shape[1]
    args = (grams, resid)
    shapes = (
        jax.ShapeDtypeStruct((rhs, columns), BF16),
        jax.ShapeDtypeStruct((rhs, rhs), F32),
    )
    return pl.pallas_call(
        tail_kernel,
        grid=(1,),
        out_shape=shapes,
        in_specs=[whole(a.shape) for a in args],
        out_specs=tuple(whole(s.shape) for s in shapes),
        compiler_params=params(),
        name="tail",
    )(*args)


def shards(
    basis, near_blocks, near_src, near_count, p2m, m2l, send_list, send_count, far_src, far_class
):
    blocks, rhs, columns = basis.shape
    leaves = near_src.shape[0]
    classes, terms, _ = m2l.shape
    devices = lax.axis_size("gx")
    peers = devices * lax.axis_size("bulk")
    slots = send_list.shape[2]
    total_rows = columns * peers
    halves = 2

    sent, own = sent_multipoles(basis, p2m, send_list[0], send_count, halves)
    sent = sent.reshape(peers, slots * halves, sent.shape[1])
    received = exchange(sent).reshape(peers * slots * halves, sent.shape[2])

    up = [(i, i + 1) for i in range(devices - 1)]
    down = [(j, i) for i, j in up]
    before = lax.ppermute(own, "gx", up)
    after = lax.ppermute(own, "gx", down)

    near = near_field(near_src, near_count, before, own, after, near_blocks)

    class_hot = (far_class[:, None, :] == jnp.arange(classes)[None, :, None]).astype(BF16)
    rows = jnp.arange(peers * slots * halves)[None, None, None, :]
    wanted = far_src[None, :, :, None] * halves + jnp.arange(halves)[:, None, None, None]
    source_hot = (wanted == rows).astype(BF16)
    pick = jnp.einsum("gce,hgef->hcgf", class_hot, source_hot, preferred_element_type=F32)
    pick = pick.astype(BF16).reshape(halves, classes * leaves, -1)

    image, sums = far_field(received, pick, m2l, p2m, near, basis, halves, peers)
    sums = all_sum(sums)
    resid, grams, projections = residual(sums, basis, image, total_rows)
    next_block, factor = tail(exchange(grams), resid)
    return (next_block, projections.reshape(blocks, rhs, rhs), factor)


def solution(mesh):
    return jax.shard_map(
        shards,
        mesh=mesh,
        in_specs=(
            P(None, None, AXES),
            P(AXES, None, None, None),
            P(AXES, None),
            P(AXES),
            P(AXES, None, None),
            P(),
            P(AXES, None, None),
            P(AXES, None),
            P(AXES, None),
            P(AXES, None),
        ),
        out_specs=(P(None, AXES), P(), P()),
        check_vma=False,
    )
```

```python
import functools

import jax
import jax.numpy as jnp
from jax import lax
from jax.experimental import pallas as pl
from jax.experimental.pallas import tpu as pltpu
from jax.sharding import PartitionSpec as P

F32 = jnp.float32
BF16 = jnp.bfloat16
AXES = ("gx", "hi", "lo")
MIB = 1024 * 1024


def dot(a, b, dims=((1,), (0,)), precision=None):
    return lax.dot_general(a, b, (dims, ((), ())), precision=precision, preferred_element_type=F32)


def dot_nt(a, b, precision=None):
    return dot(a, b, ((1,), (1,)), precision)


def split_parts(values):
    upper = values.astype(BF16)
    lower = (values - upper.astype(F32)).astype(BF16)
    return (upper, lower)


def params(mib):
    return pltpu.CompilerParams(vmem_limit_bytes=mib * MIB)


def in_hbm(array):
    return pltpu.with_memory_space_constraint(array, pltpu.HBM)


def whole(shape):
    return pl.BlockSpec(shape, lambda *_: (0,) * len(shape))


def chosen_rows(listing, leaves, slots, halves):
    receivers = listing.shape[0]
    rows = receivers * slots * halves
    row = lax.broadcasted_iota(jnp.int32, (rows, receivers), 0) // (slots * halves)
    hot = row == lax.broadcasted_iota(jnp.int32, (rows, receivers), 1)
    spread = dot(hot.astype(F32).astype(BF16), listing)
    row = lax.broadcasted_iota(jnp.int32, spread.shape, 0)
    lane = lax.broadcasted_iota(jnp.int32, spread.shape, 1)
    slot = row // halves % slots
    leaf = jnp.sum(jnp.where(lane == slot, spread, 0.0), axis=1, keepdims=True)
    live = jnp.sum(jnp.where(lane == slots, spread, 0.0), axis=1, keepdims=True)
    row = lax.broadcasted_iota(jnp.int32, (rows, leaves * halves), 0)
    lane = lax.broadcasted_iota(jnp.int32, (rows, leaves * halves), 1)
    wanted = leaf * halves + (row % halves).astype(F32)
    held = (row // halves % slots).astype(F32) < live
    return ((lane.astype(F32) == wanted) & held).astype(F32).astype(BF16)


def one_side(listing, side, near_devices):
    peers = listing.shape[0]
    rows = lax.broadcasted_iota(jnp.int32, (peers // 2, peers), 0)
    wanted = rows // near_devices * (2 * near_devices) + side * near_devices + rows % near_devices
    hot = wanted == lax.broadcasted_iota(jnp.int32, (peers // 2, peers), 1)
    return dot(hot.astype(F32).astype(BF16), listing).astype(BF16)


def send_kernel(halves, slots, near_devices, side, x, p2m, listing, out, whole_out, own, scratch):
    leaves, panels, terms = p2m.shape
    rhs = x.shape[1]
    part = rhs // halves
    own[...] = x[0]
    for g in range(leaves):
        mult = dot(x[0, :, g * panels : (g + 1) * panels], p2m[g])
        for h in range(halves):
            scratch[:, g * halves + h, :] = mult[h * part : (h + 1) * part]
    lists = listing[...]
    chosen = chosen_rows(one_side(lists, side[0], near_devices), leaves, slots, halves)
    tall = leaves * halves
    for j in range(part // 2):
        first, second = scratch[2 * j].astype(BF16), scratch[2 * j + 1].astype(BF16)
        whole_out[2 * j * tall : (2 * j + 1) * tall, :] = first
        whole_out[(2 * j + 1) * tall : (2 * j + 2) * tall, :] = second
        pair = jnp.concatenate([first, second], axis=1)
        out[:, j * 2 * terms : (j + 1) * 2 * terms] = dot(chosen, pair).astype(BF16)
    whole_out[part * tall :, :] = one_side(lists, 1 - side[0], near_devices)


def relay_kernel(halves, slots, leaves, given, out):
    tall, terms = leaves * halves, given.shape[1]
    part = out.shape[1] // terms
    chosen = chosen_rows(given[part * tall :, :], leaves, slots, halves)
    for j in range(part // 2):
        rows = [given[i * tall : (i + 1) * tall, :] for i in (2 * j, 2 * j + 1)]
        pair = jnp.concatenate(rows, axis=1)
        out[:, j * 2 * terms : (j + 1) * 2 * terms] = dot(chosen, pair).astype(BF16)


def sent_multipoles(side, basis, p2m, listing, slots, halves):
    blocks, rhs, columns = basis.shape
    leaves, panels, terms = p2m.shape
    peers = listing.shape[0]
    rows, width = peers // 2 * slots * halves, rhs // halves * terms
    shapes = (
        jax.ShapeDtypeStruct((rows, width), BF16),
        jax.ShapeDtypeStruct((rhs * leaves + peers // 2, terms), BF16),
        jax.ShapeDtypeStruct((rhs, columns), BF16),
    )
    return pl.pallas_call(
        functools.partial(send_kernel, halves, slots, lax.axis_size("lo")),
        grid=(1,),
        out_shape=shapes,
        in_specs=[
            pl.BlockSpec(memory_space=pltpu.SMEM),
            pl.BlockSpec((1, rhs, columns), lambda i: (blocks - 1, 0, 0)),
            whole(p2m.shape),
            whole(listing.shape),
        ],
        out_specs=tuple(whole(s.shape) for s in shapes),
        scratch_shapes=[pltpu.VMEM((rhs // halves, leaves * halves, terms), F32)],
        compiler_params=params(20),
        name="send",
    )(side, in_hbm(basis), in_hbm(p2m), listing)


def relayed_multipoles(given, leaves, slots, halves, rhs):
    receivers = given.shape[0] - rhs * leaves
    shape = (receivers * slots * halves, rhs // halves * given.shape[1])
    return pl.pallas_call(
        functools.partial(relay_kernel, halves, slots, leaves),
        grid=(1,),
        out_shape=jax.ShapeDtypeStruct(shape, BF16),
        in_specs=[whole(given.shape)],
        out_specs=whole(shape),
        compiler_params=params(16),
        cost_estimate=pl.CostEstimate(flops=shape[0] * shape[1] * 64, bytes_accessed=2**21, transcendentals=0),
        name="relay",
    )(given)


def near_kernel(src_ref, count_ref, before, own, after, blocks_ref, out_ref, wide):
    columns = own.shape[1]
    slots, panels = blocks_ref.shape[1], blocks_ref.shape[2]
    g = pl.program_id(0)

    @pl.when(g == 0)
    def _():
        wide[:, :columns] = before[...]
        wide[:, columns : 2 * columns] = own[...]
        wide[:, 2 * columns :] = after[...]

    for i in range(blocks_ref.shape[0]):
        leaf = g * blocks_ref.shape[0] + i
        here = pl.ds(pl.multiple_of(columns + leaf * panels, panels), panels)
        total = [wide[:, here].astype(F32), 0.0]
        for k in range(slots):
            place = pl.multiple_of(src_ref[leaf, k] * panels, panels)
            source = wide[:, pl.ds(place, panels)]
            source = jnp.where(k < count_ref[leaf], source, jnp.zeros_like(source))
            total[k % 2] += dot_nt(source, blocks_ref[i, k])
        out_ref[:, i * panels : (i + 1) * panels] = total[0] + total[1]


def near_field(near_src, near_count, before, own, after, near_blocks):
    leaves, slots, panels, _ = near_blocks.shape
    rhs, columns = own.shape
    grid_spec = pltpu.PrefetchScalarGridSpec(
        num_scalar_prefetch=2,
        grid=(leaves // 2,),
        in_specs=[
            whole((rhs, columns)),
            whole((rhs, columns)),
            whole((rhs, columns)),
            pl.BlockSpec((2, slots, panels, panels), lambda g, *_: (g, 0, 0, 0)),
        ],
        out_specs=pl.BlockSpec((rhs, 2 * panels), lambda g, *_: (0, g)),
        scratch_shapes=[pltpu.VMEM((rhs, 3 * columns), BF16)],
    )
    return pl.pallas_call(
        near_kernel,
        grid_spec=grid_spec,
        out_shape=jax.ShapeDtypeStruct((rhs, columns), F32),
        compiler_params=params(16),
        cost_estimate=pl.CostEstimate(
            flops=2 * rhs * near_blocks.size,
            bytes_accessed=near_blocks.size * 2 + 7 * rhs * columns * 2,
            transcendentals=0,
        ),
        name="near",
    )(near_src, near_count, before, own, after, near_blocks)


def far_kernel(
    halves, ours, theirs, pick, near, m2l_hbm, p2m_hbm, basis_hbm, image_ref, sums_ref, *scratch
):
    recv, lhs, loc, both, m2l, p2m, basis, sems = scratch
    moves = [
        pltpu.make_async_copy(source, target, sems.at[i])
        for i, (source, target) in enumerate(
            ((m2l_hbm, m2l), (p2m_hbm, p2m), (basis_hbm, basis))
        )
    ]
    for move in moves:
        move.start()
    leaves, panels, terms = p2m.shape
    classes = m2l.shape[0]
    blocks, rhs, columns = basis.shape
    part = rhs // halves
    group = 8
    rows = ours.shape[0]
    recv[:rows], recv[rows:] = ours[...], theirs[...]
    for h in range(halves):
        for j in range(0, part, group):
            got = dot(pick[h], recv[:, j * terms : (j + group) * terms]).astype(BF16)
            for t in range(group):
                base = (h * part + j + t) * leaves
                for c in range(classes):
                    lhs[base : base + leaves, c * terms : (c + 1) * terms] = got[
                        c * leaves : (c + 1) * leaves, t * terms : (t + 1) * terms
                    ]
    moves[0].wait()
    weights = m2l[...].reshape(classes * terms, terms)
    tall = 256
    for i in range(rhs * leaves // tall):
        got = dot(lhs[i * tall : (i + 1) * tall, :], weights)
        loc[i * tall // leaves : (i + 1) * tall // leaves] = got.reshape(
            tall // leaves, leaves, terms
        )
    moves[1].wait()
    for g in range(leaves):
        cols = slice(g * panels, (g + 1) * panels)
        image = near[:, cols] + dot_nt(loc[:, g, :].astype(BF16), p2m[g])
        image_ref[:, cols] = image
        both[:rhs, cols], both[rhs:, cols] = split_parts(image)
    moves[2].wait()
    inner = dot_nt(both[...], basis[...].reshape(blocks * rhs, columns))
    pack(inner[:rhs] + inner[rhs:], sums_ref)


def pack_sizes(rhs, wide, peers):
    rows = rhs * wide // 128 // peers
    return rows, -(-rows // 8) * 8


def pack(products, out_ref):
    peers, piece, lanes = out_ref.shape
    rhs, wide = products.shape
    rows, _ = pack_sizes(rhs, wide, peers)
    if rows < piece:
        out_ref[...] = jnp.zeros_like(out_ref)
    tall = jnp.concatenate(
        [products[:, i * lanes : (i + 1) * lanes] for i in range(wide // lanes)], axis=0
    )
    for p in range(peers):
        out_ref[p, :rows, :] = tall[p * rows : (p + 1) * rows]


def unpack(in_ref, rhs, wide):
    peers, _, lanes = in_ref.shape
    rows, _ = pack_sizes(rhs, wide, peers)
    tall = jnp.concatenate([in_ref[p, :rows, :] for p in range(peers)], axis=0)
    return jnp.concatenate(
        [tall[i * rhs : (i + 1) * rhs] for i in range(wide // lanes)], axis=1
    )


def far_field(ours, theirs, pick, m2l, p2m, near, basis, halves, peers):
    leaves, panels, terms = p2m.shape
    classes = m2l.shape[0]
    blocks, rhs, columns = basis.shape
    _, piece = pack_sizes(rhs, blocks * rhs, peers)
    args = (ours, theirs, pick, near)
    anywhere = pl.BlockSpec(memory_space=pl.ANY)
    return pl.pallas_call(
        functools.partial(far_kernel, halves),
        grid=(1,),
        out_shape=(
            jax.ShapeDtypeStruct((rhs, columns), F32),
            jax.ShapeDtypeStruct((peers, piece, 128), F32),
        ),
        in_specs=[whole(a.shape) for a in args] + [anywhere] * 3,
        out_specs=(whole((rhs, columns)), whole((peers, piece, 128))),
        scratch_shapes=[
            pltpu.VMEM((2 * ours.shape[0], ours.shape[1]), BF16),
            pltpu.VMEM((rhs * leaves, classes * terms), BF16),
            pltpu.VMEM((rhs, leaves, terms), F32),
            pltpu.VMEM((2 * rhs, columns), BF16),
            pltpu.VMEM(m2l.shape, BF16),
            pltpu.VMEM(p2m.shape, BF16),
            pltpu.VMEM(basis.shape, BF16),
            pltpu.SemaphoreType.DMA((3,)),
        ],
        compiler_params=params(32),
        name="far",
    )(*args, in_hbm(m2l), in_hbm(p2m), in_hbm(basis))


def exchange(pieces, axes=AXES):
    return lax.all_to_all(pieces, axes, split_axis=0, concat_axis=0, tiled=True)


def add_kernel(in_ref, out_ref):
    total = jnp.sum(in_ref[...], axis=0)
    out_ref[...] = jnp.broadcast_to(total[None], out_ref.shape)


def added(pieces, copies):
    shape = (copies, *pieces.shape[1:])
    return pl.pallas_call(
        add_kernel,
        grid=(1,),
        out_shape=jax.ShapeDtypeStruct(shape, F32),
        in_specs=[whole(pieces.shape)],
        out_specs=whole(shape),
        compiler_params=params(16),
        name="add",
    )(pieces)


def resid_kernel(total_rows, sums, basis, image, resid_ref, gram_ref, proj_ref):
    blocks, rhs, columns = basis.shape
    wide = blocks * rhs
    proj = unpack(sums, rhs, wide) * (1.0 / total_rows)
    proj_ref[...] = proj.T
    coef = jnp.concatenate(split_parts(proj), axis=0)
    step = 1024
    for i in range(columns // step):
        cols = slice(i * step, (i + 1) * step)
        by_basis = dot(coef, basis[:, :, cols].reshape(wide, step))
        resid = image[:, cols] - (by_basis[:rhs] + by_basis[rhs:])
        resid_ref[:rhs, cols], resid_ref[rhs:, cols] = split_parts(resid)
    both = resid_ref[...]
    square = dot_nt(both, both)
    gram = square[:rhs, :rhs] + square[:rhs, rhs:] + square[rhs:, :rhs] + square[rhs:, rhs:]
    half = rhs // 2
    folded = jnp.concatenate([gram[:half], gram[half:]], axis=1) * (1.0 / total_rows)
    gram_ref[...] = jnp.broadcast_to(folded[None], gram_ref.shape)


def residual(sums, basis, image, total_rows, copies):
    blocks, rhs, columns = basis.shape
    args = (sums, basis, image)
    shapes = (
        jax.ShapeDtypeStruct((2 * rhs, columns), BF16),
        jax.ShapeDtypeStruct((copies, rhs // 2, 2 * rhs), F32),
        jax.ShapeDtypeStruct((blocks * rhs, rhs), F32),
    )
    return pl.pallas_call(
        functools.partial(resid_kernel, total_rows),
        grid=(1,),
        out_shape=shapes,
        in_specs=[whole(a.shape) for a in args],
        out_specs=tuple(whole(s.shape) for s in shapes),
        compiler_params=params(24),
        name="residual",
    )(*args)


def factored(gram):
    size = gram.shape[0]
    rows = lax.broadcasted_iota(jnp.int32, (size, size), 0)
    cols = lax.broadcasted_iota(jnp.int32, (size, size), 1)
    eye = (rows == cols).astype(F32)
    both = jnp.concatenate([gram, eye], axis=1)
    tiles = [both[8 * i : 8 * i + 8] for i in range(size // 8)]
    sub = lax.broadcasted_iota(jnp.int32, (8, 2 * size), 0)
    for j in range(size):
        t, o = divmod(j, 8)
        row = tiles[t][o : o + 1]
        pivot = 1.0 / row[:, j : j + 1]
        scaled = row * pivot
        for i in range(t, size // 8):
            column = tiles[i][:, j : j + 1]
            change = column * scaled
            if i == t:
                change = jnp.where(sub > o, change, 0.0)
            tiles[i] = tiles[i] - change
    both = jnp.concatenate(tiles, axis=0)
    pivots = jnp.sum(both[:, :size] * eye, axis=1, keepdims=True)
    both = both * (1.0 / jnp.sqrt(pivots))
    upper = jnp.where(cols >= rows, both[:, :size], 0.0)
    return upper.T, both[:, size:]


def tail_kernel(grams, resid, next_ref, factor_ref):
    rhs = factor_ref.shape[0]
    columns = resid.shape[1]
    folded = jnp.sum(grams[...], axis=0)
    gram = jnp.concatenate([folded[:, :rhs], folded[:, rhs:]], axis=0)
    lower, inverse = factored(gram)
    factor_ref[...] = lower
    coef = jnp.concatenate(split_parts(inverse), axis=0)
    step = 1024
    for i in range(columns // step):
        cols = slice(i * step, (i + 1) * step)
        first = dot(coef, resid[:rhs, cols])
        second = dot(coef[:rhs], resid[rhs:, cols])
        next_ref[:, cols] = (first[:rhs] + first[rhs:] + second).astype(BF16)


def tail(grams, resid):
    rhs, columns = resid.shape[0] // 2, resid.shape[1]
    args = (grams, resid)
    shapes = (
        jax.ShapeDtypeStruct((rhs, columns), BF16),
        jax.ShapeDtypeStruct((rhs, rhs), F32),
    )
    return pl.pallas_call(
        tail_kernel,
        grid=(1,),
        out_shape=shapes,
        in_specs=[whole(a.shape) for a in args],
        out_specs=tuple(whole(s.shape) for s in shapes),
        compiler_params=params(16),
        name="tail",
    )(*args)


def shards(
    basis, near_blocks, near_src, near_count, p2m, m2l, send_list, send_count, far_src, far_class
):
    blocks, rhs, columns = basis.shape
    leaves = near_src.shape[0]
    classes, terms, _ = m2l.shape
    devices, near_devices = lax.axis_size("gx"), lax.axis_size("lo")
    peers = 2 * devices * near_devices
    slots = send_list.shape[2]
    total_rows = columns * peers
    halves = 2
    side = lax.axis_index("hi")
    same_side = ("gx", "lo")

    listing = jnp.concatenate([send_list[0], send_count[0][:, None]], axis=1)
    listing = jnp.pad(listing, ((0, 0), (0, terms - slots - 1))).astype(BF16)
    sent, given, own = sent_multipoles(side[None], basis, p2m, listing, slots, halves)
    given = lax.ppermute(given, "hi", [(0, 1), (1, 0)])
    ours = exchange(sent.reshape(peers // 2, slots * halves, -1), same_side).reshape(sent.shape)

    up = [(i, i + 1) for i in range(devices - 1)]
    down = [(j, i) for i, j in up]
    before = lax.ppermute(own, "gx", up)
    after = lax.ppermute(own, "gx", down)

    relayed = relayed_multipoles(given, leaves, slots, halves, rhs)
    theirs = exchange(relayed.reshape(peers // 2, slots * halves, -1), same_side)
    theirs = theirs.reshape(sent.shape)

    near = near_field(near_src, near_count, before, own, after, near_blocks)

    sender = far_src // slots
    place = sender // (2 * near_devices) * near_devices + sender % near_devices
    place = place + jnp.where(sender // near_devices % 2 == side, 0, peers // 2)
    place = place * slots + far_src % slots
    class_hot = (far_class[:, None, :] == jnp.arange(classes)[None, :, None]).astype(BF16)
    rows = jnp.arange(peers * slots * halves)[None, None, None, :]
    wanted = place[None, :, :, None] * halves + jnp.arange(halves)[:, None, None, None]
    source_hot = (wanted == rows).astype(BF16)
    pick = jnp.einsum("gce,hgef->hcgf", class_hot, source_hot, preferred_element_type=F32)
    pick = pick.astype(BF16).reshape(halves, classes * leaves, -1)

    image, sums = far_field(ours, theirs, pick, m2l, p2m, near, basis, halves, peers)
    sums = exchange(added(exchange(sums), peers))
    resid, grams, projections = residual(sums, basis, image, total_rows, 2 * near_devices)
    grams = exchange(added(exchange(grams, ("hi", "lo")), devices), ("gx",))
    next_block, factor = tail(grams, resid)
    return (next_block, projections.reshape(blocks, rhs, rhs), factor)


def solution(mesh):
    devices, segments = mesh.shape["gx"], mesh.shape["bulk"]
    mesh = jax.sharding.Mesh(mesh.devices.reshape(devices, 2, segments // 2), AXES)
    return jax.shard_map(
        shards,
        mesh=mesh,
        in_specs=(
            P(None, None, AXES),
            P(AXES, None, None, None),
            P(AXES, None),
            P(AXES),
            P(AXES, None, None),
            P(),
            P(AXES, None, None),
            P(AXES, None),
            P(AXES, None),
            P(AXES, None),
        ),
        out_specs=(P(None, AXES), P(), P()),
        check_vma=False,
    )
```

```python
import functools

import jax
import jax.numpy as jnp
from jax import lax
from jax.experimental import pallas as pl
from jax.experimental.pallas import tpu as pltpu
from jax.sharding import PartitionSpec as P

F32 = jnp.float32
BF16 = jnp.bfloat16
AXES = ("gx", "hi", "lo")
MIB = 1024 * 1024


def dot(a, b, dims=((1,), (0,)), precision=None):
    return lax.dot_general(a, b, (dims, ((), ())), precision=precision, preferred_element_type=F32)


def dot_nt(a, b, precision=None):
    return dot(a, b, ((1,), (1,)), precision)


def split_parts(values):
    upper = values.astype(BF16)
    lower = (values - upper.astype(F32)).astype(BF16)
    return (upper, lower)


def params(mib):
    return pltpu.CompilerParams(vmem_limit_bytes=mib * MIB)


def in_hbm(array):
    return pltpu.with_memory_space_constraint(array, pltpu.HBM)


def whole(shape):
    return pl.BlockSpec(shape, lambda *_: (0,) * len(shape))


def send_kernel(halves, x, p2m, listed, counts, out, own, scratch, lists):
    leaves, panels, terms = p2m.shape
    rhs = x.shape[1]
    part = rhs // halves
    slots, peers = listed.shape
    own[...] = x[0]
    for g in range(leaves):
        mult = dot(x[0, :, g * panels : (g + 1) * panels], p2m[g])
        for h in range(halves):
            scratch[:, g * halves + h, :] = mult[h * part : (h + 1) * part]
    tall = leaves * halves
    for j in range(part):
        out[j * tall : (j + 1) * tall, :] = scratch[j].astype(BF16)
    lists[...] = jnp.zeros_like(lists)
    lists[:slots, :peers] = listed[...].astype(F32)
    lists[slots : slots + 1, :peers] = counts[...].astype(F32)
    out[part * tall :, :] = lists[...].astype(BF16)


def relay_kernel(halves, slots, leaves, near_devices, side, own, given, out):
    tall, terms = leaves * halves, given.shape[1]
    rows, part = out.shape[0], out.shape[1] // terms
    each = 2 * slots * halves
    peers = 2 * rows // each
    receiver = lax.broadcasted_iota(jnp.int32, (rows, terms), 0) // each
    far_part, near_part = receiver // near_devices, receiver % near_devices
    device = far_part * (2 * near_devices) + side[0] * near_devices + near_part
    hot = (device == lax.broadcasted_iota(jnp.int32, (rows, terms), 1)).astype(F32).astype(BF16)
    spread = [dot_nt(hot, ref[part * tall :, :]) for ref in (own, given)]
    row = lax.broadcasted_iota(jnp.int32, spread[0].shape, 0)
    lane = lax.broadcasted_iota(jnp.int32, spread[0].shape, 1)
    spread = jnp.where(row // (slots * halves) % 2 == 0, spread[0], spread[1])
    slot = row // halves % slots
    leaf = jnp.sum(jnp.where(lane == slot, spread, 0.0), axis=1, keepdims=True)
    live = jnp.sum(jnp.where(lane == slots, spread, 0.0), axis=1, keepdims=True)
    row = lax.broadcasted_iota(jnp.int32, (rows, 2 * tall), 0)
    lane = lax.broadcasted_iota(jnp.int32, (rows, 2 * tall), 1).astype(F32)
    offset = row // (slots * halves) % 2 * tall + row % halves
    held = (row // halves % slots).astype(F32) < live
    chosen = ((lane == leaf * halves + offset.astype(F32)) & held).astype(F32).astype(BF16)
    for j in range(part // 2):
        pairs = [
            jnp.concatenate(
                [ref[i * tall : (i + 1) * tall, :] for i in (2 * j, 2 * j + 1)], axis=1
            )
            for ref in (own, given)
        ]
        got = dot(chosen, jnp.concatenate(pairs, axis=0))
        out[:, j * 2 * terms : (j + 1) * 2 * terms] = got.astype(BF16)


def all_multipoles(basis, p2m, listed, counts, halves):
    blocks, rhs, columns = basis.shape
    leaves, panels, terms = p2m.shape
    shapes = (
        jax.ShapeDtypeStruct((rhs * leaves + 16, terms), BF16),
        jax.ShapeDtypeStruct((rhs, columns), BF16),
    )
    return pl.pallas_call(
        functools.partial(send_kernel, halves),
        grid=(1,),
        out_shape=shapes,
        in_specs=[
            pl.BlockSpec((1, rhs, columns), lambda i: (blocks - 1, 0, 0)),
            whole(p2m.shape),
            whole(listed.shape),
            whole(counts.shape),
        ],
        out_specs=tuple(whole(s.shape) for s in shapes),
        scratch_shapes=[
            pltpu.VMEM((rhs // halves, leaves * halves, terms), F32),
            pltpu.VMEM((16, terms), F32),
        ],
        compiler_params=params(16),
        name="send",
    )(in_hbm(basis), in_hbm(p2m), listed, counts)


def relayed_multipoles(side, own, given, leaves, slots, halves, rhs, receivers):
    terms = own.shape[1]
    shape = (receivers * 2 * slots * halves, rhs // halves * terms)
    return pl.pallas_call(
        functools.partial(relay_kernel, halves, slots, leaves, lax.axis_size("lo")),
        grid=(1,),
        out_shape=jax.ShapeDtypeStruct(shape, BF16),
        in_specs=[
            pl.BlockSpec(memory_space=pltpu.SMEM),
            whole(own.shape),
            whole(given.shape),
        ],
        out_specs=whole(shape),
        compiler_params=params(16),
        name="relay",
    )(side, own, given)


def near_kernel(src_ref, count_ref, before, own, after, blocks_ref, out_ref, wide):
    columns = own.shape[1]
    slots, panels = blocks_ref.shape[1], blocks_ref.shape[2]
    g = pl.program_id(0)

    @pl.when(g == 0)
    def _():
        wide[:, :columns] = before[...]
        wide[:, columns : 2 * columns] = own[...]
        wide[:, 2 * columns :] = after[...]

    for i in range(blocks_ref.shape[0]):
        leaf = g * blocks_ref.shape[0] + i
        here = pl.ds(pl.multiple_of(columns + leaf * panels, panels), panels)
        total = [wide[:, here].astype(F32), 0.0]
        for k in range(slots):
            place = pl.multiple_of(src_ref[leaf, k] * panels, panels)
            source = wide[:, pl.ds(place, panels)]
            source = jnp.where(k < count_ref[leaf], source, jnp.zeros_like(source))
            total[k % 2] += dot_nt(source, blocks_ref[i, k])
        out_ref[:, i * panels : (i + 1) * panels] = total[0] + total[1]


def near_field(near_src, near_count, before, own, after, near_blocks):
    leaves, slots, panels, _ = near_blocks.shape
    rhs, columns = own.shape
    grid_spec = pltpu.PrefetchScalarGridSpec(
        num_scalar_prefetch=2,
        grid=(leaves // 2,),
        in_specs=[
            whole((rhs, columns)),
            whole((rhs, columns)),
            whole((rhs, columns)),
            pl.BlockSpec((2, slots, panels, panels), lambda g, *_: (g, 0, 0, 0)),
        ],
        out_specs=pl.BlockSpec((rhs, 2 * panels), lambda g, *_: (0, g)),
        scratch_shapes=[pltpu.VMEM((rhs, 3 * columns), BF16)],
    )
    return pl.pallas_call(
        near_kernel,
        grid_spec=grid_spec,
        out_shape=jax.ShapeDtypeStruct((rhs, columns), F32),
        compiler_params=params(16),
        cost_estimate=pl.CostEstimate(
            flops=2 * rhs * near_blocks.size,
            bytes_accessed=near_blocks.size * 2 + 7 * rhs * columns * 2,
            transcendentals=0,
        ),
        name="near",
    )(near_src, near_count, before, in_hbm(own), after, in_hbm(near_blocks))


def far_kernel(
    halves, recv, pick, near, m2l_hbm, p2m_hbm, basis_hbm, image_ref, sums_ref, *scratch
):
    lhs, loc, both, m2l, p2m, basis, sems = scratch
    moves = [
        pltpu.make_async_copy(source, target, sems.at[i])
        for i, (source, target) in enumerate(
            ((m2l_hbm, m2l), (p2m_hbm, p2m), (basis_hbm, basis))
        )
    ]
    for move in moves:
        move.start()
    leaves, panels, terms = p2m.shape
    classes = m2l.shape[0]
    blocks, rhs, columns = basis.shape
    part = rhs // halves
    group = 8
    for h in range(halves):
        for j in range(0, part, group):
            got = dot(pick[h], recv[:, j * terms : (j + group) * terms]).astype(BF16)
            for t in range(group):
                base = (h * part + j + t) * leaves
                for c in range(classes):
                    lhs[base : base + leaves, c * terms : (c + 1) * terms] = got[
                        c * leaves : (c + 1) * leaves, t * terms : (t + 1) * terms
                    ]
    moves[0].wait()
    weights = m2l[...].reshape(classes * terms, terms)
    tall = 256
    for i in range(rhs * leaves // tall):
        got = dot(lhs[i * tall : (i + 1) * tall, :], weights)
        loc[i * tall // leaves : (i + 1) * tall // leaves] = got.reshape(
            tall // leaves, leaves, terms
        )
    moves[1].wait()
    for g in range(leaves):
        cols = slice(g * panels, (g + 1) * panels)
        image = near[:, cols] + dot_nt(loc[:, g, :].astype(BF16), p2m[g])
        image_ref[:, cols] = image
        both[:rhs, cols], both[rhs:, cols] = split_parts(image)
    moves[2].wait()
    inner = dot_nt(both[...], basis[...].reshape(blocks * rhs, columns))
    pack(inner[:rhs] + inner[rhs:], sums_ref)


def pack_sizes(rhs, wide, peers):
    rows = rhs * wide // 128 // peers
    return rows, -(-rows // 8) * 8


def pack(products, out_ref):
    peers, piece, lanes = out_ref.shape
    rhs, wide = products.shape
    rows, _ = pack_sizes(rhs, wide, peers)
    if rows < piece:
        out_ref[...] = jnp.zeros_like(out_ref)
    tall = jnp.concatenate(
        [products[:, i * lanes : (i + 1) * lanes] for i in range(wide // lanes)], axis=0
    )
    for p in range(peers):
        out_ref[p, :rows, :] = tall[p * rows : (p + 1) * rows]


def unpack(in_ref, rhs, wide):
    peers, _, lanes = in_ref.shape
    rows, _ = pack_sizes(rhs, wide, peers)
    tall = jnp.concatenate([in_ref[p, :rows, :] for p in range(peers)], axis=0)
    return jnp.concatenate(
        [tall[i * rhs : (i + 1) * rhs] for i in range(wide // lanes)], axis=1
    )


def far_field(recv, pick, m2l, p2m, near, basis, halves, peers):
    leaves, panels, terms = p2m.shape
    classes = m2l.shape[0]
    blocks, rhs, columns = basis.shape
    _, piece = pack_sizes(rhs, blocks * rhs, peers)
    args = (recv, pick, near)
    anywhere = pl.BlockSpec(memory_space=pl.ANY)
    return pl.pallas_call(
        functools.partial(far_kernel, halves),
        grid=(1,),
        out_shape=(
            jax.ShapeDtypeStruct((rhs, columns), F32),
            jax.ShapeDtypeStruct((peers, piece, 128), F32),
        ),
        in_specs=[whole(a.shape) for a in args] + [anywhere] * 3,
        out_specs=(whole((rhs, columns)), whole((peers, piece, 128))),
        scratch_shapes=[
            pltpu.VMEM((rhs * leaves, classes * terms), BF16),
            pltpu.VMEM((rhs, leaves, terms), F32),
            pltpu.VMEM((2 * rhs, columns), BF16),
            pltpu.VMEM(m2l.shape, BF16),
            pltpu.VMEM(p2m.shape, BF16),
            pltpu.VMEM(basis.shape, BF16),
            pltpu.SemaphoreType.DMA((3,)),
        ],
        compiler_params=params(32),
        name="far",
    )(*args, in_hbm(m2l), in_hbm(p2m), in_hbm(basis))


def exchange(pieces, axes=AXES):
    return lax.all_to_all(pieces, axes, split_axis=0, concat_axis=0, tiled=True)


def add_kernel(in_ref, out_ref):
    total = jnp.sum(in_ref[...], axis=0)
    out_ref[...] = jnp.broadcast_to(total[None], out_ref.shape)


def added(pieces, copies):
    shape = (copies, *pieces.shape[1:])
    return pl.pallas_call(
        add_kernel,
        grid=(1,),
        out_shape=jax.ShapeDtypeStruct(shape, F32),
        in_specs=[whole(pieces.shape)],
        out_specs=whole(shape),
        compiler_params=params(16),
        name="add",
    )(pieces)


def resid_kernel(total_rows, sums, image, basis_hbm, resid_ref, gram_ref, proj_ref, basis, sems):
    blocks, rhs, columns = basis.shape
    wide = blocks * rhs
    steps = sems.shape[0]
    step = columns // steps
    moves = []
    for i in range(steps):
        part = (slice(None), slice(None), pl.ds(i * step, step))
        moves.append(pltpu.make_async_copy(basis_hbm.at[part], basis.at[part], sems.at[i]))
        moves[i].start()
    proj = unpack(sums, rhs, wide) * (1.0 / total_rows)
    proj_ref[...] = proj.T
    coef = jnp.concatenate(split_parts(proj), axis=0)
    for i in range(steps):
        cols = slice(i * step, (i + 1) * step)
        moves[i].wait()
        by_basis = dot(coef, basis[:, :, cols].reshape(wide, step))
        resid = image[:, cols] - (by_basis[:rhs] + by_basis[rhs:])
        resid_ref[:rhs, cols], resid_ref[rhs:, cols] = split_parts(resid)
    both = resid_ref[...]
    square = dot_nt(both, both)
    gram = square[:rhs, :rhs] + square[:rhs, rhs:] + square[rhs:, :rhs] + square[rhs:, rhs:]
    half = rhs // 2
    folded = jnp.concatenate([gram[:half], gram[half:]], axis=1) * (1.0 / total_rows)
    gram_ref[...] = folded


def residual(sums, basis, image, total_rows):
    blocks, rhs, columns = basis.shape
    args = (sums, image)
    shapes = (
        jax.ShapeDtypeStruct((2 * rhs, columns), BF16),
        jax.ShapeDtypeStruct((rhs // 2, 2 * rhs), F32),
        jax.ShapeDtypeStruct((blocks * rhs, rhs), F32),
    )
    return pl.pallas_call(
        functools.partial(resid_kernel, total_rows),
        grid=(1,),
        out_shape=shapes,
        in_specs=[whole(a.shape) for a in args] + [pl.BlockSpec(memory_space=pl.ANY)],
        out_specs=tuple(whole(s.shape) for s in shapes),
        scratch_shapes=[pltpu.VMEM(basis.shape, BF16), pltpu.SemaphoreType.DMA((4,))],
        compiler_params=params(24),
        name="residual",
    )(*args, in_hbm(basis))


def factored(gram):
    size = gram.shape[0]
    rows = lax.broadcasted_iota(jnp.int32, (size, size), 0)
    cols = lax.broadcasted_iota(jnp.int32, (size, size), 1)
    eye = (rows == cols).astype(F32)
    both = jnp.concatenate([gram, eye], axis=1)
    tiles = [both[8 * i : 8 * i + 8] for i in range(size // 8)]
    sub = lax.broadcasted_iota(jnp.int32, (8, 2 * size), 0)
    for j in range(size):
        t, o = divmod(j, 8)
        row = tiles[t][o : o + 1]
        pivot = 1.0 / row[:, j : j + 1]
        scaled = row * pivot
        for i in range(t, size // 8):
            column = tiles[i][:, j : j + 1]
            change = column * scaled
            if i == t:
                change = jnp.where(sub > o, change, 0.0)
            tiles[i] = tiles[i] - change
    both = jnp.concatenate(tiles, axis=0)
    pivots = jnp.sum(both[:, :size] * eye, axis=1, keepdims=True)
    both = both * (1.0 / jnp.sqrt(pivots))
    upper = jnp.where(cols >= rows, both[:, :size], 0.0)
    return upper.T, both[:, size:]


def tail_kernel(grams, resid, next_ref, factor_ref):
    rhs = factor_ref.shape[0]
    columns = resid.shape[1]
    folded = jnp.sum(grams[...], axis=0)
    gram = jnp.concatenate([folded[:, :rhs], folded[:, rhs:]], axis=0)
    lower, inverse = factored(gram)
    factor_ref[...] = lower
    coef = jnp.concatenate(split_parts(inverse), axis=0)
    step = 1024
    for i in range(columns // step):
        cols = slice(i * step, (i + 1) * step)
        first = dot(coef, resid[:rhs, cols])
        second = dot(coef[:rhs], resid[rhs:, cols])
        next_ref[:, cols] = (first[:rhs] + first[rhs:] + second).astype(BF16)


def tail(grams, resid):
    rhs, columns = resid.shape[0] // 2, resid.shape[1]
    args = (grams, resid)
    shapes = (
        jax.ShapeDtypeStruct((rhs, columns), BF16),
        jax.ShapeDtypeStruct((rhs, rhs), F32),
    )
    return pl.pallas_call(
        tail_kernel,
        grid=(1,),
        out_shape=shapes,
        in_specs=[whole(a.shape) for a in args],
        out_specs=tuple(whole(s.shape) for s in shapes),
        compiler_params=params(16),
        name="tail",
    )(*args)


def shards(
    basis, near_blocks, near_src, near_count, p2m, m2l, send_list, send_count, far_src, far_class
):
    blocks, rhs, columns = basis.shape
    leaves = near_src.shape[0]
    classes, terms, _ = m2l.shape
    devices, near_devices = lax.axis_size("gx"), lax.axis_size("lo")
    peers = 2 * devices * near_devices
    slots = send_list.shape[2]
    total_rows = columns * peers
    halves = 2
    side = lax.axis_index("hi")
    same_side = ("gx", "lo")

    payload, own = all_multipoles(basis, p2m, send_list[0].T, send_count, halves)
    flip = [(0, 1), (1, 0)]
    given = lax.ppermute(payload, "hi", flip)
    up = [(i, i + 1) for i in range(devices - 1)]
    down = [(j, i) for i, j in up]
    before = lax.ppermute(own, "gx", up)
    after = lax.ppermute(own, "gx", down)
    given, before, after = lax.optimization_barrier((given, before, after))
    relayed = relayed_multipoles(
        side[None], payload, given, leaves, slots, halves, rhs, peers // 2
    )
    received = exchange(relayed.reshape(peers // 2, 2 * slots * halves, -1), same_side)
    received = received.reshape(relayed.shape)

    near = near_field(near_src, near_count, before, own, after, near_blocks)

    sender = far_src // slots
    place = sender // (2 * near_devices) * near_devices + sender % near_devices
    place = place * 2 + (sender // near_devices % 2 != side).astype(jnp.int32)
    place = place * slots + far_src % slots
    class_hot = (far_class[:, None, :] == jnp.arange(classes)[None, :, None]).astype(BF16)
    rows = jnp.arange(peers * slots * halves)[None, None, None, :]
    wanted = place[None, :, :, None] * halves + jnp.arange(halves)[:, None, None, None]
    source_hot = (wanted == rows).astype(BF16)
    pick = jnp.einsum("gce,hgef->hcgf", class_hot, source_hot, preferred_element_type=F32)
    pick = pick.astype(BF16).reshape(halves, classes * leaves, -1)

    image, sums = far_field(received, pick, m2l, p2m, near, basis, halves, peers)
    sums = exchange(added(exchange(sums), peers))
    resid, gram, projections = residual(sums, basis, image, total_rows)
    pair = jnp.stack([gram, lax.ppermute(gram, "hi", flip)])
    grams = exchange(added(pair, peers // 2), same_side)
    next_block, factor = tail(grams, resid)
    return (next_block, projections.reshape(blocks, rhs, rhs), factor)


def solution(mesh):
    devices, segments = mesh.shape["gx"], mesh.shape["bulk"]
    mesh = jax.sharding.Mesh(mesh.devices.reshape(devices, 2, segments // 2), AXES)
    return jax.shard_map(
        shards,
        mesh=mesh,
        in_specs=(
            P(None, None, AXES),
            P(AXES, None, None, None),
            P(AXES, None),
            P(AXES),
            P(AXES, None, None),
            P(),
            P(AXES, None, None),
            P(AXES, None),
            P(AXES, None),
            P(AXES, None),
        ),
        out_specs=(P(None, AXES), P(), P()),
        check_vma=False,
    )
```

```python
import functools

import jax
import jax.numpy as jnp
from jax import lax
from jax.experimental import pallas as pl
from jax.experimental.pallas import tpu as pltpu
from jax.sharding import PartitionSpec as P

F32 = jnp.float32
BF16 = jnp.bfloat16
AXES = ("gx", "hi", "lo")
MIB = 1024 * 1024


def dot(a, b, dims=((1,), (0,)), precision=None):
    return lax.dot_general(a, b, (dims, ((), ())), precision=precision, preferred_element_type=F32)


def dot_nt(a, b, precision=None):
    return dot(a, b, ((1,), (1,)), precision)


def split_parts(values):
    upper = values.astype(BF16)
    lower = (values - upper.astype(F32)).astype(BF16)
    return (upper, lower)


def params(mib):
    return pltpu.CompilerParams(vmem_limit_bytes=mib * MIB)


def in_hbm(array):
    return pltpu.with_memory_space_constraint(array, pltpu.HBM)


def whole(shape):
    return pl.BlockSpec(shape, lambda *_: (0,) * len(shape))


def send_kernel(halves, x, p2m, listed, counts, out, own, scratch, lists):
    leaves, panels, terms = p2m.shape
    rhs = x.shape[1]
    part = rhs // halves
    slots, peers = listed.shape
    own[...] = x[0]
    for g in range(leaves):
        mult = dot(x[0, :, g * panels : (g + 1) * panels], p2m[g])
        for h in range(halves):
            scratch[:, g * halves + h, :] = mult[h * part : (h + 1) * part]
    tall = leaves * halves
    for j in range(part):
        out[j * tall : (j + 1) * tall, :] = scratch[j].astype(BF16)
    lists[...] = jnp.zeros_like(lists)
    lists[:slots, :peers] = listed[...].astype(F32)
    lists[slots : slots + 1, :peers] = counts[...].astype(F32)
    out[part * tall :, :] = lists[...].astype(BF16)


def choose_kernel(halves, slots, leaves, near_devices, side, given, out):
    tall, terms = leaves * halves, given.shape[1]
    rows, part = out.shape[0], out.shape[1] // terms
    each = slots * halves
    receiver = lax.broadcasted_iota(jnp.int32, (rows, terms), 0) // each
    far_part, near_part = receiver // near_devices, receiver % near_devices
    device = far_part * (2 * near_devices) + side[0] * near_devices + near_part
    hot = (device == lax.broadcasted_iota(jnp.int32, (rows, terms), 1)).astype(F32).astype(BF16)
    spread = dot_nt(hot, given[part * tall :, :])
    row = lax.broadcasted_iota(jnp.int32, spread.shape, 0)
    lane = lax.broadcasted_iota(jnp.int32, spread.shape, 1)
    slot = row // halves % slots
    leaf = jnp.sum(jnp.where(lane == slot, spread, 0.0), axis=1, keepdims=True)
    live = jnp.sum(jnp.where(lane == slots, spread, 0.0), axis=1, keepdims=True)
    row = lax.broadcasted_iota(jnp.int32, (rows, tall), 0)
    lane = lax.broadcasted_iota(jnp.int32, (rows, tall), 1).astype(F32)
    held = (row // halves % slots).astype(F32) < live
    wanted = leaf * halves + (row % halves).astype(F32)
    chosen = ((lane == wanted) & held).astype(F32).astype(BF16)
    for j in range(part // 2):
        pair = [given[i * tall : (i + 1) * tall, :] for i in (2 * j, 2 * j + 1)]
        got = dot(chosen, jnp.concatenate(pair, axis=1))
        out[:, j * 2 * terms : (j + 1) * 2 * terms] = got.astype(BF16)


def all_multipoles(basis, p2m, listed, counts, halves):
    blocks, rhs, columns = basis.shape
    leaves, panels, terms = p2m.shape
    shapes = (
        jax.ShapeDtypeStruct((rhs * leaves + 16, terms), BF16),
        jax.ShapeDtypeStruct((rhs, columns), BF16),
    )
    return pl.pallas_call(
        functools.partial(send_kernel, halves),
        grid=(1,),
        out_shape=shapes,
        in_specs=[
            pl.BlockSpec((1, rhs, columns), lambda i: (blocks - 1, 0, 0)),
            whole(p2m.shape),
            whole(listed.shape),
            whole(counts.shape),
        ],
        out_specs=tuple(whole(s.shape) for s in shapes),
        scratch_shapes=[
            pltpu.VMEM((rhs // halves, leaves * halves, terms), F32),
            pltpu.VMEM((16, terms), F32),
        ],
        compiler_params=params(16),
        name="send",
    )(in_hbm(basis), in_hbm(p2m), in_hbm(listed), in_hbm(counts))


def chosen_multipoles(side, given, leaves, slots, halves, rhs, receivers):
    terms = given.shape[1]
    shape = (receivers * slots * halves, rhs // halves * terms)
    return pl.pallas_call(
        functools.partial(choose_kernel, halves, slots, leaves, lax.axis_size("lo")),
        grid=(1,),
        out_shape=jax.ShapeDtypeStruct(shape, BF16),
        in_specs=[pl.BlockSpec(memory_space=pltpu.SMEM), whole(given.shape)],
        out_specs=whole(shape),
        compiler_params=params(16),
        name="choose",
    )(side, given)


def near_kernel(src_ref, count_ref, before, own, after, blocks_ref, *refs):
    brought = len(refs) // 2 - 1
    out_ref, wide, sems = refs[brought], refs[-2], refs[-1]
    moves = [
        pltpu.make_async_copy(refs[i], refs[brought + 1 + i], sems.at[i]) for i in range(brought)
    ]
    columns = own.shape[1]
    slots, panels = blocks_ref.shape[1], blocks_ref.shape[2]
    g = pl.program_id(0)

    @pl.when(g == 0)
    def _():
        for move in moves:
            move.start()
        wide[:, :columns] = before[...]
        wide[:, columns : 2 * columns] = own[...]
        wide[:, 2 * columns :] = after[...]

    for i in range(blocks_ref.shape[0]):
        leaf = g * blocks_ref.shape[0] + i
        here = pl.ds(pl.multiple_of(columns + leaf * panels, panels), panels)
        total = [wide[:, here].astype(F32), 0.0]
        for k in range(slots):
            place = pl.multiple_of(src_ref[leaf, k] * panels, panels)
            source = wide[:, pl.ds(place, panels)]
            source = jnp.where(k < count_ref[leaf], source, jnp.zeros_like(source))
            total[k % 2] += dot_nt(source, blocks_ref[i, k])
        out_ref[:, i * panels : (i + 1) * panels] = total[0] + total[1]

    @pl.when(g == pl.num_programs(0) - 1)
    def _():
        for move in moves:
            move.wait()


def near_field(near_src, near_count, before, own, after, near_blocks, bring):
    leaves, slots, panels, _ = near_blocks.shape
    rhs, columns = own.shape
    anywhere = pl.BlockSpec(memory_space=pl.ANY)
    grid_spec = pltpu.PrefetchScalarGridSpec(
        num_scalar_prefetch=2,
        grid=(leaves // 2,),
        in_specs=[
            whole((rhs, columns)),
            whole((rhs, columns)),
            whole((rhs, columns)),
            pl.BlockSpec((2, slots, panels, panels), lambda g, *_: (g, 0, 0, 0)),
        ]
        + [anywhere] * len(bring),
        out_specs=[pl.BlockSpec((rhs, 2 * panels), lambda g, *_: (0, g))]
        + [anywhere] * len(bring),
        scratch_shapes=[
            pltpu.VMEM((rhs, 3 * columns), BF16),
            pltpu.SemaphoreType.DMA((len(bring),)),
        ],
    )
    return pl.pallas_call(
        near_kernel,
        grid_spec=grid_spec,
        out_shape=[jax.ShapeDtypeStruct((rhs, columns), F32)]
        + [pltpu.VMEM(a.shape, a.dtype) for a in bring],
        compiler_params=params(16),
        cost_estimate=pl.CostEstimate(
            flops=2 * rhs * near_blocks.size,
            bytes_accessed=near_blocks.size * 2 + 7 * rhs * columns * 2,
            transcendentals=0,
        ),
        name="near",
    )(
        near_src,
        near_count,
        before,
        in_hbm(own),
        after,
        in_hbm(near_blocks),
        *[in_hbm(a) for a in bring],
    )


def far_kernel(
    halves, ours, theirs, pick, near, m2l, p2m, basis, image_ref, sums_ref, recv, lhs, loc, both
):
    leaves, panels, terms = p2m.shape
    classes = m2l.shape[0]
    blocks, rhs, columns = basis.shape
    part = rhs // halves
    group = 8
    rows = ours.shape[0]
    recv[:rows], recv[rows:] = ours[...], theirs[...]
    for h in range(halves):
        for j in range(0, part, group):
            got = dot(pick[h], recv[:, j * terms : (j + group) * terms]).astype(BF16)
            for t in range(group):
                base = (h * part + j + t) * leaves
                for c in range(classes):
                    lhs[base : base + leaves, c * terms : (c + 1) * terms] = got[
                        c * leaves : (c + 1) * leaves, t * terms : (t + 1) * terms
                    ]
    weights = m2l[...].reshape(classes * terms, terms)
    tall = 256
    for i in range(rhs * leaves // tall):
        got = dot(lhs[i * tall : (i + 1) * tall, :], weights)
        loc[i * tall // leaves : (i + 1) * tall // leaves] = got.reshape(
            tall // leaves, leaves, terms
        )
    for g in range(leaves):
        cols = slice(g * panels, (g + 1) * panels)
        image = near[:, cols] + dot_nt(loc[:, g, :].astype(BF16), p2m[g])
        image_ref[:, cols] = image
        both[:rhs, cols], both[rhs:, cols] = split_parts(image)
    inner = dot_nt(both[...], basis[...].reshape(blocks * rhs, columns))
    pack(inner[:rhs] + inner[rhs:], sums_ref)


def pack_sizes(rhs, wide, peers):
    rows = rhs * wide // 128 // peers
    return rows, -(-rows // 8) * 8


def pack(products, out_ref):
    peers, piece, lanes = out_ref.shape
    rhs, wide = products.shape
    rows, _ = pack_sizes(rhs, wide, peers)
    if rows < piece:
        out_ref[...] = jnp.zeros_like(out_ref)
    tall = jnp.concatenate(
        [products[:, i * lanes : (i + 1) * lanes] for i in range(wide // lanes)], axis=0
    )
    for p in range(peers):
        out_ref[p, :rows, :] = tall[p * rows : (p + 1) * rows]


def unpack(in_ref, rhs, wide):
    peers, _, lanes = in_ref.shape
    rows, _ = pack_sizes(rhs, wide, peers)
    tall = jnp.concatenate([in_ref[p, :rows, :] for p in range(peers)], axis=0)
    return jnp.concatenate(
        [tall[i * rhs : (i + 1) * rhs] for i in range(wide // lanes)], axis=1
    )


def far_field(ours, theirs, pick, m2l, p2m, near, basis, halves, peers):
    leaves, panels, terms = p2m.shape
    classes = m2l.shape[0]
    blocks, rhs, columns = basis.shape
    _, piece = pack_sizes(rhs, blocks * rhs, peers)
    args = (ours, theirs, pick, near, m2l, p2m, basis)
    return pl.pallas_call(
        functools.partial(far_kernel, halves),
        grid=(1,),
        out_shape=(
            jax.ShapeDtypeStruct((rhs, columns), F32),
            jax.ShapeDtypeStruct((peers, piece, 128), F32),
        ),
        in_specs=[whole(a.shape) for a in args],
        out_specs=(whole((rhs, columns)), whole((peers, piece, 128))),
        scratch_shapes=[
            pltpu.VMEM((2 * ours.shape[0], ours.shape[1]), BF16),
            pltpu.VMEM((rhs * leaves, classes * terms), BF16),
            pltpu.VMEM((rhs, leaves, terms), F32),
            pltpu.VMEM((2 * rhs, columns), BF16),
        ],
        compiler_params=params(32),
        name="far",
    )(*args)


def exchange(pieces, axes=AXES):
    return lax.all_to_all(pieces, axes, split_axis=0, concat_axis=0, tiled=True)


def add_kernel(in_ref, out_ref):
    total = jnp.sum(in_ref[...], axis=0)
    out_ref[...] = jnp.broadcast_to(total[None], out_ref.shape)


def added(pieces, copies):
    shape = (copies, *pieces.shape[1:])
    return pl.pallas_call(
        add_kernel,
        grid=(1,),
        out_shape=jax.ShapeDtypeStruct(shape, F32),
        in_specs=[whole(pieces.shape)],
        out_specs=whole(shape),
        compiler_params=params(16),
        name="add",
    )(pieces)


def resid_kernel(total_rows, sums, image, basis, resid_ref, gram_ref, proj_ref):
    blocks, rhs, columns = basis.shape
    wide = blocks * rhs
    proj = unpack(sums, rhs, wide) * (1.0 / total_rows)
    proj_ref[...] = proj.T
    coef = jnp.concatenate(split_parts(proj), axis=0)
    step = 1024
    for i in range(columns // step):
        cols = slice(i * step, (i + 1) * step)
        by_basis = dot(coef, basis[:, :, cols].reshape(wide, step))
        resid = image[:, cols] - (by_basis[:rhs] + by_basis[rhs:])
        resid_ref[:rhs, cols], resid_ref[rhs:, cols] = split_parts(resid)
    both = resid_ref[...]
    square = dot_nt(both, both)
    gram = square[:rhs, :rhs] + square[:rhs, rhs:] + square[rhs:, :rhs] + square[rhs:, rhs:]
    half = rhs // 2
    folded = jnp.concatenate([gram[:half], gram[half:]], axis=1) * (1.0 / total_rows)
    gram_ref[...] = folded


def residual(sums, basis, image, total_rows):
    blocks, rhs, columns = basis.shape
    args = (sums, image, basis)
    shapes = (
        jax.ShapeDtypeStruct((2 * rhs, columns), BF16),
        jax.ShapeDtypeStruct((rhs // 2, 2 * rhs), F32),
        jax.ShapeDtypeStruct((blocks * rhs, rhs), F32),
    )
    return pl.pallas_call(
        functools.partial(resid_kernel, total_rows),
        grid=(1,),
        out_shape=shapes,
        in_specs=[whole(a.shape) for a in args],
        out_specs=tuple(whole(s.shape) for s in shapes),
        compiler_params=params(24),
        name="residual",
    )(*args)


def factored(gram):
    size = gram.shape[0]
    rows = lax.broadcasted_iota(jnp.int32, (size, size), 0)
    cols = lax.broadcasted_iota(jnp.int32, (size, size), 1)
    eye = (rows == cols).astype(F32)
    both = jnp.concatenate([gram, eye], axis=1)
    tiles = [both[8 * i : 8 * i + 8] for i in range(size // 8)]
    sub = lax.broadcasted_iota(jnp.int32, (8, 2 * size), 0)
    for j in range(size):
        t, o = divmod(j, 8)
        row = tiles[t][o : o + 1]
        pivot = 1.0 / row[:, j : j + 1]
        scaled = row * pivot
        for i in range(t, size // 8):
            column = tiles[i][:, j : j + 1]
            change = column * scaled
            if i == t:
                change = jnp.where(sub > o, change, 0.0)
            tiles[i] = tiles[i] - change
    both = jnp.concatenate(tiles, axis=0)
    pivots = jnp.sum(both[:, :size] * eye, axis=1, keepdims=True)
    both = both * (1.0 / jnp.sqrt(pivots))
    upper = jnp.where(cols >= rows, both[:, :size], 0.0)
    return upper.T, both[:, size:]


def tail_kernel(grams, resid, next_ref, factor_ref):
    rhs = factor_ref.shape[0]
    columns = resid.shape[1]
    folded = jnp.sum(grams[...], axis=0)
    gram = jnp.concatenate([folded[:, :rhs], folded[:, rhs:]], axis=0)
    lower, inverse = factored(gram)
    factor_ref[...] = lower
    coef = jnp.concatenate(split_parts(inverse), axis=0)
    step = 1024
    for i in range(columns // step):
        cols = slice(i * step, (i + 1) * step)
        first = dot(coef, resid[:rhs, cols])
        second = dot(coef[:rhs], resid[rhs:, cols])
        next_ref[:, cols] = (first[:rhs] + first[rhs:] + second).astype(BF16)


def tail(grams, resid):
    rhs, columns = resid.shape[0] // 2, resid.shape[1]
    args = (grams, resid)
    shapes = (
        jax.ShapeDtypeStruct((rhs, columns), BF16),
        jax.ShapeDtypeStruct((rhs, rhs), F32),
    )
    return pl.pallas_call(
        tail_kernel,
        grid=(1,),
        out_shape=shapes,
        in_specs=[whole(a.shape) for a in args],
        out_specs=tuple(whole(s.shape) for s in shapes),
        compiler_params=params(16),
        name="tail",
    )(*args)


def shards(
    basis, near_blocks, near_src, near_count, p2m, m2l, send_list, send_count, far_src, far_class
):
    blocks, rhs, columns = basis.shape
    leaves = near_src.shape[0]
    classes, terms, _ = m2l.shape
    devices, near_devices = lax.axis_size("gx"), lax.axis_size("lo")
    peers = 2 * devices * near_devices
    slots = send_list.shape[2]
    total_rows = columns * peers
    halves = 2
    side = lax.axis_index("hi")
    same_side = ("gx", "lo")

    payload, own = all_multipoles(basis, p2m, send_list[0].T, send_count, halves)
    flip = [(0, 1), (1, 0)]
    given = lax.ppermute(payload, "hi", flip)
    up = [(i, i + 1) for i in range(devices - 1)]
    down = [(j, i) for i, j in up]
    before = lax.ppermute(own, "gx", up)
    after = lax.ppermute(own, "gx", down)
    given, before, after = lax.optimization_barrier((given, before, after))
    received = []
    for multipoles in (payload, given):
        chosen = chosen_multipoles(side[None], multipoles, leaves, slots, halves, rhs, peers // 2)
        got = exchange(chosen.reshape(peers // 2, slots * halves, -1), same_side)
        received.append(got.reshape(chosen.shape))

    near, basis_near, p2m_near, m2l_near = near_field(
        near_src, near_count, before, own, after, near_blocks, (basis, p2m, m2l)
    )

    sender = far_src // slots
    place = sender // (2 * near_devices) * near_devices + sender % near_devices
    place = place + jnp.where(sender // near_devices % 2 == side, 0, peers // 2)
    place = place * slots + far_src % slots
    class_hot = (far_class[:, None, :] == jnp.arange(classes)[None, :, None]).astype(BF16)
    rows = jnp.arange(peers * slots * halves)[None, None, None, :]
    wanted = place[None, :, :, None] * halves + jnp.arange(halves)[:, None, None, None]
    source_hot = (wanted == rows).astype(BF16)
    pick = jnp.einsum("gce,hgef->hcgf", class_hot, source_hot, preferred_element_type=F32)
    pick = pick.astype(BF16).reshape(halves, classes * leaves, -1)

    image, sums = far_field(
        *received, pick, m2l_near, p2m_near, near, basis_near, halves, peers
    )
    sums = exchange(added(exchange(sums), peers))
    resid, gram, projections = residual(sums, basis_near, image, total_rows)
    pair = jnp.stack([gram, lax.ppermute(gram, "hi", flip)])
    grams = exchange(added(pair, peers // 2), same_side)
    next_block, factor = tail(grams, resid)
    return (next_block, projections.reshape(blocks, rhs, rhs), factor)


def solution(mesh):
    devices, segments = mesh.shape["gx"], mesh.shape["bulk"]
    mesh = jax.sharding.Mesh(mesh.devices.reshape(devices, 2, segments // 2), AXES)
    return jax.shard_map(
        shards,
        mesh=mesh,
        in_specs=(
            P(None, None, AXES),
            P(AXES, None, None, None),
            P(AXES, None),
            P(AXES),
            P(AXES, None, None),
            P(),
            P(AXES, None, None),
            P(AXES, None),
            P(AXES, None),
            P(AXES, None),
        ),
        out_specs=(P(None, AXES), P(), P()),
        check_vma=False,
    )
```

```python
import functools

import jax
import jax.numpy as jnp
from jax import lax
from jax.experimental import pallas as pl
from jax.experimental.pallas import tpu as pltpu
from jax.sharding import PartitionSpec as P

F32 = jnp.float32
BF16 = jnp.bfloat16
AXES = ("gx", "hi", "lo")
MIB = 1024 * 1024


def dot(a, b, dims=((1,), (0,)), precision=None):
    return lax.dot_general(a, b, (dims, ((), ())), precision=precision, preferred_element_type=F32)


def dot_nt(a, b, precision=None):
    return dot(a, b, ((1,), (1,)), precision)


def split_parts(values):
    upper = values.astype(BF16)
    lower = (values - upper.astype(F32)).astype(BF16)
    return (upper, lower)


def params(mib):
    return pltpu.CompilerParams(vmem_limit_bytes=mib * MIB)


def in_hbm(array):
    return pltpu.with_memory_space_constraint(array, pltpu.HBM)


def whole(shape):
    return pl.BlockSpec(shape, lambda *_: (0,) * len(shape))


def send_kernel(halves, x, p2m, listed, counts, out, own, scratch, lists):
    leaves, panels, terms = p2m.shape
    rhs = x.shape[1]
    part = rhs // halves
    slots, peers = listed.shape
    own[...] = x[0]
    for g in range(leaves):
        mult = dot(x[0, :, g * panels : (g + 1) * panels], p2m[g])
        for h in range(halves):
            scratch[:, g * halves + h, :] = mult[h * part : (h + 1) * part]
    tall = leaves * halves
    for j in range(part):
        out[j * tall : (j + 1) * tall, :] = scratch[j].astype(BF16)
    lists[...] = jnp.zeros_like(lists)
    lists[:slots, :peers] = listed[...].astype(F32)
    lists[slots : slots + 1, :peers] = counts[...].astype(F32)
    out[part * tall :, :] = lists[...].astype(BF16)


def choose_kernel(halves, slots, leaves, near_devices, side, given, out):
    tall, terms = leaves * halves, given.shape[1]
    rows, part = out.shape[0], out.shape[1] // terms
    each = slots * halves
    receiver = lax.broadcasted_iota(jnp.int32, (rows, terms), 0) // each
    far_part, near_part = receiver // near_devices, receiver % near_devices
    device = far_part * (2 * near_devices) + side[0] * near_devices + near_part
    hot = (device == lax.broadcasted_iota(jnp.int32, (rows, terms), 1)).astype(F32).astype(BF16)
    spread = dot_nt(hot, given[part * tall :, :])
    row = lax.broadcasted_iota(jnp.int32, spread.shape, 0)
    lane = lax.broadcasted_iota(jnp.int32, spread.shape, 1)
    slot = row // halves % slots
    leaf = jnp.sum(jnp.where(lane == slot, spread, 0.0), axis=1, keepdims=True)
    live = jnp.sum(jnp.where(lane == slots, spread, 0.0), axis=1, keepdims=True)
    row = lax.broadcasted_iota(jnp.int32, (rows, tall), 0)
    lane = lax.broadcasted_iota(jnp.int32, (rows, tall), 1).astype(F32)
    held = (row // halves % slots).astype(F32) < live
    wanted = leaf * halves + (row % halves).astype(F32)
    chosen = ((lane == wanted) & held).astype(F32).astype(BF16)
    for j in range(part // 2):
        pair = [given[i * tall : (i + 1) * tall, :] for i in (2 * j, 2 * j + 1)]
        got = dot(chosen, jnp.concatenate(pair, axis=1))
        out[:, j * 2 * terms : (j + 1) * 2 * terms] = got.astype(BF16)


def all_multipoles(basis, p2m, listed, counts, halves):
    blocks, rhs, columns = basis.shape
    leaves, panels, terms = p2m.shape
    shapes = (
        jax.ShapeDtypeStruct((rhs * leaves + 16, terms), BF16),
        jax.ShapeDtypeStruct((rhs, columns), BF16),
    )
    return pl.pallas_call(
        functools.partial(send_kernel, halves),
        grid=(1,),
        out_shape=shapes,
        in_specs=[
            pl.BlockSpec((1, rhs, columns), lambda i: (blocks - 1, 0, 0)),
            whole(p2m.shape),
            whole(listed.shape),
            whole(counts.shape),
        ],
        out_specs=tuple(whole(s.shape) for s in shapes),
        scratch_shapes=[
            pltpu.VMEM((rhs // halves, leaves * halves, terms), F32),
            pltpu.VMEM((16, terms), F32),
        ],
        compiler_params=params(8),
        name="send",
    )(in_hbm(basis), in_hbm(p2m), in_hbm(listed), in_hbm(counts))


def chosen_multipoles(side, given, leaves, slots, halves, rhs, receivers):
    terms = given.shape[1]
    shape = (receivers * slots * halves, rhs // halves * terms)
    return pl.pallas_call(
        functools.partial(choose_kernel, halves, slots, leaves, lax.axis_size("lo")),
        grid=(1,),
        out_shape=jax.ShapeDtypeStruct(shape, BF16),
        in_specs=[pl.BlockSpec(memory_space=pltpu.SMEM), whole(given.shape)],
        out_specs=whole(shape),
        compiler_params=params(8),
        name="choose",
    )(side, given)


def near_kernel(src_ref, count_ref, before, own, after, blocks_ref, *refs):
    brought = len(refs) // 2 - 1
    out_ref, wide, sems = refs[brought], refs[-2], refs[-1]
    moves = [
        pltpu.make_async_copy(refs[i], refs[brought + 1 + i], sems.at[i]) for i in range(brought)
    ]
    columns = own.shape[1]
    slots, panels = blocks_ref.shape[1], blocks_ref.shape[2]
    g = pl.program_id(0)

    @pl.when(g == 0)
    def _():
        for move in moves:
            move.start()
        wide[:, :columns] = before[...]
        wide[:, columns : 2 * columns] = own[...]
        wide[:, 2 * columns :] = after[...]

    for i in range(blocks_ref.shape[0]):
        leaf = g * blocks_ref.shape[0] + i
        here = pl.ds(pl.multiple_of(columns + leaf * panels, panels), panels)
        total = [wide[:, here].astype(F32), 0.0]
        for k in range(slots):
            place = pl.multiple_of(src_ref[leaf, k] * panels, panels)
            source = wide[:, pl.ds(place, panels)]
            source = jnp.where(k < count_ref[leaf], source, jnp.zeros_like(source))
            total[k % 2] += dot_nt(source, blocks_ref[i, k])
        out_ref[:, i * panels : (i + 1) * panels] = total[0] + total[1]

    @pl.when(g == pl.num_programs(0) - 1)
    def _():
        for move in moves:
            move.wait()


def near_field(near_src, near_count, before, own, after, near_blocks, bring):
    leaves, slots, panels, _ = near_blocks.shape
    rhs, columns = own.shape
    anywhere = pl.BlockSpec(memory_space=pl.ANY)
    grid_spec = pltpu.PrefetchScalarGridSpec(
        num_scalar_prefetch=2,
        grid=(leaves // 2,),
        in_specs=[
            whole((rhs, columns)),
            whole((rhs, columns)),
            whole((rhs, columns)),
            pl.BlockSpec((2, slots, panels, panels), lambda g, *_: (g, 0, 0, 0)),
        ]
        + [anywhere] * len(bring),
        out_specs=[pl.BlockSpec((rhs, 2 * panels), lambda g, *_: (0, g))]
        + [anywhere] * len(bring),
        scratch_shapes=[
            pltpu.VMEM((rhs, 3 * columns), BF16),
            pltpu.SemaphoreType.DMA((len(bring),)),
        ],
    )
    return pl.pallas_call(
        near_kernel,
        grid_spec=grid_spec,
        out_shape=[jax.ShapeDtypeStruct((rhs, columns), F32)]
        + [pltpu.VMEM(a.shape, a.dtype) for a in bring],
        compiler_params=params(12),
        cost_estimate=pl.CostEstimate(
            flops=2 * rhs * near_blocks.size,
            bytes_accessed=near_blocks.size * 2 + 7 * rhs * columns * 2,
            transcendentals=0,
        ),
        name="near",
    )(
        near_src,
        near_count,
        before,
        in_hbm(own),
        after,
        in_hbm(near_blocks),
        *[in_hbm(a) for a in bring],
    )


def far_kernel(
    halves, ours, theirs, pick, near, m2l, p2m, basis, image_ref, sums_ref, recv, lhs, loc, both
):
    leaves, panels, terms = p2m.shape
    classes = m2l.shape[0]
    blocks, rhs, columns = basis.shape
    part = rhs // halves
    group = 8
    rows = ours.shape[0]
    recv[:rows], recv[rows:] = ours[...], theirs[...]
    for h in range(halves):
        for j in range(0, part, group):
            got = dot(pick[h], recv[:, j * terms : (j + group) * terms]).astype(BF16)
            for t in range(group):
                base = (h * part + j + t) * leaves
                for c in range(classes):
                    lhs[base : base + leaves, c * terms : (c + 1) * terms] = got[
                        c * leaves : (c + 1) * leaves, t * terms : (t + 1) * terms
                    ]
    weights = m2l[...].reshape(classes * terms, terms)
    tall = 256
    for i in range(rhs * leaves // tall):
        got = dot(lhs[i * tall : (i + 1) * tall, :], weights)
        loc[i * tall // leaves : (i + 1) * tall // leaves] = got.reshape(
            tall // leaves, leaves, terms
        )
    for g in range(leaves):
        cols = slice(g * panels, (g + 1) * panels)
        image = near[:, cols] + dot_nt(loc[:, g, :].astype(BF16), p2m[g])
        image_ref[:, cols] = image
        both[:rhs, cols], both[rhs:, cols] = split_parts(image)
    inner = dot_nt(both[...], basis[...].reshape(blocks * rhs, columns))
    pack(inner[:rhs] + inner[rhs:], sums_ref)


def pack_sizes(rhs, wide, peers):
    rows = rhs * wide // 128 // peers
    return rows, -(-rows // 8) * 8


def pack(products, out_ref):
    peers, piece, lanes = out_ref.shape
    rhs, wide = products.shape
    rows, _ = pack_sizes(rhs, wide, peers)
    if rows < piece:
        out_ref[...] = jnp.zeros_like(out_ref)
    tall = jnp.concatenate(
        [products[:, i * lanes : (i + 1) * lanes] for i in range(wide // lanes)], axis=0
    )
    for p in range(peers):
        out_ref[p, :rows, :] = tall[p * rows : (p + 1) * rows]


def unpack(in_ref, rhs, wide):
    peers, _, lanes = in_ref.shape
    rows, _ = pack_sizes(rhs, wide, peers)
    tall = jnp.concatenate([in_ref[p, :rows, :] for p in range(peers)], axis=0)
    return jnp.concatenate(
        [tall[i * rhs : (i + 1) * rhs] for i in range(wide // lanes)], axis=1
    )


def far_field(ours, theirs, pick, m2l, p2m, near, basis, halves, peers):
    leaves, panels, terms = p2m.shape
    classes = m2l.shape[0]
    blocks, rhs, columns = basis.shape
    _, piece = pack_sizes(rhs, blocks * rhs, peers)
    args = (ours, theirs, pick, near, m2l, p2m, basis)
    return pl.pallas_call(
        functools.partial(far_kernel, halves),
        grid=(1,),
        out_shape=(
            jax.ShapeDtypeStruct((rhs, columns), F32),
            jax.ShapeDtypeStruct((peers, piece, 128), F32),
        ),
        in_specs=[whole(a.shape) for a in args],
        out_specs=(whole((rhs, columns)), whole((peers, piece, 128))),
        scratch_shapes=[
            pltpu.VMEM((2 * ours.shape[0], ours.shape[1]), BF16),
            pltpu.VMEM((rhs * leaves, classes * terms), BF16),
            pltpu.VMEM((rhs, leaves, terms), F32),
            pltpu.VMEM((2 * rhs, columns), BF16),
        ],
        compiler_params=params(16),
        name="far",
    )(*args)


def exchange(pieces, axes=AXES):
    return lax.all_to_all(pieces, axes, split_axis=0, concat_axis=0, tiled=True)


def add_kernel(in_ref, out_ref):
    total = jnp.sum(in_ref[...], axis=0)
    out_ref[...] = jnp.broadcast_to(total[None], out_ref.shape)


def added(pieces, copies):
    shape = (copies, *pieces.shape[1:])
    return pl.pallas_call(
        add_kernel,
        grid=(1,),
        out_shape=jax.ShapeDtypeStruct(shape, F32),
        in_specs=[whole(pieces.shape)],
        out_specs=whole(shape),
        compiler_params=params(4),
        name="add",
    )(pieces)


def resid_kernel(total_rows, sums, image, basis, resid_ref, gram_ref, proj_ref):
    blocks, rhs, columns = basis.shape
    wide = blocks * rhs
    proj = unpack(sums, rhs, wide) * (1.0 / total_rows)
    proj_ref[...] = proj.T
    coef = jnp.concatenate(split_parts(proj), axis=0)
    step = 1024
    for i in range(columns // step):
        cols = slice(i * step, (i + 1) * step)
        by_basis = dot(coef, basis[:, :, cols].reshape(wide, step))
        resid = image[:, cols] - (by_basis[:rhs] + by_basis[rhs:])
        resid_ref[:rhs, cols], resid_ref[rhs:, cols] = split_parts(resid)
    both = resid_ref[...]
    square = dot_nt(both, both)
    gram = square[:rhs, :rhs] + square[:rhs, rhs:] + square[rhs:, :rhs] + square[rhs:, rhs:]
    half = rhs // 2
    folded = jnp.concatenate([gram[:half], gram[half:]], axis=1) * (1.0 / total_rows)
    gram_ref[...] = folded


def residual(sums, basis, image, total_rows):
    blocks, rhs, columns = basis.shape
    args = (sums, image, basis)
    shapes = (
        jax.ShapeDtypeStruct((2 * rhs, columns), BF16),
        jax.ShapeDtypeStruct((rhs // 2, 2 * rhs), F32),
        jax.ShapeDtypeStruct((blocks * rhs, rhs), F32),
    )
    return pl.pallas_call(
        functools.partial(resid_kernel, total_rows),
        grid=(1,),
        out_shape=shapes,
        in_specs=[whole(a.shape) for a in args],
        out_specs=tuple(whole(s.shape) for s in shapes),
        compiler_params=params(10),
        name="residual",
    )(*args)


def factored(gram):
    size = gram.shape[0]
    rows = lax.broadcasted_iota(jnp.int32, (size, size), 0)
    cols = lax.broadcasted_iota(jnp.int32, (size, size), 1)
    eye = (rows == cols).astype(F32)
    both = jnp.concatenate([gram, eye], axis=1)
    tiles = [both[8 * i : 8 * i + 8] for i in range(size // 8)]
    sub = lax.broadcasted_iota(jnp.int32, (8, 2 * size), 0)
    for j in range(size):
        t, o = divmod(j, 8)
        row = tiles[t][o : o + 1]
        pivot = 1.0 / row[:, j : j + 1]
        scaled = row * pivot
        for i in range(t, size // 8):
            column = tiles[i][:, j : j + 1]
            change = column * scaled
            if i == t:
                change = jnp.where(sub > o, change, 0.0)
            tiles[i] = tiles[i] - change
    both = jnp.concatenate(tiles, axis=0)
    pivots = jnp.sum(both[:, :size] * eye, axis=1, keepdims=True)
    both = both * (1.0 / jnp.sqrt(pivots))
    upper = jnp.where(cols >= rows, both[:, :size], 0.0)
    return upper.T, both[:, size:]


def tail_kernel(grams, resid, next_ref, factor_ref):
    rhs = factor_ref.shape[0]
    columns = resid.shape[1]
    folded = jnp.sum(grams[...], axis=0)
    gram = jnp.concatenate([folded[:, :rhs], folded[:, rhs:]], axis=0)
    lower, inverse = factored(gram)
    factor_ref[...] = lower
    coef = jnp.concatenate(split_parts(inverse), axis=0)
    step = 1024
    for i in range(columns // step):
        cols = slice(i * step, (i + 1) * step)
        first = dot(coef, resid[:rhs, cols])
        second = dot(coef[:rhs], resid[rhs:, cols])
        next_ref[:, cols] = (first[:rhs] + first[rhs:] + second).astype(BF16)


def tail(grams, resid):
    rhs, columns = resid.shape[0] // 2, resid.shape[1]
    args = (grams, resid)
    shapes = (
        jax.ShapeDtypeStruct((rhs, columns), BF16),
        jax.ShapeDtypeStruct((rhs, rhs), F32),
    )
    return pl.pallas_call(
        tail_kernel,
        grid=(1,),
        out_shape=shapes,
        in_specs=[whole(a.shape) for a in args],
        out_specs=tuple(whole(s.shape) for s in shapes),
        compiler_params=params(6),
        name="tail",
    )(*args)


def shards(
    basis, near_blocks, near_src, near_count, p2m, m2l, send_list, send_count, far_src, far_class
):
    blocks, rhs, columns = basis.shape
    leaves = near_src.shape[0]
    classes, terms, _ = m2l.shape
    devices, near_devices = lax.axis_size("gx"), lax.axis_size("lo")
    peers = 2 * devices * near_devices
    slots = send_list.shape[2]
    total_rows = columns * peers
    halves = 2
    side = lax.axis_index("hi")
    same_side = ("gx", "lo")

    payload, own = all_multipoles(basis, p2m, send_list[0].T, send_count, halves)
    flip = [(0, 1), (1, 0)]
    given = lax.ppermute(payload, "hi", flip)
    up = [(i, i + 1) for i in range(devices - 1)]
    down = [(j, i) for i, j in up]
    before = lax.ppermute(own, "gx", up)
    after = lax.ppermute(own, "gx", down)
    received = []
    for multipoles in (payload, given):
        chosen = chosen_multipoles(side[None], multipoles, leaves, slots, halves, rhs, peers // 2)
        chosen, before, after = lax.optimization_barrier((chosen, before, after))
        got = exchange(chosen.reshape(peers // 2, slots * halves, -1), same_side)
        received.append(got.reshape(chosen.shape))

    near, basis_near, p2m_near, m2l_near = near_field(
        near_src, near_count, before, own, after, near_blocks, (basis, p2m, m2l)
    )

    sender = far_src // slots
    place = sender // (2 * near_devices) * near_devices + sender % near_devices
    place = place + jnp.where(sender // near_devices % 2 == side, 0, peers // 2)
    place = place * slots + far_src % slots
    class_hot = (far_class[:, None, :] == jnp.arange(classes)[None, :, None]).astype(BF16)
    rows = jnp.arange(peers * slots * halves)[None, None, None, :]
    wanted = place[None, :, :, None] * halves + jnp.arange(halves)[:, None, None, None]
    source_hot = (wanted == rows).astype(BF16)
    pick = jnp.einsum("gce,hgef->hcgf", class_hot, source_hot, preferred_element_type=F32)
    pick = pick.astype(BF16).reshape(halves, classes * leaves, -1)

    image, sums = far_field(
        *received, pick, m2l_near, p2m_near, near, basis_near, halves, peers
    )
    sums = exchange(added(exchange(sums), peers))
    resid, gram, projections = residual(sums, basis_near, image, total_rows)
    pair = jnp.stack([gram, lax.ppermute(gram, "hi", flip)])
    grams = exchange(added(pair, peers // 2), same_side)
    next_block, factor = tail(grams, resid)
    return (next_block, projections.reshape(blocks, rhs, rhs), factor)


def solution(mesh):
    devices, segments = mesh.shape["gx"], mesh.shape["bulk"]
    mesh = jax.sharding.Mesh(mesh.devices.reshape(devices, 2, segments // 2), AXES)
    return jax.shard_map(
        shards,
        mesh=mesh,
        in_specs=(
            P(None, None, AXES),
            P(AXES, None, None, None),
            P(AXES, None),
            P(AXES),
            P(AXES, None, None),
            P(),
            P(AXES, None, None),
            P(AXES, None),
            P(AXES, None),
            P(AXES, None),
        ),
        out_specs=(P(None, AXES), P(), P()),
        check_vma=False,
    )
```

```python
import functools

import jax
import jax.numpy as jnp
from jax import lax
from jax.experimental import pallas as pl
from jax.experimental.pallas import tpu as pltpu
from jax.sharding import PartitionSpec as P

F32 = jnp.float32
BF16 = jnp.bfloat16
AXES = ("gx", "hi", "lo")
MIB = 1024 * 1024


def dot(a, b, dims=((1,), (0,)), precision=None):
    return lax.dot_general(a, b, (dims, ((), ())), precision=precision, preferred_element_type=F32)


def dot_nt(a, b, precision=None):
    return dot(a, b, ((1,), (1,)), precision)


def split_parts(values):
    upper = values.astype(BF16)
    lower = (values - upper.astype(F32)).astype(BF16)
    return (upper, lower)


def params(mib):
    return pltpu.CompilerParams(vmem_limit_bytes=mib * MIB)


def in_hbm(array):
    return pltpu.with_memory_space_constraint(array, pltpu.HBM)


def whole(shape):
    return pl.BlockSpec(shape, lambda *_: (0,) * len(shape))


def send_kernel(halves, x, p2m, listed, counts, out, own, scratch, lists):
    leaves, panels, terms = p2m.shape
    rhs = x.shape[1]
    part = rhs // halves
    slots, peers = listed.shape
    own[...] = x[0]
    for g in range(leaves):
        mult = dot(x[0, :, g * panels : (g + 1) * panels], p2m[g])
        for h in range(halves):
            scratch[:, g * halves + h, :] = mult[h * part : (h + 1) * part]
    tall = leaves * halves
    for j in range(part):
        out[j * tall : (j + 1) * tall, :] = scratch[j].astype(BF16)
    lists[...] = jnp.zeros_like(lists)
    lists[:slots, :peers] = listed[...].astype(F32)
    lists[slots : slots + 1, :peers] = counts[...].astype(F32)
    out[part * tall :, :] = lists[...].astype(BF16)


def choose_kernel(halves, slots, leaves, near_devices, side, given, out):
    tall, terms = leaves * halves, given.shape[1]
    rows, part = out.shape[0], out.shape[1] // terms
    each = slots * halves
    receiver = lax.broadcasted_iota(jnp.int32, (rows, terms), 0) // each
    far_part, near_part = receiver // near_devices, receiver % near_devices
    device = far_part * (2 * near_devices) + side[0] * near_devices + near_part
    hot = (device == lax.broadcasted_iota(jnp.int32, (rows, terms), 1)).astype(F32).astype(BF16)
    spread = dot_nt(hot, given[part * tall :, :])
    row = lax.broadcasted_iota(jnp.int32, spread.shape, 0)
    lane = lax.broadcasted_iota(jnp.int32, spread.shape, 1)
    slot = row // halves % slots
    leaf = jnp.sum(jnp.where(lane == slot, spread, 0.0), axis=1, keepdims=True)
    live = jnp.sum(jnp.where(lane == slots, spread, 0.0), axis=1, keepdims=True)
    row = lax.broadcasted_iota(jnp.int32, (rows, tall), 0)
    lane = lax.broadcasted_iota(jnp.int32, (rows, tall), 1).astype(F32)
    held = (row // halves % slots).astype(F32) < live
    wanted = leaf * halves + (row % halves).astype(F32)
    chosen = ((lane == wanted) & held).astype(F32).astype(BF16)
    for j in range(part // 2):
        pair = [given[i * tall : (i + 1) * tall, :] for i in (2 * j, 2 * j + 1)]
        got = dot(chosen, jnp.concatenate(pair, axis=1))
        out[:, j * 2 * terms : (j + 1) * 2 * terms] = got.astype(BF16)


def all_multipoles(basis, p2m, listed, counts, halves):
    blocks, rhs, columns = basis.shape
    leaves, panels, terms = p2m.shape
    shapes = (
        jax.ShapeDtypeStruct((rhs * leaves + 16, terms), BF16),
        jax.ShapeDtypeStruct((rhs, columns), BF16),
    )
    return pl.pallas_call(
        functools.partial(send_kernel, halves),
        grid=(1,),
        out_shape=shapes,
        in_specs=[
            pl.BlockSpec((1, rhs, columns), lambda i: (blocks - 1, 0, 0)),
            whole(p2m.shape),
            whole(listed.shape),
            whole(counts.shape),
        ],
        out_specs=tuple(whole(s.shape) for s in shapes),
        scratch_shapes=[
            pltpu.VMEM((rhs // halves, leaves * halves, terms), F32),
            pltpu.VMEM((16, terms), F32),
        ],
        compiler_params=params(8),
        name="send",
    )(in_hbm(basis), in_hbm(p2m), in_hbm(listed), in_hbm(counts))


def chosen_multipoles(side, given, leaves, slots, halves, rhs, receivers):
    terms = given.shape[1]
    shape = (receivers * slots * halves, rhs // halves * terms)
    return pl.pallas_call(
        functools.partial(choose_kernel, halves, slots, leaves, lax.axis_size("lo")),
        grid=(1,),
        out_shape=jax.ShapeDtypeStruct(shape, BF16),
        in_specs=[pl.BlockSpec(memory_space=pltpu.SMEM), whole(given.shape)],
        out_specs=whole(shape),
        compiler_params=params(8),
        name="choose",
    )(side, given)


def near_kernel(src_ref, count_ref, before, own, after, blocks_ref, out_ref, wide):
    columns = own.shape[1]
    slots, panels = blocks_ref.shape[1], blocks_ref.shape[2]
    g = pl.program_id(0)

    @pl.when(g == 0)
    def _():
        wide[:, :columns] = before[...]
        wide[:, columns : 2 * columns] = own[...]
        wide[:, 2 * columns :] = after[...]

    for i in range(blocks_ref.shape[0]):
        leaf = g * blocks_ref.shape[0] + i
        here = pl.ds(pl.multiple_of(columns + leaf * panels, panels), panels)
        total = [wide[:, here].astype(F32), 0.0]
        for k in range(slots):
            place = pl.multiple_of(src_ref[leaf, k] * panels, panels)
            source = wide[:, pl.ds(place, panels)]
            source = jnp.where(k < count_ref[leaf], source, jnp.zeros_like(source))
            total[k % 2] += dot_nt(source, blocks_ref[i, k])
        out_ref[:, i * panels : (i + 1) * panels] = total[0] + total[1]


def near_field(near_src, near_count, before, own, after, near_blocks):
    leaves, slots, panels, _ = near_blocks.shape
    rhs, columns = own.shape
    grid_spec = pltpu.PrefetchScalarGridSpec(
        num_scalar_prefetch=2,
        grid=(leaves // 2,),
        in_specs=[
            whole((rhs, columns)),
            whole((rhs, columns)),
            whole((rhs, columns)),
            pl.BlockSpec((2, slots, panels, panels), lambda g, *_: (g, 0, 0, 0)),
        ],
        out_specs=pl.BlockSpec((rhs, 2 * panels), lambda g, *_: (0, g)),
        scratch_shapes=[pltpu.VMEM((rhs, 3 * columns), BF16)],
    )
    return pl.pallas_call(
        near_kernel,
        grid_spec=grid_spec,
        out_shape=jax.ShapeDtypeStruct((rhs, columns), F32),
        compiler_params=params(12),
        cost_estimate=pl.CostEstimate(
            flops=2 * rhs * near_blocks.size,
            bytes_accessed=near_blocks.size * 2 + 7 * rhs * columns * 2,
            transcendentals=0,
        ),
        name="near",
    )(near_src, near_count, in_hbm(before), in_hbm(own), in_hbm(after), in_hbm(near_blocks))


def far_kernel(
    halves, ours, theirs, pick, near, m2l_hbm, p2m_hbm, basis_hbm, image_ref, sums_ref, *scratch
):
    recv, lhs, loc, both, m2l, p2m, basis, sems = scratch
    moves = [
        pltpu.make_async_copy(source, target, sems.at[i])
        for i, (source, target) in enumerate(
            ((m2l_hbm, m2l), (p2m_hbm, p2m), (basis_hbm, basis))
        )
    ]
    for move in moves:
        move.start()
    leaves, panels, terms = p2m.shape
    classes = m2l.shape[0]
    blocks, rhs, columns = basis.shape
    part = rhs // halves
    group = 8
    rows = ours.shape[0]
    recv[:rows], recv[rows:] = ours[...], theirs[...]
    for h in range(halves):
        for j in range(0, part, group):
            got = dot(pick[h], recv[:, j * terms : (j + group) * terms]).astype(BF16)
            for t in range(group):
                base = (h * part + j + t) * leaves
                for c in range(classes):
                    lhs[base : base + leaves, c * terms : (c + 1) * terms] = got[
                        c * leaves : (c + 1) * leaves, t * terms : (t + 1) * terms
                    ]
    moves[0].wait()
    weights = m2l[...].reshape(classes * terms, terms)
    tall = 256
    for i in range(rhs * leaves // tall):
        got = dot(lhs[i * tall : (i + 1) * tall, :], weights)
        loc[i * tall // leaves : (i + 1) * tall // leaves] = got.reshape(
            tall // leaves, leaves, terms
        )
    moves[1].wait()
    for g in range(leaves):
        cols = slice(g * panels, (g + 1) * panels)
        image = near[:, cols] + dot_nt(loc[:, g, :].astype(BF16), p2m[g])
        image_ref[:, cols] = image
        both[:rhs, cols], both[rhs:, cols] = split_parts(image)
    moves[2].wait()
    inner = dot_nt(both[...], basis[...].reshape(blocks * rhs, columns))
    pack(inner[:rhs] + inner[rhs:], sums_ref)


def pack_sizes(rhs, wide, peers):
    rows = rhs * wide // 128 // peers
    return rows, -(-rows // 8) * 8


def pack(products, out_ref):
    peers, piece, lanes = out_ref.shape
    rhs, wide = products.shape
    rows, _ = pack_sizes(rhs, wide, peers)
    if rows < piece:
        out_ref[...] = jnp.zeros_like(out_ref)
    tall = jnp.concatenate(
        [products[:, i * lanes : (i + 1) * lanes] for i in range(wide // lanes)], axis=0
    )
    for p in range(peers):
        out_ref[p, :rows, :] = tall[p * rows : (p + 1) * rows]


def unpack(in_ref, rhs, wide):
    peers, _, lanes = in_ref.shape
    rows, _ = pack_sizes(rhs, wide, peers)
    tall = jnp.concatenate([in_ref[p, :rows, :] for p in range(peers)], axis=0)
    return jnp.concatenate(
        [tall[i * rhs : (i + 1) * rhs] for i in range(wide // lanes)], axis=1
    )


def far_field(ours, theirs, pick, m2l, p2m, near, basis, halves, peers):
    leaves, panels, terms = p2m.shape
    classes = m2l.shape[0]
    blocks, rhs, columns = basis.shape
    _, piece = pack_sizes(rhs, blocks * rhs, peers)
    args = (ours, theirs, pick, near)
    anywhere = pl.BlockSpec(memory_space=pl.ANY)
    return pl.pallas_call(
        functools.partial(far_kernel, halves),
        grid=(1,),
        out_shape=(
            jax.ShapeDtypeStruct((rhs, columns), F32),
            jax.ShapeDtypeStruct((peers, piece, 128), F32),
        ),
        in_specs=[whole(a.shape) for a in args] + [anywhere] * 3,
        out_specs=(whole((rhs, columns)), whole((peers, piece, 128))),
        scratch_shapes=[
            pltpu.VMEM((2 * ours.shape[0], ours.shape[1]), BF16),
            pltpu.VMEM((rhs * leaves, classes * terms), BF16),
            pltpu.VMEM((rhs, leaves, terms), F32),
            pltpu.VMEM((2 * rhs, columns), BF16),
            pltpu.VMEM(m2l.shape, BF16),
            pltpu.VMEM(p2m.shape, BF16),
            pltpu.VMEM(basis.shape, BF16),
            pltpu.SemaphoreType.DMA((3,)),
        ],
        compiler_params=params(24),
        name="far",
    )(*args, in_hbm(m2l), in_hbm(p2m), in_hbm(basis))


def exchange(pieces, axes=AXES):
    return lax.all_to_all(pieces, axes, split_axis=0, concat_axis=0, tiled=True)


def add_kernel(in_ref, out_ref):
    total = jnp.sum(in_ref[...], axis=0)
    out_ref[...] = jnp.broadcast_to(total[None], out_ref.shape)


def added(pieces, copies):
    shape = (copies, *pieces.shape[1:])
    return pl.pallas_call(
        add_kernel,
        grid=(1,),
        out_shape=jax.ShapeDtypeStruct(shape, F32),
        in_specs=[whole(pieces.shape)],
        out_specs=whole(shape),
        compiler_params=params(4),
        name="add",
    )(pieces)


def resid_kernel(total_rows, sums, image, basis_hbm, resid_ref, gram_ref, proj_ref, basis, sems):
    blocks, rhs, columns = basis.shape
    wide = blocks * rhs
    steps = sems.shape[0]
    step = columns // steps
    moves = []
    for i in range(steps):
        part = (slice(None), slice(None), pl.ds(i * step, step))
        moves.append(pltpu.make_async_copy(basis_hbm.at[part], basis.at[part], sems.at[i]))
        moves[i].start()
    proj = unpack(sums, rhs, wide) * (1.0 / total_rows)
    proj_ref[...] = proj.T
    coef = jnp.concatenate(split_parts(proj), axis=0)
    for i in range(steps):
        cols = slice(i * step, (i + 1) * step)
        moves[i].wait()
        by_basis = dot(coef, basis[:, :, cols].reshape(wide, step))
        resid = image[:, cols] - (by_basis[:rhs] + by_basis[rhs:])
        resid_ref[:rhs, cols], resid_ref[rhs:, cols] = split_parts(resid)
    both = resid_ref[...]
    square = dot_nt(both, both)
    gram = square[:rhs, :rhs] + square[:rhs, rhs:] + square[rhs:, :rhs] + square[rhs:, rhs:]
    half = rhs // 2
    folded = jnp.concatenate([gram[:half], gram[half:]], axis=1) * (1.0 / total_rows)
    gram_ref[...] = folded


def residual(sums, basis, image, total_rows):
    blocks, rhs, columns = basis.shape
    args = (sums, image)
    shapes = (
        jax.ShapeDtypeStruct((2 * rhs, columns), BF16),
        jax.ShapeDtypeStruct((rhs // 2, 2 * rhs), F32),
        jax.ShapeDtypeStruct((blocks * rhs, rhs), F32),
    )
    return pl.pallas_call(
        functools.partial(resid_kernel, total_rows),
        grid=(1,),
        out_shape=shapes,
        in_specs=[whole(a.shape) for a in args] + [pl.BlockSpec(memory_space=pl.ANY)],
        out_specs=tuple(whole(s.shape) for s in shapes),
        scratch_shapes=[pltpu.VMEM(basis.shape, BF16), pltpu.SemaphoreType.DMA((4,))],
        compiler_params=params(16),
        name="residual",
    )(*args, in_hbm(basis))


def factored(gram, done):
    size = gram.shape[0]
    rows = lax.broadcasted_iota(jnp.int32, (size, size), 0)
    cols = lax.broadcasted_iota(jnp.int32, (size, size), 1)
    both = jnp.concatenate([gram, (rows == cols).astype(F32)], axis=1)
    tiles = [both[8 * i : 8 * i + 8] for i in range(size // 8)]
    for j in range(0, size, 2):
        t, o = divmod(j, 8)
        first, second = tiles[t][o : o + 1], tiles[t][o + 1 : o + 2]
        a, b, c = first[:, j : j + 1], first[:, j + 1 : j + 2], second[:, j + 1 : j + 2]
        scale = 1.0 / (a * c - b * b)
        upper = (c * first - b * second) * scale
        lower = (a * second - b * first) * scale
        for i in range(t, size // 8):
            change = tiles[i][:, j : j + 1] * upper + tiles[i][:, j + 1 : j + 2] * lower
            tiles[i] = tiles[i] - change
        ratio = b / a
        done[j : j + 1, :] = first / jnp.sqrt(a)
        done[j + 1 : j + 2, :] = (second - ratio * first) / jnp.sqrt(c - ratio * b)
    both = done[...]
    return jnp.where(cols >= rows, both[:, :size], 0.0).T, both[:, size:]


def tail_kernel(grams, resid, next_ref, factor_ref, done):
    rhs = factor_ref.shape[0]
    columns = resid.shape[1]
    folded = jnp.sum(grams[...], axis=0)
    gram = jnp.concatenate([folded[:, :rhs], folded[:, rhs:]], axis=0)
    lower, inverse = factored(gram, done)
    factor_ref[...] = lower
    coef = jnp.concatenate(split_parts(inverse), axis=0)
    step = 1024
    for i in range(columns // step):
        cols = slice(i * step, (i + 1) * step)
        first = dot(coef, resid[:rhs, cols])
        second = dot(coef[:rhs], resid[rhs:, cols])
        next_ref[:, cols] = (first[:rhs] + first[rhs:] + second).astype(BF16)


def tail(grams, resid):
    rhs, columns = resid.shape[0] // 2, resid.shape[1]
    args = (grams, resid)
    shapes = (
        jax.ShapeDtypeStruct((rhs, columns), BF16),
        jax.ShapeDtypeStruct((rhs, rhs), F32),
    )
    return pl.pallas_call(
        tail_kernel,
        grid=(1,),
        out_shape=shapes,
        in_specs=[whole(a.shape) for a in args],
        out_specs=tuple(whole(s.shape) for s in shapes),
        scratch_shapes=[pltpu.VMEM((rhs, 2 * rhs), F32)],
        compiler_params=params(6),
        name="tail",
    )(*args)


def shards(
    basis, near_blocks, near_src, near_count, p2m, m2l, send_list, send_count, far_src, far_class
):
    blocks, rhs, columns = basis.shape
    leaves = near_src.shape[0]
    classes, terms, _ = m2l.shape
    devices, near_devices = lax.axis_size("gx"), lax.axis_size("lo")
    peers = 2 * devices * near_devices
    slots = send_list.shape[2]
    total_rows = columns * peers
    halves = 2
    side = lax.axis_index("hi")
    same_side = ("gx", "lo")

    payload, own = all_multipoles(basis, p2m, send_list[0].T, send_count, halves)
    flip = [(0, 1), (1, 0)]
    given = lax.ppermute(payload, "hi", flip)
    up = [(i, i + 1) for i in range(devices - 1)]
    down = [(j, i) for i, j in up]
    before = lax.ppermute(own, "gx", up)
    after = lax.ppermute(own, "gx", down)
    given, before, after = lax.optimization_barrier((given, before, after))
    received = []
    for multipoles in (payload, given):
        chosen = chosen_multipoles(side[None], multipoles, leaves, slots, halves, rhs, peers // 2)
        got = exchange(chosen.reshape(peers // 2, slots * halves, -1), same_side)
        received.append(got.reshape(chosen.shape))

    near = near_field(near_src, near_count, before, own, after, near_blocks)

    sender = far_src // slots
    place = sender // (2 * near_devices) * near_devices + sender % near_devices
    place = place + jnp.where(sender // near_devices % 2 == side, 0, peers // 2)
    place = place * slots + far_src % slots
    class_hot = (far_class[:, None, :] == jnp.arange(classes)[None, :, None]).astype(BF16)
    rows = jnp.arange(peers * slots * halves)[None, None, None, :]
    wanted = place[None, :, :, None] * halves + jnp.arange(halves)[:, None, None, None]
    source_hot = (wanted == rows).astype(BF16)
    pick = jnp.einsum("gce,hgef->hcgf", class_hot, source_hot, preferred_element_type=F32)
    pick = pick.astype(BF16).reshape(halves, classes * leaves, -1)

    image, sums = far_field(*received, pick, m2l, p2m, near, basis, halves, peers)
    sums = exchange(added(exchange(sums), peers))
    resid, gram, projections = residual(sums, basis, image, total_rows)
    pair = jnp.stack([gram, lax.ppermute(gram, "hi", flip)])
    grams = exchange(added(pair, peers // 2), same_side)
    next_block, factor = tail(grams, resid)
    return (next_block, projections.reshape(blocks, rhs, rhs), factor)


def solution(mesh):
    devices, segments = mesh.shape["gx"], mesh.shape["bulk"]
    mesh = jax.sharding.Mesh(mesh.devices.reshape(devices, 2, segments // 2), AXES)
    return jax.shard_map(
        shards,
        mesh=mesh,
        in_specs=(
            P(None, None, AXES),
            P(AXES, None, None, None),
            P(AXES, None),
            P(AXES),
            P(AXES, None, None),
            P(),
            P(AXES, None, None),
            P(AXES, None),
            P(AXES, None),
            P(AXES, None),
        ),
        out_specs=(P(None, AXES), P(), P()),
        check_vma=False,
    )
```

```python
import functools

import jax
import jax.numpy as jnp
from jax import lax
from jax.experimental import pallas as pl
from jax.experimental.pallas import tpu as pltpu
from jax.sharding import PartitionSpec as P

F32 = jnp.float32
BF16 = jnp.bfloat16
AXES = ("gx", "hi", "lo")
MIB = 1024 * 1024


def dot(a, b, dims=((1,), (0,)), precision=None):
    return lax.dot_general(a, b, (dims, ((), ())), precision=precision, preferred_element_type=F32)


def dot_nt(a, b, precision=None):
    return dot(a, b, ((1,), (1,)), precision)


def split_parts(values):
    upper = values.astype(BF16)
    lower = (values - upper.astype(F32)).astype(BF16)
    return (upper, lower)


def params(mib):
    return pltpu.CompilerParams(vmem_limit_bytes=mib * MIB)


def in_hbm(array):
    return pltpu.with_memory_space_constraint(array, pltpu.HBM)


def whole(shape):
    return pl.BlockSpec(shape, lambda *_: (0,) * len(shape))


def send_kernel(halves, x, p2m, listed, counts, out, own_top, own_low, scratch, lists):
    leaves, panels, terms = p2m.shape
    rhs = x.shape[1]
    part = rhs // halves
    slots, peers = listed.shape
    own_top[...], own_low[...] = x[0, : rhs // 2], x[0, rhs // 2 :]
    for g in range(leaves):
        mult = dot(x[0, :, g * panels : (g + 1) * panels], p2m[g])
        for h in range(halves):
            scratch[:, g * halves + h, :] = mult[h * part : (h + 1) * part]
    tall = leaves * halves
    for j in range(part):
        out[j * tall : (j + 1) * tall, :] = scratch[j].astype(BF16)
    lists[...] = jnp.zeros_like(lists)
    lists[:slots, :peers] = listed[...].astype(F32)
    lists[slots : slots + 1, :peers] = counts[...].astype(F32)
    out[part * tall :, :] = lists[...].astype(BF16)


def choose_kernel(halves, slots, leaves, near_devices, side, given, out):
    tall, terms = leaves * halves, given.shape[1]
    rows, part = out.shape[0], out.shape[1] // terms
    each = slots * halves
    receiver = lax.broadcasted_iota(jnp.int32, (rows, terms), 0) // each
    far_part, near_part = receiver // near_devices, receiver % near_devices
    device = far_part * (2 * near_devices) + side[0] * near_devices + near_part
    hot = (device == lax.broadcasted_iota(jnp.int32, (rows, terms), 1)).astype(F32).astype(BF16)
    spread = dot_nt(hot, given[part * tall :, :])
    row = lax.broadcasted_iota(jnp.int32, spread.shape, 0)
    lane = lax.broadcasted_iota(jnp.int32, spread.shape, 1)
    slot = row // halves % slots
    leaf = jnp.sum(jnp.where(lane == slot, spread, 0.0), axis=1, keepdims=True)
    live = jnp.sum(jnp.where(lane == slots, spread, 0.0), axis=1, keepdims=True)
    row = lax.broadcasted_iota(jnp.int32, (rows, tall), 0)
    lane = lax.broadcasted_iota(jnp.int32, (rows, tall), 1).astype(F32)
    held = (row // halves % slots).astype(F32) < live
    wanted = leaf * halves + (row % halves).astype(F32)
    chosen = ((lane == wanted) & held).astype(F32).astype(BF16)
    for j in range(part // 2):
        pair = [given[i * tall : (i + 1) * tall, :] for i in (2 * j, 2 * j + 1)]
        got = dot(chosen, jnp.concatenate(pair, axis=1))
        out[:, j * 2 * terms : (j + 1) * 2 * terms] = got.astype(BF16)


def all_multipoles(basis, p2m, listed, counts, halves):
    blocks, rhs, columns = basis.shape
    leaves, panels, terms = p2m.shape
    shapes = (
        jax.ShapeDtypeStruct((rhs * leaves + 16, terms), BF16),
        jax.ShapeDtypeStruct((rhs // 2, columns), BF16),
        jax.ShapeDtypeStruct((rhs // 2, columns), BF16),
    )
    return pl.pallas_call(
        functools.partial(send_kernel, halves),
        grid=(1,),
        out_shape=shapes,
        in_specs=[
            pl.BlockSpec((1, rhs, columns), lambda i: (blocks - 1, 0, 0)),
            whole(p2m.shape),
            whole(listed.shape),
            whole(counts.shape),
        ],
        out_specs=tuple(whole(s.shape) for s in shapes),
        scratch_shapes=[
            pltpu.VMEM((rhs // halves, leaves * halves, terms), F32),
            pltpu.VMEM((16, terms), F32),
        ],
        compiler_params=params(8),
        name="send",
    )(in_hbm(basis), in_hbm(p2m), in_hbm(listed), in_hbm(counts))


def chosen_multipoles(side, given, leaves, slots, halves, rhs, receivers):
    terms = given.shape[1]
    shape = (receivers * slots * halves, rhs // halves * terms)
    return pl.pallas_call(
        functools.partial(choose_kernel, halves, slots, leaves, lax.axis_size("lo")),
        grid=(1,),
        out_shape=jax.ShapeDtypeStruct(shape, BF16),
        in_specs=[pl.BlockSpec(memory_space=pltpu.SMEM), whole(given.shape)],
        out_specs=whole(shape),
        compiler_params=params(8),
        name="choose",
    )(side, given)


def near_kernel(src_ref, count_ref, *refs):
    pieces, (blocks_ref, out_ref, wide) = refs[:6], refs[6:]
    half, columns = pieces[0].shape
    slots, panels = blocks_ref.shape[1], blocks_ref.shape[2]
    g = pl.program_id(0)

    @pl.when(g == 0)
    def _():
        for i, piece in enumerate(pieces):
            rows, place = slice(i % 2 * half, (i % 2 + 1) * half), i // 2 * columns
            wide[rows, place : place + columns] = piece[...]

    for i in range(blocks_ref.shape[0]):
        leaf = g * blocks_ref.shape[0] + i
        here = pl.ds(pl.multiple_of(columns + leaf * panels, panels), panels)
        total = [wide[:, here].astype(F32), 0.0]
        for k in range(slots):
            place = pl.multiple_of(src_ref[k, leaf] * panels, panels)
            source = wide[:, pl.ds(place, panels)]
            source = jnp.where(k < count_ref[leaf], source, jnp.zeros_like(source))
            total[k % 2] += dot_nt(source, blocks_ref[i, k])
        out_ref[:, i * panels : (i + 1) * panels] = total[0] + total[1]


def near_field(near_src, near_count, pieces, near_blocks):
    leaves, slots, panels, _ = near_blocks.shape
    half, columns = pieces[0].shape
    rhs = 2 * half
    grid_spec = pltpu.PrefetchScalarGridSpec(
        num_scalar_prefetch=2,
        grid=(leaves // 2,),
        in_specs=[
            *[whole((half, columns))] * 6,
            pl.BlockSpec((2, slots, panels, panels), lambda g, *_: (g, 0, 0, 0)),
        ],
        out_specs=pl.BlockSpec((rhs, 2 * panels), lambda g, *_: (0, g)),
        scratch_shapes=[pltpu.VMEM((rhs, 3 * columns), BF16)],
    )
    return pl.pallas_call(
        near_kernel,
        grid_spec=grid_spec,
        out_shape=jax.ShapeDtypeStruct((rhs, columns), F32),
        compiler_params=params(12),
        cost_estimate=pl.CostEstimate(
            flops=2 * rhs * near_blocks.size,
            bytes_accessed=near_blocks.size * 2 + 7 * rhs * columns * 2,
            transcendentals=0,
        ),
        name="near",
    )(near_src.T, near_count, *[in_hbm(p) for p in pieces], in_hbm(near_blocks))


def far_kernel(
    halves, ours, theirs, pick, near, m2l_hbm, p2m_hbm, basis_hbm, image_ref, sums_ref, basis, *scratch
):
    recv, lhs, loc, both, m2l, p2m, sems = scratch
    moves = [
        pltpu.make_async_copy(source, target, sems.at[i])
        for i, (source, target) in enumerate(
            ((m2l_hbm, m2l), (p2m_hbm, p2m), (basis_hbm, basis))
        )
    ]
    for move in moves:
        move.start()
    leaves, panels, terms = p2m.shape
    classes = m2l.shape[0]
    blocks, rhs, columns = basis.shape
    part = rhs // halves
    group = 8
    rows = ours.shape[0]
    recv[:rows], recv[rows:] = ours[...], theirs[...]
    for h in range(halves):
        for j in range(0, part, group):
            got = dot(pick[h], recv[:, j * terms : (j + group) * terms]).astype(BF16)
            for t in range(group):
                base = (h * part + j + t) * leaves
                for c in range(classes):
                    lhs[base : base + leaves, c * terms : (c + 1) * terms] = got[
                        c * leaves : (c + 1) * leaves, t * terms : (t + 1) * terms
                    ]
    moves[0].wait()
    weights = m2l[...].reshape(classes * terms, terms)
    tall = 256
    for i in range(rhs * leaves // tall):
        got = dot(lhs[i * tall : (i + 1) * tall, :], weights)
        loc[i * tall // leaves : (i + 1) * tall // leaves] = got.reshape(
            tall // leaves, leaves, terms
        )
    moves[1].wait()
    for g in range(leaves):
        cols = slice(g * panels, (g + 1) * panels)
        image = near[:, cols] + dot_nt(loc[:, g, :].astype(BF16), p2m[g])
        image_ref[:, cols] = image
        both[:rhs, cols], both[rhs:, cols] = split_parts(image)
    moves[2].wait()
    inner = dot_nt(both[...], basis[...].reshape(blocks * rhs, columns))
    pack(inner[:rhs] + inner[rhs:], sums_ref)


def pack_sizes(rhs, wide, peers):
    rows = rhs * wide // 128 // peers
    return rows, -(-rows // 8) * 8


def pack(products, out_ref):
    peers, piece, lanes = out_ref.shape
    rhs, wide = products.shape
    rows, _ = pack_sizes(rhs, wide, peers)
    if rows < piece:
        out_ref[...] = jnp.zeros_like(out_ref)
    tall = jnp.concatenate(
        [products[:, i * lanes : (i + 1) * lanes] for i in range(wide // lanes)], axis=0
    )
    for p in range(peers):
        out_ref[p, :rows, :] = tall[p * rows : (p + 1) * rows]


def unpack(in_ref, rhs, wide):
    peers, _, lanes = in_ref.shape
    rows, _ = pack_sizes(rhs, wide, peers)
    tall = jnp.concatenate([in_ref[p, :rows, :] for p in range(peers)], axis=0)
    return jnp.concatenate(
        [tall[i * rhs : (i + 1) * rhs] for i in range(wide // lanes)], axis=1
    )


def far_field(ours, theirs, pick, m2l, p2m, near, basis, halves, peers):
    leaves, panels, terms = p2m.shape
    classes = m2l.shape[0]
    blocks, rhs, columns = basis.shape
    _, piece = pack_sizes(rhs, blocks * rhs, peers)
    args = (ours, theirs, pick, near)
    anywhere = pl.BlockSpec(memory_space=pl.ANY)
    return pl.pallas_call(
        functools.partial(far_kernel, halves),
        grid=(1,),
        out_shape=(
            jax.ShapeDtypeStruct((rhs, columns), F32),
            jax.ShapeDtypeStruct((peers, piece, 128), F32),
            pltpu.VMEM(basis.shape, BF16),
        ),
        in_specs=[whole(a.shape) for a in args] + [anywhere] * 3,
        out_specs=(
            whole((rhs, columns)),
            whole((peers, piece, 128)),
            pl.BlockSpec(memory_space=pltpu.VMEM),
        ),
        scratch_shapes=[
            pltpu.VMEM((2 * ours.shape[0], ours.shape[1]), BF16),
            pltpu.VMEM((rhs * leaves, classes * terms), BF16),
            pltpu.VMEM((rhs, leaves, terms), F32),
            pltpu.VMEM((2 * rhs, columns), BF16),
            pltpu.VMEM(m2l.shape, BF16),
            pltpu.VMEM(p2m.shape, BF16),
            pltpu.SemaphoreType.DMA((3,)),
        ],
        compiler_params=params(24),
        name="far",
    )(*args, in_hbm(m2l), in_hbm(p2m), in_hbm(basis))


def exchange(pieces, axes=AXES):
    return lax.all_to_all(pieces, axes, split_axis=0, concat_axis=0, tiled=True)


def add_kernel(in_ref, out_ref):
    total = jnp.sum(in_ref[...], axis=0)
    out_ref[...] = jnp.broadcast_to(total[None], out_ref.shape)


def added(pieces, copies):
    shape = (copies, *pieces.shape[1:])
    return pl.pallas_call(
        add_kernel,
        grid=(1,),
        out_shape=jax.ShapeDtypeStruct(shape, F32),
        in_specs=[whole(pieces.shape)],
        out_specs=whole(shape),
        compiler_params=params(4),
        name="add",
    )(pieces)


def resid_kernel(total_rows, sums, image, basis, resid_ref, gram_ref, proj_ref):
    blocks, rhs, columns = basis.shape
    wide = blocks * rhs
    proj = unpack(sums, rhs, wide) * (1.0 / total_rows)
    proj_ref[...] = proj.T
    coef = jnp.concatenate(split_parts(proj), axis=0)
    step = 1024
    for i in range(columns // step):
        cols = slice(i * step, (i + 1) * step)
        by_basis = dot(coef, basis[:, :, cols].reshape(wide, step))
        resid = image[:, cols] - (by_basis[:rhs] + by_basis[rhs:])
        resid_ref[:rhs, cols], resid_ref[rhs:, cols] = split_parts(resid)
    both = resid_ref[...]
    square = dot_nt(both, both)
    gram = square[:rhs, :rhs] + square[:rhs, rhs:] + square[rhs:, :rhs] + square[rhs:, rhs:]
    half = rhs // 2
    folded = jnp.concatenate([gram[:half], gram[half:]], axis=1) * (1.0 / total_rows)
    gram_ref[...] = folded


def residual(sums, basis, image, total_rows):
    blocks, rhs, columns = basis.shape
    args = (sums, image, basis)
    shapes = (
        jax.ShapeDtypeStruct((2 * rhs, columns), BF16),
        jax.ShapeDtypeStruct((rhs // 2, 2 * rhs), F32),
        jax.ShapeDtypeStruct((blocks * rhs, rhs), F32),
    )
    return pl.pallas_call(
        functools.partial(resid_kernel, total_rows),
        grid=(1,),
        out_shape=shapes,
        in_specs=[whole(a.shape) for a in args],
        out_specs=tuple(whole(s.shape) for s in shapes),
        compiler_params=params(24),
        name="residual",
    )(*args)


def factored(gram, done):
    size = gram.shape[0]
    rows = lax.broadcasted_iota(jnp.int32, (size, size), 0)
    cols = lax.broadcasted_iota(jnp.int32, (size, size), 1)
    both = jnp.concatenate([gram, (rows == cols).astype(F32)], axis=1)
    tiles = [both[8 * i : 8 * i + 8] for i in range(size // 8)]
    for j in range(0, size, 2):
        t, o = divmod(j, 8)
        first, second = tiles[t][o : o + 1], tiles[t][o + 1 : o + 2]
        a, b, c = first[:, j : j + 1], first[:, j + 1 : j + 2], second[:, j + 1 : j + 2]
        scale = 1.0 / (a * c - b * b)
        upper = (c * first - b * second) * scale
        lower = (a * second - b * first) * scale
        for i in range(t, size // 8):
            change = tiles[i][:, j : j + 1] * upper + tiles[i][:, j + 1 : j + 2] * lower
            tiles[i] = tiles[i] - change
        ratio = b / a
        done[j : j + 1, :] = first / jnp.sqrt(a)
        done[j + 1 : j + 2, :] = (second - ratio * first) / jnp.sqrt(c - ratio * b)
    both = done[...]
    return jnp.where(cols >= rows, both[:, :size], 0.0).T, both[:, size:]


def tail_kernel(grams, resid, next_ref, factor_ref, done):
    rhs = factor_ref.shape[0]
    columns = resid.shape[1]
    folded = jnp.sum(grams[...], axis=0)
    gram = jnp.concatenate([folded[:, :rhs], folded[:, rhs:]], axis=0)
    lower, inverse = factored(gram, done)
    factor_ref[...] = lower
    coef = jnp.concatenate(split_parts(inverse), axis=0)
    step = 1024
    for i in range(columns // step):
        cols = slice(i * step, (i + 1) * step)
        first = dot(coef, resid[:rhs, cols])
        second = dot(coef[:rhs], resid[rhs:, cols])
        next_ref[:, cols] = (first[:rhs] + first[rhs:] + second).astype(BF16)


def tail(grams, resid):
    rhs, columns = resid.shape[0] // 2, resid.shape[1]
    args = (grams, resid)
    shapes = (
        jax.ShapeDtypeStruct((rhs, columns), BF16),
        jax.ShapeDtypeStruct((rhs, rhs), F32),
    )
    return pl.pallas_call(
        tail_kernel,
        grid=(1,),
        out_shape=shapes,
        in_specs=[whole(a.shape) for a in args],
        out_specs=tuple(whole(s.shape) for s in shapes),
        scratch_shapes=[pltpu.VMEM((rhs, 2 * rhs), F32)],
        compiler_params=params(6),
        name="tail",
    )(*args)


def shards(
    basis, near_blocks, near_src, near_count, p2m, m2l, send_list, send_count, far_src, far_class
):
    blocks, rhs, columns = basis.shape
    leaves = near_src.shape[0]
    classes, terms, _ = m2l.shape
    devices, near_devices = lax.axis_size("gx"), lax.axis_size("lo")
    peers = 2 * devices * near_devices
    slots = send_list.shape[2]
    total_rows = columns * peers
    halves = 2
    side = lax.axis_index("hi")
    same_side = ("gx", "lo")

    payload, *own = all_multipoles(basis, p2m, send_list[0].T, send_count, halves)
    flip = [(0, 1), (1, 0)]
    given = lax.ppermute(payload, "hi", flip)
    up = [(i, i + 1) for i in range(devices - 1)]
    down = [(j, i) for i, j in up]
    pieces = [lax.ppermute(half, "gx", way) for way in (up, down) for half in own]

    sender = far_src // slots
    place = sender // (2 * near_devices) * near_devices + sender % near_devices
    place = place + jnp.where(sender // near_devices % 2 == side, 0, peers // 2)
    place = place * slots + far_src % slots
    class_hot = (far_class[:, None, :] == jnp.arange(classes)[None, :, None]).astype(BF16)
    rows = jnp.arange(peers * slots * halves)[None, None, None, :]
    wanted = place[None, :, :, None] * halves + jnp.arange(halves)[:, None, None, None]
    source_hot = (wanted == rows).astype(BF16)
    pick = jnp.einsum("gce,hgef->hcgf", class_hot, source_hot, preferred_element_type=F32)
    pick = pick.astype(BF16).reshape(halves, classes * leaves, -1)

    given, pick = lax.optimization_barrier((given, pick))
    received = []
    for multipoles in (payload, given):
        chosen = chosen_multipoles(side[None], multipoles, leaves, slots, halves, rhs, peers // 2)
        if multipoles is given:
            chosen, *pieces = lax.optimization_barrier((chosen, *pieces))
        got = exchange(chosen.reshape(peers // 2, slots * halves, -1), same_side)
        received.append(got.reshape(chosen.shape))

    pieces = [*pieces[:2], *own, *pieces[2:]]
    near = near_field(near_src, near_count, pieces, near_blocks)
    image, sums, basis_near = far_field(*received, pick, m2l, p2m, near, basis, halves, peers)
    sums = exchange(added(exchange(sums), peers))
    resid, gram, projections = residual(sums, basis_near, image, total_rows)
    pair = jnp.stack([gram, lax.ppermute(gram, "hi", flip)])
    grams = exchange(added(pair, peers // 2), same_side)
    next_block, factor = tail(grams, resid)
    return (next_block, projections.reshape(blocks, rhs, rhs), factor)


def solution(mesh):
    devices, segments = mesh.shape["gx"], mesh.shape["bulk"]
    mesh = jax.sharding.Mesh(mesh.devices.reshape(devices, 2, segments // 2), AXES)
    return jax.shard_map(
        shards,
        mesh=mesh,
        in_specs=(
            P(None, None, AXES),
            P(AXES, None, None, None),
            P(AXES, None),
            P(AXES),
            P(AXES, None, None),
            P(),
            P(AXES, None, None),
            P(AXES, None),
            P(AXES, None),
            P(AXES, None),
        ),
        out_specs=(P(None, AXES), P(), P()),
        check_vma=False,
    )
```

```python
import functools

import jax
import jax.numpy as jnp
from jax import lax
from jax.experimental import pallas as pl
from jax.experimental.pallas import tpu as pltpu
from jax.sharding import PartitionSpec as P

F32 = jnp.float32
BF16 = jnp.bfloat16
AXES = ("gx", "hi", "lo")
MIB = 1024 * 1024


def dot(a, b, dims=((1,), (0,)), precision=None):
    return lax.dot_general(a, b, (dims, ((), ())), precision=precision, preferred_element_type=F32)


def dot_nt(a, b, precision=None):
    return dot(a, b, ((1,), (1,)), precision)


def split_parts(values):
    upper = values.astype(BF16)
    lower = (values - upper.astype(F32)).astype(BF16)
    return (upper, lower)


def params(mib):
    return pltpu.CompilerParams(vmem_limit_bytes=mib * MIB)


def in_hbm(array):
    return pltpu.with_memory_space_constraint(array, pltpu.HBM)


def whole(shape):
    return pl.BlockSpec(shape, lambda *_: (0,) * len(shape))


def send_kernel(halves, x, p2m, listed, counts, out, own, scratch, lists):
    leaves, panels, terms = p2m.shape
    rhs = x.shape[1]
    part = rhs // halves
    slots, peers = listed.shape
    own[...] = x[0]
    for g in range(leaves):
        mult = dot(x[0, :, g * panels : (g + 1) * panels], p2m[g])
        for h in range(halves):
            scratch[:, g * halves + h, :] = mult[h * part : (h + 1) * part]
    tall = leaves * halves
    for j in range(part):
        out[j * tall : (j + 1) * tall, :] = scratch[j].astype(BF16)
    lists[...] = jnp.zeros_like(lists)
    lists[:slots, :peers] = listed[...].astype(F32)
    lists[slots : slots + 1, :peers] = counts[...].astype(F32)
    out[part * tall :, :] = lists[...].astype(BF16)


def choose_kernel(halves, slots, leaves, near_devices, side, given, out):
    tall, terms = leaves * halves, given.shape[1]
    rows, part = out.shape[0], out.shape[1] // terms
    each = slots * halves
    receiver = lax.broadcasted_iota(jnp.int32, (rows, terms), 0) // each
    far_part, near_part = receiver // near_devices, receiver % near_devices
    device = far_part * (2 * near_devices) + side[0] * near_devices + near_part
    hot = (device == lax.broadcasted_iota(jnp.int32, (rows, terms), 1)).astype(F32).astype(BF16)
    spread = dot_nt(hot, given[part * tall :, :])
    row = lax.broadcasted_iota(jnp.int32, spread.shape, 0)
    lane = lax.broadcasted_iota(jnp.int32, spread.shape, 1)
    slot = row // halves % slots
    leaf = jnp.sum(jnp.where(lane == slot, spread, 0.0), axis=1, keepdims=True)
    live = jnp.sum(jnp.where(lane == slots, spread, 0.0), axis=1, keepdims=True)
    row = lax.broadcasted_iota(jnp.int32, (rows, tall), 0)
    lane = lax.broadcasted_iota(jnp.int32, (rows, tall), 1).astype(F32)
    held = (row // halves % slots).astype(F32) < live
    wanted = leaf * halves + (row % halves).astype(F32)
    chosen = ((lane == wanted) & held).astype(F32).astype(BF16)
    for j in range(part // 2):
        pair = [given[i * tall : (i + 1) * tall, :] for i in (2 * j, 2 * j + 1)]
        got = dot(chosen, jnp.concatenate(pair, axis=1))
        out[:, j * 2 * terms : (j + 1) * 2 * terms] = got.astype(BF16)


def all_multipoles(basis, p2m, listed, counts, halves):
    blocks, rhs, columns = basis.shape
    leaves, panels, terms = p2m.shape
    shapes = (
        jax.ShapeDtypeStruct((rhs * leaves + 16, terms), BF16),
        jax.ShapeDtypeStruct((rhs, columns), BF16),
    )
    return pl.pallas_call(
        functools.partial(send_kernel, halves),
        grid=(1,),
        out_shape=shapes,
        in_specs=[
            pl.BlockSpec((1, rhs, columns), lambda i: (blocks - 1, 0, 0)),
            whole(p2m.shape),
            whole(listed.shape),
            whole(counts.shape),
        ],
        out_specs=tuple(whole(s.shape) for s in shapes),
        scratch_shapes=[
            pltpu.VMEM((rhs // halves, leaves * halves, terms), F32),
            pltpu.VMEM((16, terms), F32),
        ],
        compiler_params=params(8),
        name="send",
    )(in_hbm(basis), in_hbm(p2m), in_hbm(listed), in_hbm(counts))


def chosen_multipoles(side, given, leaves, slots, halves, rhs, receivers):
    terms = given.shape[1]
    shape = (receivers * slots * halves, rhs // halves * terms)
    return pl.pallas_call(
        functools.partial(choose_kernel, halves, slots, leaves, lax.axis_size("lo")),
        grid=(1,),
        out_shape=jax.ShapeDtypeStruct(shape, BF16),
        in_specs=[pl.BlockSpec(memory_space=pltpu.SMEM), whole(given.shape)],
        out_specs=whole(shape),
        compiler_params=params(8),
        cost_estimate=pl.CostEstimate(flops=7 * 10**10, bytes_accessed=0, transcendentals=0),
        name="choose",
    )(side, given)


def near_kernel(src_ref, count_ref, *refs):
    pieces, (blocks_ref, out_ref, wide) = refs[:3], refs[3:]
    columns = pieces[0].shape[1]
    slots, panels = blocks_ref.shape[1], blocks_ref.shape[2]
    g = pl.program_id(0)

    @pl.when(g == 0)
    def _():
        for i, piece in enumerate(pieces):
            wide[:, i * columns : (i + 1) * columns] = piece[...]

    for i in range(blocks_ref.shape[0]):
        leaf = g * blocks_ref.shape[0] + i
        here = pl.ds(pl.multiple_of(columns + leaf * panels, panels), panels)
        total = [wide[:, here].astype(F32), 0.0]
        for k in range(slots):
            place = pl.multiple_of(src_ref[k, leaf] * panels, panels)
            source = wide[:, pl.ds(place, panels)]
            source = jnp.where(k < count_ref[leaf], source, jnp.zeros_like(source))
            total[k % 2] += dot_nt(source, blocks_ref[i, k])
        out_ref[:, i * panels : (i + 1) * panels] = total[0] + total[1]


def near_field(near_src, near_count, pieces, near_blocks):
    leaves, slots, panels, _ = near_blocks.shape
    rhs, columns = pieces[0].shape
    grid_spec = pltpu.PrefetchScalarGridSpec(
        num_scalar_prefetch=2,
        grid=(leaves // 2,),
        in_specs=[
            *[whole((rhs, columns))] * 3,
            pl.BlockSpec((2, slots, panels, panels), lambda g, *_: (g, 0, 0, 0)),
        ],
        out_specs=pl.BlockSpec((rhs, 2 * panels), lambda g, *_: (0, g)),
        scratch_shapes=[pltpu.VMEM((rhs, 3 * columns), BF16)],
    )
    return pl.pallas_call(
        near_kernel,
        grid_spec=grid_spec,
        out_shape=jax.ShapeDtypeStruct((rhs, columns), F32),
        compiler_params=params(12),
        cost_estimate=pl.CostEstimate(
            flops=2 * rhs * near_blocks.size,
            bytes_accessed=near_blocks.size * 2 + 7 * rhs * columns * 2,
            transcendentals=0,
        ),
        name="near",
    )(near_src.T, near_count, *[in_hbm(p) for p in pieces], in_hbm(near_blocks))


def far_kernel(
    halves, ours, theirs, pick, near, m2l_hbm, p2m_hbm, basis_hbm, image_ref, sums_ref, basis, *scratch
):
    recv, lhs, loc, both, m2l, p2m, sems = scratch
    moves = [
        pltpu.make_async_copy(source, target, sems.at[i])
        for i, (source, target) in enumerate(
            ((m2l_hbm, m2l), (p2m_hbm, p2m), (basis_hbm, basis))
        )
    ]
    for move in moves:
        move.start()
    leaves, panels, terms = p2m.shape
    classes = m2l.shape[0]
    blocks, rhs, columns = basis.shape
    part = rhs // halves
    group = 8
    rows = ours.shape[0]
    recv[:rows], recv[rows:] = ours[...], theirs[...]
    for h in range(halves):
        for j in range(0, part, group):
            got = dot(pick[h], recv[:, j * terms : (j + group) * terms]).astype(BF16)
            for t in range(group):
                base = (h * part + j + t) * leaves
                for c in range(classes):
                    lhs[base : base + leaves, c * terms : (c + 1) * terms] = got[
                        c * leaves : (c + 1) * leaves, t * terms : (t + 1) * terms
                    ]
    moves[0].wait()
    weights = m2l[...].reshape(classes * terms, terms)
    tall = 256
    for i in range(rhs * leaves // tall):
        got = dot(lhs[i * tall : (i + 1) * tall, :], weights)
        loc[i * tall // leaves : (i + 1) * tall // leaves] = got.reshape(
            tall // leaves, leaves, terms
        )
    moves[1].wait()
    for g in range(leaves):
        cols = slice(g * panels, (g + 1) * panels)
        image = near[:, cols] + dot_nt(loc[:, g, :].astype(BF16), p2m[g])
        image_ref[:, cols] = image
        both[:rhs, cols], both[rhs:, cols] = split_parts(image)
    moves[2].wait()
    inner = dot_nt(both[...], basis[...].reshape(blocks * rhs, columns))
    pack(inner[:rhs] + inner[rhs:], sums_ref)


def pack_sizes(rhs, wide, peers):
    rows = rhs * wide // 128 // peers
    return rows, -(-rows // 8) * 8


def pack(products, out_ref):
    peers, piece, lanes = out_ref.shape
    rhs, wide = products.shape
    rows, _ = pack_sizes(rhs, wide, peers)
    if rows < piece:
        out_ref[...] = jnp.zeros_like(out_ref)
    tall = jnp.concatenate(
        [products[:, i * lanes : (i + 1) * lanes] for i in range(wide // lanes)], axis=0
    )
    for p in range(peers):
        out_ref[p, :rows, :] = tall[p * rows : (p + 1) * rows]


def unpack(in_ref, rhs, wide):
    peers, _, lanes = in_ref.shape
    rows, _ = pack_sizes(rhs, wide, peers)
    tall = jnp.concatenate([in_ref[p, :rows, :] for p in range(peers)], axis=0)
    return jnp.concatenate(
        [tall[i * rhs : (i + 1) * rhs] for i in range(wide // lanes)], axis=1
    )


def far_field(ours, theirs, pick, m2l, p2m, near, basis, halves, peers):
    leaves, panels, terms = p2m.shape
    classes = m2l.shape[0]
    blocks, rhs, columns = basis.shape
    _, piece = pack_sizes(rhs, blocks * rhs, peers)
    args = (ours, theirs, pick, near)
    anywhere = pl.BlockSpec(memory_space=pl.ANY)
    return pl.pallas_call(
        functools.partial(far_kernel, halves),
        grid=(1,),
        out_shape=(
            jax.ShapeDtypeStruct((rhs, columns), F32),
            jax.ShapeDtypeStruct((peers, piece, 128), F32),
            pltpu.VMEM(basis.shape, BF16),
        ),
        in_specs=[whole(a.shape) for a in args] + [anywhere] * 3,
        out_specs=(
            whole((rhs, columns)),
            whole((peers, piece, 128)),
            pl.BlockSpec(memory_space=pltpu.VMEM),
        ),
        scratch_shapes=[
            pltpu.VMEM((2 * ours.shape[0], ours.shape[1]), BF16),
            pltpu.VMEM((rhs * leaves, classes * terms), BF16),
            pltpu.VMEM((rhs, leaves, terms), F32),
            pltpu.VMEM((2 * rhs, columns), BF16),
            pltpu.VMEM(m2l.shape, BF16),
            pltpu.VMEM(p2m.shape, BF16),
            pltpu.SemaphoreType.DMA((3,)),
        ],
        compiler_params=params(24),
        name="far",
    )(*args, in_hbm(m2l), in_hbm(p2m), in_hbm(basis))


def exchange(pieces, axes=AXES):
    return lax.all_to_all(pieces, axes, split_axis=0, concat_axis=0, tiled=True)


def add_kernel(in_ref, out_ref):
    total = jnp.sum(in_ref[...], axis=0)
    out_ref[...] = jnp.broadcast_to(total[None], out_ref.shape)


def added(pieces, copies):
    shape = (copies, *pieces.shape[1:])
    return pl.pallas_call(
        add_kernel,
        grid=(1,),
        out_shape=jax.ShapeDtypeStruct(shape, F32),
        in_specs=[whole(pieces.shape)],
        out_specs=whole(shape),
        compiler_params=params(4),
        name="add",
    )(pieces)


def resid_kernel(total_rows, sums, image, basis, resid_ref, gram_ref, proj_ref):
    blocks, rhs, columns = basis.shape
    wide = blocks * rhs
    proj = unpack(sums, rhs, wide) * (1.0 / total_rows)
    proj_ref[...] = proj.T
    coef = jnp.concatenate(split_parts(proj), axis=0)
    step = 1024
    for i in range(columns // step):
        cols = slice(i * step, (i + 1) * step)
        by_basis = dot(coef, basis[:, :, cols].reshape(wide, step))
        resid = image[:, cols] - (by_basis[:rhs] + by_basis[rhs:])
        resid_ref[:rhs, cols], resid_ref[rhs:, cols] = split_parts(resid)
    both = resid_ref[...]
    square = dot_nt(both, both)
    gram = square[:rhs, :rhs] + square[:rhs, rhs:] + square[rhs:, :rhs] + square[rhs:, rhs:]
    half = rhs // 2
    folded = jnp.concatenate([gram[:half], gram[half:]], axis=1) * (1.0 / total_rows)
    gram_ref[...] = folded


def residual(sums, basis, image, total_rows):
    blocks, rhs, columns = basis.shape
    args = (sums, image, basis)
    shapes = (
        jax.ShapeDtypeStruct((2 * rhs, columns), BF16),
        jax.ShapeDtypeStruct((rhs // 2, 2 * rhs), F32),
        jax.ShapeDtypeStruct((blocks * rhs, rhs), F32),
    )
    return pl.pallas_call(
        functools.partial(resid_kernel, total_rows),
        grid=(1,),
        out_shape=shapes,
        in_specs=[whole(a.shape) for a in args],
        out_specs=tuple(whole(s.shape) for s in shapes),
        compiler_params=params(24),
        name="residual",
    )(*args)


def factored(gram, done):
    size = gram.shape[0]
    rows = lax.broadcasted_iota(jnp.int32, (size, size), 0)
    cols = lax.broadcasted_iota(jnp.int32, (size, size), 1)
    both = jnp.concatenate([gram, (rows == cols).astype(F32)], axis=1)
    tiles = [both[8 * i : 8 * i + 8] for i in range(size // 8)]
    for j in range(0, size, 2):
        t, o = divmod(j, 8)
        first, second = tiles[t][o : o + 1], tiles[t][o + 1 : o + 2]
        a, b, c = first[:, j : j + 1], first[:, j + 1 : j + 2], second[:, j + 1 : j + 2]
        scale = 1.0 / (a * c - b * b)
        upper = (c * first - b * second) * scale
        lower = (a * second - b * first) * scale
        for i in range(t, size // 8):
            change = tiles[i][:, j : j + 1] * upper + tiles[i][:, j + 1 : j + 2] * lower
            tiles[i] = tiles[i] - change
        ratio = b / a
        done[j : j + 1, :] = first / jnp.sqrt(a)
        done[j + 1 : j + 2, :] = (second - ratio * first) / jnp.sqrt(c - ratio * b)
    both = done[...]
    return jnp.where(cols >= rows, both[:, :size], 0.0).T, both[:, size:]


def tail_kernel(grams, resid, next_ref, factor_ref, done):
    rhs = factor_ref.shape[0]
    columns = resid.shape[1]
    folded = jnp.sum(grams[...], axis=0)
    gram = jnp.concatenate([folded[:, :rhs], folded[:, rhs:]], axis=0)
    lower, inverse = factored(gram, done)
    factor_ref[...] = lower
    coef = jnp.concatenate(split_parts(inverse), axis=0)
    step = 1024
    for i in range(columns // step):
        cols = slice(i * step, (i + 1) * step)
        first = dot(coef, resid[:rhs, cols])
        second = dot(coef[:rhs], resid[rhs:, cols])
        next_ref[:, cols] = (first[:rhs] + first[rhs:] + second).astype(BF16)


def tail(grams, resid):
    rhs, columns = resid.shape[0] // 2, resid.shape[1]
    args = (grams, resid)
    shapes = (
        jax.ShapeDtypeStruct((rhs, columns), BF16),
        jax.ShapeDtypeStruct((rhs, rhs), F32),
    )
    return pl.pallas_call(
        tail_kernel,
        grid=(1,),
        out_shape=shapes,
        in_specs=[whole(a.shape) for a in args],
        out_specs=tuple(whole(s.shape) for s in shapes),
        scratch_shapes=[pltpu.VMEM((rhs, 2 * rhs), F32)],
        compiler_params=params(6),
        name="tail",
    )(*args)


def shards(
    basis, near_blocks, near_src, near_count, p2m, m2l, send_list, send_count, far_src, far_class
):
    blocks, rhs, columns = basis.shape
    leaves = near_src.shape[0]
    classes, terms, _ = m2l.shape
    devices, near_devices = lax.axis_size("gx"), lax.axis_size("lo")
    peers = 2 * devices * near_devices
    slots = send_list.shape[2]
    total_rows = columns * peers
    halves = 2
    side = lax.axis_index("hi")
    same_side = ("gx", "lo")

    payload, own = all_multipoles(basis, p2m, send_list[0].T, send_count, halves)
    flip = [(0, 1), (1, 0)]
    given = lax.ppermute(payload, "hi", flip)
    up = [(i, i + 1) for i in range(devices - 1)]
    down = [(j, i) for i, j in up]
    pieces = [lax.ppermute(own, "gx", way) for way in (up, down)]

    sender = far_src // slots
    place = sender // (2 * near_devices) * near_devices + sender % near_devices
    place = place + jnp.where(sender // near_devices % 2 == side, 0, peers // 2)
    place = place * slots + far_src % slots
    class_hot = (far_class[:, None, :] == jnp.arange(classes)[None, :, None]).astype(BF16)
    rows = jnp.arange(peers * slots * halves)[None, None, None, :]
    wanted = place[None, :, :, None] * halves + jnp.arange(halves)[:, None, None, None]
    source_hot = (wanted == rows).astype(BF16)
    pick = jnp.einsum("gce,hgef->hcgf", class_hot, source_hot, preferred_element_type=F32)
    pick = pick.astype(BF16).reshape(halves, classes * leaves, -1)

    given, pick = lax.optimization_barrier((given, pick))
    received = []
    for multipoles in (payload, given):
        chosen = chosen_multipoles(side[None], multipoles, leaves, slots, halves, rhs, peers // 2)
        if multipoles is given:
            chosen, *pieces = lax.optimization_barrier((chosen, *pieces))
        got = exchange(chosen.reshape(peers // 2, slots * halves, -1), same_side)
        received.append(got.reshape(chosen.shape))

    before, after = pieces
    near = near_field(near_src, near_count, (before, own, after), near_blocks)
    image, sums, basis_near = far_field(*received, pick, m2l, p2m, near, basis, halves, peers)
    sums = exchange(added(exchange(sums), peers))
    resid, gram, projections = residual(sums, basis_near, image, total_rows)
    pair = jnp.stack([gram, lax.ppermute(gram, "hi", flip)])
    grams = exchange(added(pair, peers // 2), same_side)
    next_block, factor = tail(grams, resid)
    return (next_block, projections.reshape(blocks, rhs, rhs), factor)


def solution(mesh):
    devices, segments = mesh.shape["gx"], mesh.shape["bulk"]
    mesh = jax.sharding.Mesh(mesh.devices.reshape(devices, 2, segments // 2), AXES)
    return jax.shard_map(
        shards,
        mesh=mesh,
        in_specs=(
            P(None, None, AXES),
            P(AXES, None, None, None),
            P(AXES, None),
            P(AXES),
            P(AXES, None, None),
            P(),
            P(AXES, None, None),
            P(AXES, None),
            P(AXES, None),
            P(AXES, None),
        ),
        out_specs=(P(None, AXES), P(), P()),
        check_vma=False,
    )
```

```python
import functools

import jax
import jax.numpy as jnp
from jax import lax
from jax.experimental import pallas as pl
from jax.experimental.pallas import tpu as pltpu
from jax.sharding import PartitionSpec as P

F32 = jnp.float32
BF16 = jnp.bfloat16
AXES = ("gx", "hi", "lo")
MIB = 1024 * 1024


def dot(a, b, dims=((1,), (0,)), precision=None):
    return lax.dot_general(a, b, (dims, ((), ())), precision=precision, preferred_element_type=F32)


def dot_nt(a, b, precision=None):
    return dot(a, b, ((1,), (1,)), precision)


def split_parts(values):
    upper = values.astype(BF16)
    lower = (values - upper.astype(F32)).astype(BF16)
    return (upper, lower)


def params(mib):
    return pltpu.CompilerParams(vmem_limit_bytes=mib * MIB)


def in_hbm(array):
    return pltpu.with_memory_space_constraint(array, pltpu.HBM)


def whole(shape):
    return pl.BlockSpec(shape, lambda *_: (0,) * len(shape))


def send_kernel(halves, x, p2m, listed, counts, out, own, scratch, lists):
    leaves, panels, terms = p2m.shape
    rhs = x.shape[1]
    part = rhs // halves
    slots, peers = listed.shape
    own[...] = x[0]
    for g in range(leaves):
        mult = dot(x[0, :, g * panels : (g + 1) * panels], p2m[g])
        for h in range(halves):
            scratch[:, g * halves + h, :] = mult[h * part : (h + 1) * part]
    tall = leaves * halves
    for j in range(part):
        out[j * tall : (j + 1) * tall, :] = scratch[j].astype(BF16)
    lists[...] = jnp.zeros_like(lists)
    lists[:slots, :peers] = listed[...].astype(F32)
    lists[slots : slots + 1, :peers] = counts[...].astype(F32)
    out[part * tall :, :] = lists[...].astype(BF16)


def choose_kernel(halves, slots, leaves, near_devices, side, given, out):
    tall, terms = leaves * halves, given.shape[1]
    rows, part = out.shape[0], out.shape[1] // terms
    each = slots * halves
    receiver = lax.broadcasted_iota(jnp.int32, (rows, terms), 0) // each
    far_part, near_part = receiver // near_devices, receiver % near_devices
    device = far_part * (2 * near_devices) + side[0] * near_devices + near_part
    hot = (device == lax.broadcasted_iota(jnp.int32, (rows, terms), 1)).astype(F32).astype(BF16)
    spread = dot_nt(hot, given[part * tall :, :])
    row = lax.broadcasted_iota(jnp.int32, spread.shape, 0)
    lane = lax.broadcasted_iota(jnp.int32, spread.shape, 1)
    slot = row // halves % slots
    leaf = jnp.sum(jnp.where(lane == slot, spread, 0.0), axis=1, keepdims=True)
    live = jnp.sum(jnp.where(lane == slots, spread, 0.0), axis=1, keepdims=True)
    row = lax.broadcasted_iota(jnp.int32, (rows, tall), 0)
    lane = lax.broadcasted_iota(jnp.int32, (rows, tall), 1).astype(F32)
    held = (row // halves % slots).astype(F32) < live
    wanted = leaf * halves + (row % halves).astype(F32)
    chosen = ((lane == wanted) & held).astype(F32).astype(BF16)
    for j in range(part // 2):
        pair = [given[i * tall : (i + 1) * tall, :] for i in (2 * j, 2 * j + 1)]
        got = dot(chosen, jnp.concatenate(pair, axis=1))
        out[:, j * 2 * terms : (j + 1) * 2 * terms] = got.astype(BF16)


def all_multipoles(basis, p2m, listed, counts, halves):
    blocks, rhs, columns = basis.shape
    leaves, panels, terms = p2m.shape
    shapes = (
        jax.ShapeDtypeStruct((rhs * leaves + 16, terms), BF16),
        jax.ShapeDtypeStruct((rhs, columns), BF16),
    )
    return pl.pallas_call(
        functools.partial(send_kernel, halves),
        grid=(1,),
        out_shape=shapes,
        in_specs=[
            pl.BlockSpec((1, rhs, columns), lambda i: (blocks - 1, 0, 0)),
            whole(p2m.shape),
            whole(listed.shape),
            whole(counts.shape),
        ],
        out_specs=tuple(whole(s.shape) for s in shapes),
        scratch_shapes=[
            pltpu.VMEM((rhs // halves, leaves * halves, terms), F32),
            pltpu.VMEM((16, terms), F32),
        ],
        compiler_params=params(8),
        name="send",
    )(in_hbm(basis), in_hbm(p2m), in_hbm(listed), in_hbm(counts))


def chosen_multipoles(side, given, leaves, slots, halves, rhs, receivers):
    terms = given.shape[1]
    shape = (receivers * slots * halves, rhs // halves * terms)
    return pl.pallas_call(
        functools.partial(choose_kernel, halves, slots, leaves, lax.axis_size("lo")),
        grid=(1,),
        out_shape=jax.ShapeDtypeStruct(shape, BF16),
        in_specs=[pl.BlockSpec(memory_space=pltpu.SMEM), whole(given.shape)],
        out_specs=whole(shape),
        compiler_params=params(8),
        cost_estimate=pl.CostEstimate(flops=7 * 10**10, bytes_accessed=0, transcendentals=0),
        name="choose",
    )(side, given)


def near_kernel(src_ref, count_ref, *refs):
    pieces, (blocks_ref, out_ref, wide) = refs[:3], refs[3:]
    columns = pieces[0].shape[1]
    slots, panels = blocks_ref.shape[1], blocks_ref.shape[2]
    g = pl.program_id(0)

    @pl.when(g == 0)
    def _():
        for i, piece in enumerate(pieces):
            wide[:, i * columns : (i + 1) * columns] = piece[...]

    for i in range(blocks_ref.shape[0]):
        leaf = g * blocks_ref.shape[0] + i
        here = pl.ds(pl.multiple_of(columns + leaf * panels, panels), panels)
        total = [wide[:, here].astype(F32), 0.0]
        for k in range(slots):
            place = pl.multiple_of(src_ref[k, leaf] * panels, panels)
            source = wide[:, pl.ds(place, panels)]
            source = jnp.where(k < count_ref[leaf], source, jnp.zeros_like(source))
            total[k % 2] += dot_nt(source, blocks_ref[i, k])
        out_ref[:, i * panels : (i + 1) * panels] = total[0] + total[1]


def near_field(near_src, near_count, pieces, near_blocks):
    leaves, slots, panels, _ = near_blocks.shape
    rhs, columns = pieces[0].shape
    grid_spec = pltpu.PrefetchScalarGridSpec(
        num_scalar_prefetch=2,
        grid=(leaves // 2,),
        in_specs=[
            *[whole((rhs, columns))] * 3,
            pl.BlockSpec((2, slots, panels, panels), lambda g, *_: (g, 0, 0, 0)),
        ],
        out_specs=pl.BlockSpec((rhs, 2 * panels), lambda g, *_: (0, g)),
        scratch_shapes=[pltpu.VMEM((rhs, 3 * columns), BF16)],
    )
    return pl.pallas_call(
        near_kernel,
        grid_spec=grid_spec,
        out_shape=jax.ShapeDtypeStruct((rhs, columns), F32),
        compiler_params=params(12),
        cost_estimate=pl.CostEstimate(
            flops=2 * rhs * near_blocks.size,
            bytes_accessed=near_blocks.size * 2 + 7 * rhs * columns * 2,
            transcendentals=0,
        ),
        name="near",
    )(near_src.T, near_count, *[in_hbm(p) for p in pieces], in_hbm(near_blocks))


def far_kernel(
    halves, ours, theirs, pick, near, m2l_hbm, p2m_hbm, basis_hbm, image_ref, sums_ref, basis, *scratch
):
    recv, lhs, loc, both, m2l, p2m, sems = scratch
    moves = [
        pltpu.make_async_copy(source, target, sems.at[i])
        for i, (source, target) in enumerate(
            ((m2l_hbm, m2l), (p2m_hbm, p2m), (basis_hbm, basis))
        )
    ]
    moves[0].start()
    moves[1].start()
    leaves, panels, terms = p2m.shape
    classes = m2l.shape[0]
    blocks, rhs, columns = basis.shape
    part = rhs // halves
    group = 8
    rows = ours.shape[0]
    recv[:rows], recv[rows:] = ours[...], theirs[...]
    for h in range(halves):
        if h == halves - 1:
            moves[2].start()
        for j in range(0, part, group):
            got = dot(pick[h], recv[:, j * terms : (j + group) * terms]).astype(BF16)
            for t in range(group):
                base = (h * part + j + t) * leaves
                for c in range(classes):
                    lhs[base : base + leaves, c * terms : (c + 1) * terms] = got[
                        c * leaves : (c + 1) * leaves, t * terms : (t + 1) * terms
                    ]
    moves[0].wait()
    weights = m2l[...].reshape(classes * terms, terms)
    tall = 256
    for i in range(rhs * leaves // tall):
        got = dot(lhs[i * tall : (i + 1) * tall, :], weights)
        loc[i * tall // leaves : (i + 1) * tall // leaves] = got.reshape(
            tall // leaves, leaves, terms
        )
    moves[1].wait()
    for g in range(leaves):
        cols = slice(g * panels, (g + 1) * panels)
        image = near[:, cols] + dot_nt(loc[:, g, :].astype(BF16), p2m[g])
        image_ref[:, cols] = image
        both[:rhs, cols], both[rhs:, cols] = split_parts(image)
    moves[2].wait()
    inner = dot_nt(both[...], basis[...].reshape(blocks * rhs, columns))
    pack(inner[:rhs] + inner[rhs:], sums_ref)


def pack_sizes(rhs, wide, peers):
    rows = rhs * wide // 128 // peers
    return rows, -(-rows // 8) * 8


def pack(products, out_ref):
    peers, piece, lanes = out_ref.shape
    rhs, wide = products.shape
    rows, _ = pack_sizes(rhs, wide, peers)
    if rows < piece:
        out_ref[...] = jnp.zeros_like(out_ref)
    tall = jnp.concatenate(
        [products[:, i * lanes : (i + 1) * lanes] for i in range(wide // lanes)], axis=0
    )
    for p in range(peers):
        out_ref[p, :rows, :] = tall[p * rows : (p + 1) * rows]


def unpack(in_ref, rhs, wide):
    peers, _, lanes = in_ref.shape
    rows, _ = pack_sizes(rhs, wide, peers)
    tall = jnp.concatenate([in_ref[p, :rows, :] for p in range(peers)], axis=0)
    return jnp.concatenate(
        [tall[i * rhs : (i + 1) * rhs] for i in range(wide // lanes)], axis=1
    )


def far_field(ours, theirs, pick, m2l, p2m, near, basis, halves, peers):
    leaves, panels, terms = p2m.shape
    classes = m2l.shape[0]
    blocks, rhs, columns = basis.shape
    _, piece = pack_sizes(rhs, blocks * rhs, peers)
    args = (ours, theirs, pick, near)
    anywhere = pl.BlockSpec(memory_space=pl.ANY)
    return pl.pallas_call(
        functools.partial(far_kernel, halves),
        grid=(1,),
        out_shape=(
            jax.ShapeDtypeStruct((rhs, columns), F32),
            jax.ShapeDtypeStruct((peers, piece, 128), F32),
            pltpu.VMEM(basis.shape, BF16),
        ),
        in_specs=[whole(a.shape) for a in args] + [anywhere] * 3,
        out_specs=(
            whole((rhs, columns)),
            whole((peers, piece, 128)),
            pl.BlockSpec(memory_space=pltpu.VMEM),
        ),
        scratch_shapes=[
            pltpu.VMEM((2 * ours.shape[0], ours.shape[1]), BF16),
            pltpu.VMEM((rhs * leaves, classes * terms), BF16),
            pltpu.VMEM((rhs, leaves, terms), F32),
            pltpu.VMEM((2 * rhs, columns), BF16),
            pltpu.VMEM(m2l.shape, BF16),
            pltpu.VMEM(p2m.shape, BF16),
            pltpu.SemaphoreType.DMA((3,)),
        ],
        compiler_params=params(24),
        name="far",
    )(*args, in_hbm(m2l), in_hbm(p2m), in_hbm(basis))


def exchange(pieces, axes=AXES):
    return lax.all_to_all(pieces, axes, split_axis=0, concat_axis=0, tiled=True)


def add_kernel(in_ref, out_ref):
    total = jnp.sum(in_ref[...], axis=0)
    out_ref[...] = jnp.broadcast_to(total[None], out_ref.shape)


def added(pieces, copies):
    shape = (copies, *pieces.shape[1:])
    return pl.pallas_call(
        add_kernel,
        grid=(1,),
        out_shape=jax.ShapeDtypeStruct(shape, F32),
        in_specs=[whole(pieces.shape)],
        out_specs=whole(shape),
        compiler_params=params(4),
        name="add",
    )(pieces)


def resid_kernel(total_rows, sums, image, basis, resid_ref, gram_ref, proj_ref):
    blocks, rhs, columns = basis.shape
    wide = blocks * rhs
    proj = unpack(sums, rhs, wide) * (1.0 / total_rows)
    proj_ref[...] = proj.T
    coef = jnp.concatenate(split_parts(proj), axis=0)
    step = 1024
    for i in range(columns // step):
        cols = slice(i * step, (i + 1) * step)
        by_basis = dot(coef, basis[:, :, cols].reshape(wide, step))
        resid = image[:, cols] - (by_basis[:rhs] + by_basis[rhs:])
        resid_ref[:rhs, cols], resid_ref[rhs:, cols] = split_parts(resid)
    both = resid_ref[...]
    square = dot_nt(both, both)
    gram = square[:rhs, :rhs] + square[:rhs, rhs:] + square[rhs:, :rhs] + square[rhs:, rhs:]
    half = rhs // 2
    folded = jnp.concatenate([gram[:half], gram[half:]], axis=1) * (1.0 / total_rows)
    gram_ref[...] = folded


def residual(sums, basis, image, total_rows):
    blocks, rhs, columns = basis.shape
    args = (sums, image, basis)
    shapes = (
        jax.ShapeDtypeStruct((2 * rhs, columns), BF16),
        jax.ShapeDtypeStruct((rhs // 2, 2 * rhs), F32),
        jax.ShapeDtypeStruct((blocks * rhs, rhs), F32),
    )
    return pl.pallas_call(
        functools.partial(resid_kernel, total_rows),
        grid=(1,),
        out_shape=shapes,
        in_specs=[whole(a.shape) for a in args],
        out_specs=tuple(whole(s.shape) for s in shapes),
        compiler_params=params(24),
        name="residual",
    )(*args)


def factored(gram, done):
    size = gram.shape[0]
    rows = lax.broadcasted_iota(jnp.int32, (size, size), 0)
    cols = lax.broadcasted_iota(jnp.int32, (size, size), 1)
    both = jnp.concatenate([gram, (rows == cols).astype(F32)], axis=1)
    tiles = [both[8 * i : 8 * i + 8] for i in range(size // 8)]
    for j in range(0, size, 2):
        t, o = divmod(j, 8)
        first, second = tiles[t][o : o + 1], tiles[t][o + 1 : o + 2]
        a, b, c = first[:, j : j + 1], first[:, j + 1 : j + 2], second[:, j + 1 : j + 2]
        scale = 1.0 / (a * c - b * b)
        upper = (c * first - b * second) * scale
        lower = (a * second - b * first) * scale
        for i in range(t, size // 8):
            change = tiles[i][:, j : j + 1] * upper + tiles[i][:, j + 1 : j + 2] * lower
            tiles[i] = tiles[i] - change
        ratio = b / a
        done[j : j + 1, :] = first / jnp.sqrt(a)
        done[j + 1 : j + 2, :] = (second - ratio * first) / jnp.sqrt(c - ratio * b)
    both = done[...]
    return jnp.where(cols >= rows, both[:, :size], 0.0).T, both[:, size:]


def tail_kernel(grams, resid, next_ref, factor_ref, done):
    rhs = factor_ref.shape[0]
    columns = resid.shape[1]
    folded = jnp.sum(grams[...], axis=0)
    gram = jnp.concatenate([folded[:, :rhs], folded[:, rhs:]], axis=0)
    lower, inverse = factored(gram, done)
    factor_ref[...] = lower
    coef = jnp.concatenate(split_parts(inverse), axis=0)
    step = 1024
    for i in range(columns // step):
        cols = slice(i * step, (i + 1) * step)
        first = dot(coef, resid[:rhs, cols])
        second = dot(coef[:rhs], resid[rhs:, cols])
        next_ref[:, cols] = (first[:rhs] + first[rhs:] + second).astype(BF16)


def tail(grams, resid):
    rhs, columns = resid.shape[0] // 2, resid.shape[1]
    args = (grams, resid)
    shapes = (
        jax.ShapeDtypeStruct((rhs, columns), BF16),
        jax.ShapeDtypeStruct((rhs, rhs), F32),
    )
    return pl.pallas_call(
        tail_kernel,
        grid=(1,),
        out_shape=shapes,
        in_specs=[whole(a.shape) for a in args],
        out_specs=tuple(whole(s.shape) for s in shapes),
        scratch_shapes=[pltpu.VMEM((rhs, 2 * rhs), F32)],
        compiler_params=params(6),
        name="tail",
    )(*args)


def shards(
    basis, near_blocks, near_src, near_count, p2m, m2l, send_list, send_count, far_src, far_class
):
    blocks, rhs, columns = basis.shape
    leaves = near_src.shape[0]
    classes, terms, _ = m2l.shape
    devices, near_devices = lax.axis_size("gx"), lax.axis_size("lo")
    peers = 2 * devices * near_devices
    slots = send_list.shape[2]
    total_rows = columns * peers
    halves = 2
    side = lax.axis_index("hi")
    same_side = ("gx", "lo")

    payload, own = all_multipoles(basis, p2m, send_list[0].T, send_count, halves)
    flip = [(0, 1), (1, 0)]
    given = lax.ppermute(payload, "hi", flip)
    up = [(i, i + 1) for i in range(devices - 1)]
    down = [(j, i) for i, j in up]
    sender = far_src // slots
    place = sender // (2 * near_devices) * near_devices + sender % near_devices
    place = place + jnp.where(sender // near_devices % 2 == side, 0, peers // 2)
    place = place * slots + far_src % slots
    class_hot = (far_class[:, None, :] == jnp.arange(classes)[None, :, None]).astype(BF16)
    rows = jnp.arange(peers * slots * halves)[None, None, None, :]
    wanted = place[None, :, :, None] * halves + jnp.arange(halves)[:, None, None, None]
    source_hot = (wanted == rows).astype(BF16)
    pick = jnp.einsum("gce,hgef->hcgf", class_hot, source_hot, preferred_element_type=F32)
    pick = pick.astype(BF16).reshape(halves, classes * leaves, -1)

    given, pick = lax.optimization_barrier((given, pick))

    def choose(multipoles):
        return chosen_multipoles(side[None], multipoles, leaves, slots, halves, rhs, peers // 2)

    def give(chosen):
        got = exchange(chosen.reshape(peers // 2, slots * halves, -1), same_side)
        return got.reshape(chosen.shape)

    chosen, own = lax.optimization_barrier((choose(payload), own))
    ours = give(chosen)
    before, after = lax.ppermute(own, "gx", up), lax.ppermute(own, "gx", down)
    chosen, before, after = lax.optimization_barrier((choose(given), before, after))
    theirs = give(chosen)

    near = near_field(near_src, near_count, (before, own, after), near_blocks)
    image, sums, basis_near = far_field(ours, theirs, pick, m2l, p2m, near, basis, halves, peers)
    sums = exchange(added(exchange(sums), peers))
    resid, gram, projections = residual(sums, basis_near, image, total_rows)
    pair = jnp.stack([gram, lax.ppermute(gram, "hi", flip)])
    grams = exchange(added(pair, peers // 2), same_side)
    next_block, factor = tail(grams, resid)
    return (next_block, projections.reshape(blocks, rhs, rhs), factor)


def solution(mesh):
    devices, segments = mesh.shape["gx"], mesh.shape["bulk"]
    mesh = jax.sharding.Mesh(mesh.devices.reshape(devices, 2, segments // 2), AXES)
    return jax.shard_map(
        shards,
        mesh=mesh,
        in_specs=(
            P(None, None, AXES),
            P(AXES, None, None, None),
            P(AXES, None),
            P(AXES),
            P(AXES, None, None),
            P(),
            P(AXES, None, None),
            P(AXES, None),
            P(AXES, None),
            P(AXES, None),
        ),
        out_specs=(P(None, AXES), P(), P()),
        check_vma=False,
    )
```

```python
import functools

import jax
import jax.numpy as jnp
from jax import lax
from jax.experimental import pallas as pl
from jax.experimental.pallas import tpu as pltpu
from jax.sharding import PartitionSpec as P

F32 = jnp.float32
BF16 = jnp.bfloat16
AXES = ("gx", "hi", "lo")
MIB = 1024 * 1024


def dot(a, b, dims=((1,), (0,)), precision=None):
    return lax.dot_general(a, b, (dims, ((), ())), precision=precision, preferred_element_type=F32)


def dot_nt(a, b, precision=None):
    return dot(a, b, ((1,), (1,)), precision)


def split_parts(values):
    upper = values.astype(BF16)
    lower = (values - upper.astype(F32)).astype(BF16)
    return (upper, lower)


def params(mib):
    return pltpu.CompilerParams(vmem_limit_bytes=mib * MIB)


def in_hbm(array):
    return pltpu.with_memory_space_constraint(array, pltpu.HBM)


def whole(shape):
    return pl.BlockSpec(shape, lambda *_: (0,) * len(shape))


def send_kernel(halves, x, p2m, listed, counts, out, own, scratch, lists):
    leaves, panels, terms = p2m.shape
    rhs = x.shape[1]
    part = rhs // halves
    slots, peers = listed.shape
    own[...] = x[0]
    for g in range(leaves):
        mult = dot(x[0, :, g * panels : (g + 1) * panels], p2m[g])
        for h in range(halves):
            scratch[:, g * halves + h, :] = mult[h * part : (h + 1) * part]
    tall = leaves * halves
    for j in range(part):
        out[j * tall : (j + 1) * tall, :] = scratch[j].astype(BF16)
    lists[...] = jnp.zeros_like(lists)
    lists[:slots, :peers] = listed[...].astype(F32)
    lists[slots : slots + 1, :peers] = counts[...].astype(F32)
    out[part * tall :, :] = lists[...].astype(BF16)


def choose_kernel(halves, slots, leaves, near_devices, side, given, out):
    tall, terms = leaves * halves, given.shape[1]
    rows, part = out.shape[0], out.shape[1] // terms
    each = slots * halves
    receiver = lax.broadcasted_iota(jnp.int32, (rows, terms), 0) // each
    far_part, near_part = receiver // near_devices, receiver % near_devices
    device = far_part * (2 * near_devices) + side[0] * near_devices + near_part
    hot = (device == lax.broadcasted_iota(jnp.int32, (rows, terms), 1)).astype(F32).astype(BF16)
    spread = dot_nt(hot, given[part * tall :, :])
    row = lax.broadcasted_iota(jnp.int32, spread.shape, 0)
    lane = lax.broadcasted_iota(jnp.int32, spread.shape, 1)
    slot = row // halves % slots
    leaf = jnp.sum(jnp.where(lane == slot, spread, 0.0), axis=1, keepdims=True)
    live = jnp.sum(jnp.where(lane == slots, spread, 0.0), axis=1, keepdims=True)
    row = lax.broadcasted_iota(jnp.int32, (rows, tall), 0)
    lane = lax.broadcasted_iota(jnp.int32, (rows, tall), 1).astype(F32)
    held = (row // halves % slots).astype(F32) < live
    wanted = leaf * halves + (row % halves).astype(F32)
    chosen = ((lane == wanted) & held).astype(F32).astype(BF16)
    for j in range(part // 2):
        pair = [given[i * tall : (i + 1) * tall, :] for i in (2 * j, 2 * j + 1)]
        got = dot(chosen, jnp.concatenate(pair, axis=1))
        out[:, j * 2 * terms : (j + 1) * 2 * terms] = got.astype(BF16)


def all_multipoles(basis, p2m, listed, counts, halves):
    blocks, rhs, columns = basis.shape
    leaves, panels, terms = p2m.shape
    shapes = (
        jax.ShapeDtypeStruct((rhs * leaves + 16, terms), BF16),
        jax.ShapeDtypeStruct((rhs, columns), BF16),
    )
    return pl.pallas_call(
        functools.partial(send_kernel, halves),
        grid=(1,),
        out_shape=shapes,
        in_specs=[
            pl.BlockSpec((1, rhs, columns), lambda i: (blocks - 1, 0, 0)),
            whole(p2m.shape),
            whole(listed.shape),
            whole(counts.shape),
        ],
        out_specs=tuple(whole(s.shape) for s in shapes),
        scratch_shapes=[
            pltpu.VMEM((rhs // halves, leaves * halves, terms), F32),
            pltpu.VMEM((16, terms), F32),
        ],
        compiler_params=params(8),
        name="send",
    )(in_hbm(basis), in_hbm(p2m), in_hbm(listed), in_hbm(counts))


def chosen_multipoles(side, given, leaves, slots, halves, rhs, receivers, flops):
    terms = given.shape[1]
    shape = (receivers * slots * halves, rhs // halves * terms)
    return pl.pallas_call(
        functools.partial(choose_kernel, halves, slots, leaves, lax.axis_size("lo")),
        grid=(1,),
        out_shape=jax.ShapeDtypeStruct(shape, BF16),
        in_specs=[pl.BlockSpec(memory_space=pltpu.SMEM), whole(given.shape)],
        out_specs=whole(shape),
        compiler_params=params(8),
        cost_estimate=pl.CostEstimate(flops=flops, bytes_accessed=0, transcendentals=0),
        name="choose",
    )(side, given)


def near_kernel(src_ref, count_ref, *refs):
    pieces, (blocks_ref, out_ref, wide) = refs[:3], refs[3:]
    columns = pieces[0].shape[1]
    slots, panels = blocks_ref.shape[1], blocks_ref.shape[2]
    g = pl.program_id(0)

    @pl.when(g == 0)
    def _():
        for i, piece in enumerate(pieces):
            wide[:, i * columns : (i + 1) * columns] = piece[...]

    for i in range(blocks_ref.shape[0]):
        leaf = g * blocks_ref.shape[0] + i
        here = pl.ds(pl.multiple_of(columns + leaf * panels, panels), panels)
        total = [wide[:, here].astype(F32), 0.0]
        for k in range(slots):
            place = pl.multiple_of(src_ref[k, leaf] * panels, panels)
            source = wide[:, pl.ds(place, panels)]
            source = jnp.where(k < count_ref[leaf], source, jnp.zeros_like(source))
            total[k % 2] += dot_nt(source, blocks_ref[i, k])
        out_ref[:, i * panels : (i + 1) * panels] = total[0] + total[1]


def near_field(near_src, near_count, pieces, near_blocks):
    leaves, slots, panels, _ = near_blocks.shape
    rhs, columns = pieces[0].shape
    grid_spec = pltpu.PrefetchScalarGridSpec(
        num_scalar_prefetch=2,
        grid=(leaves // 2,),
        in_specs=[
            *[whole((rhs, columns))] * 3,
            pl.BlockSpec((2, slots, panels, panels), lambda g, *_: (g, 0, 0, 0)),
        ],
        out_specs=pl.BlockSpec((rhs, 2 * panels), lambda g, *_: (0, g)),
        scratch_shapes=[pltpu.VMEM((rhs, 3 * columns), BF16)],
    )
    return pl.pallas_call(
        near_kernel,
        grid_spec=grid_spec,
        out_shape=jax.ShapeDtypeStruct((rhs, columns), F32),
        compiler_params=params(12),
        cost_estimate=pl.CostEstimate(
            flops=2 * rhs * near_blocks.size,
            bytes_accessed=near_blocks.size * 2 + 7 * rhs * columns * 2,
            transcendentals=0,
        ),
        name="near",
    )(near_src.T, near_count, *[in_hbm(p) for p in pieces], in_hbm(near_blocks))


def far_kernel(
    halves, ours, theirs, pick, near, m2l_hbm, p2m_hbm, basis_hbm, image_ref, sums_ref, basis, *scratch
):
    recv, lhs, loc, both, m2l, p2m, sems = scratch
    moves = [
        pltpu.make_async_copy(source, target, sems.at[i])
        for i, (source, target) in enumerate(
            ((m2l_hbm, m2l), (p2m_hbm, p2m), (basis_hbm, basis))
        )
    ]
    for move in moves:
        move.start()
    leaves, panels, terms = p2m.shape
    classes = m2l.shape[0]
    blocks, rhs, columns = basis.shape
    part = rhs // halves
    group = 8
    rows = ours.shape[0]
    recv[:rows], recv[rows:] = ours[...], theirs[...]
    for h in range(halves):
        for j in range(0, part, group):
            got = dot(pick[h], recv[:, j * terms : (j + group) * terms]).astype(BF16)
            for t in range(group):
                base = (h * part + j + t) * leaves
                for c in range(classes):
                    lhs[base : base + leaves, c * terms : (c + 1) * terms] = got[
                        c * leaves : (c + 1) * leaves, t * terms : (t + 1) * terms
                    ]
    moves[0].wait()
    weights = m2l[...].reshape(classes * terms, terms)
    tall = 256
    for i in range(rhs * leaves // tall):
        got = dot(lhs[i * tall : (i + 1) * tall, :], weights)
        loc[i * tall // leaves : (i + 1) * tall // leaves] = got.reshape(
            tall // leaves, leaves, terms
        )
    moves[1].wait()
    for g in range(leaves):
        cols = slice(g * panels, (g + 1) * panels)
        image = near[:, cols] + dot_nt(loc[:, g, :].astype(BF16), p2m[g])
        image_ref[:, cols] = image
        both[:rhs, cols], both[rhs:, cols] = split_parts(image)
    moves[2].wait()
    inner = dot_nt(both[...], basis[...].reshape(blocks * rhs, columns))
    pack(inner[:rhs] + inner[rhs:], sums_ref)


def pack_sizes(rhs, wide, peers):
    rows = rhs * wide // 128 // peers
    return rows, -(-rows // 8) * 8


def pack(products, out_ref):
    peers, piece, lanes = out_ref.shape
    rhs, wide = products.shape
    rows, _ = pack_sizes(rhs, wide, peers)
    if rows < piece:
        out_ref[...] = jnp.zeros_like(out_ref)
    tall = jnp.concatenate(
        [products[:, i * lanes : (i + 1) * lanes] for i in range(wide // lanes)], axis=0
    )
    for p in range(peers):
        out_ref[p, :rows, :] = tall[p * rows : (p + 1) * rows]


def unpack(in_ref, rhs, wide):
    peers, _, lanes = in_ref.shape
    rows, _ = pack_sizes(rhs, wide, peers)
    tall = jnp.concatenate([in_ref[p, :rows, :] for p in range(peers)], axis=0)
    return jnp.concatenate(
        [tall[i * rhs : (i + 1) * rhs] for i in range(wide // lanes)], axis=1
    )


def far_field(ours, theirs, pick, m2l, p2m, near, basis, halves, peers):
    leaves, panels, terms = p2m.shape
    classes = m2l.shape[0]
    blocks, rhs, columns = basis.shape
    _, piece = pack_sizes(rhs, blocks * rhs, peers)
    args = (ours, theirs, pick, near)
    anywhere = pl.BlockSpec(memory_space=pl.ANY)
    return pl.pallas_call(
        functools.partial(far_kernel, halves),
        grid=(1,),
        out_shape=(
            jax.ShapeDtypeStruct((rhs, columns), F32),
            jax.ShapeDtypeStruct((peers, piece, 128), F32),
            pltpu.VMEM(basis.shape, BF16),
        ),
        in_specs=[whole(a.shape) for a in args] + [anywhere] * 3,
        out_specs=(
            whole((rhs, columns)),
            whole((peers, piece, 128)),
            pl.BlockSpec(memory_space=pltpu.VMEM),
        ),
        scratch_shapes=[
            pltpu.VMEM((2 * ours.shape[0], ours.shape[1]), BF16),
            pltpu.VMEM((rhs * leaves, classes * terms), BF16),
            pltpu.VMEM((rhs, leaves, terms), F32),
            pltpu.VMEM((2 * rhs, columns), BF16),
            pltpu.VMEM(m2l.shape, BF16),
            pltpu.VMEM(p2m.shape, BF16),
            pltpu.SemaphoreType.DMA((3,)),
        ],
        compiler_params=params(24),
        name="far",
    )(*args, in_hbm(m2l), in_hbm(p2m), in_hbm(basis))


def exchange(pieces, axes=AXES):
    return lax.all_to_all(pieces, axes, split_axis=0, concat_axis=0, tiled=True)


def add_kernel(in_ref, out_ref):
    total = jnp.sum(in_ref[...], axis=0)
    out_ref[...] = jnp.broadcast_to(total[None], out_ref.shape)


def added(pieces, copies):
    shape = (copies, *pieces.shape[1:])
    return pl.pallas_call(
        add_kernel,
        grid=(1,),
        out_shape=jax.ShapeDtypeStruct(shape, F32),
        in_specs=[whole(pieces.shape)],
        out_specs=whole(shape),
        compiler_params=params(4),
        name="add",
    )(pieces)


def resid_kernel(total_rows, sums, image, basis, resid_ref, gram_ref, proj_ref):
    blocks, rhs, columns = basis.shape
    wide = blocks * rhs
    proj = unpack(sums, rhs, wide) * (1.0 / total_rows)
    proj_ref[...] = proj.T
    coef = jnp.concatenate(split_parts(proj), axis=0)
    step = 1024
    for i in range(columns // step):
        cols = slice(i * step, (i + 1) * step)
        by_basis = dot(coef, basis[:, :, cols].reshape(wide, step))
        resid = image[:, cols] - (by_basis[:rhs] + by_basis[rhs:])
        resid_ref[:rhs, cols], resid_ref[rhs:, cols] = split_parts(resid)
    both = resid_ref[...]
    square = dot_nt(both, both)
    gram = square[:rhs, :rhs] + square[:rhs, rhs:] + square[rhs:, :rhs] + square[rhs:, rhs:]
    half = rhs // 2
    folded = jnp.concatenate([gram[:half], gram[half:]], axis=1) * (1.0 / total_rows)
    gram_ref[...] = folded


def residual(sums, basis, image, total_rows):
    blocks, rhs, columns = basis.shape
    args = (sums, image, basis)
    shapes = (
        jax.ShapeDtypeStruct((2 * rhs, columns), BF16),
        jax.ShapeDtypeStruct((rhs // 2, 2 * rhs), F32),
        jax.ShapeDtypeStruct((blocks * rhs, rhs), F32),
    )
    return pl.pallas_call(
        functools.partial(resid_kernel, total_rows),
        grid=(1,),
        out_shape=shapes,
        in_specs=[whole(a.shape) for a in args],
        out_specs=tuple(whole(s.shape) for s in shapes),
        compiler_params=params(24),
        name="residual",
    )(*args)


def factored(gram, done):
    size = gram.shape[0]
    rows = lax.broadcasted_iota(jnp.int32, (size, size), 0)
    cols = lax.broadcasted_iota(jnp.int32, (size, size), 1)
    both = jnp.concatenate([gram, (rows == cols).astype(F32)], axis=1)
    tiles = [both[8 * i : 8 * i + 8] for i in range(size // 8)]
    for j in range(0, size, 2):
        t, o = divmod(j, 8)
        first, second = tiles[t][o : o + 1], tiles[t][o + 1 : o + 2]
        a, b, c = first[:, j : j + 1], first[:, j + 1 : j + 2], second[:, j + 1 : j + 2]
        scale = 1.0 / (a * c - b * b)
        upper = (c * first - b * second) * scale
        lower = (a * second - b * first) * scale
        for i in range(t, size // 8):
            change = tiles[i][:, j : j + 1] * upper + tiles[i][:, j + 1 : j + 2] * lower
            tiles[i] = tiles[i] - change
        ratio = b / a
        done[j : j + 1, :] = first / jnp.sqrt(a)
        done[j + 1 : j + 2, :] = (second - ratio * first) / jnp.sqrt(c - ratio * b)
    both = done[...]
    return jnp.where(cols >= rows, both[:, :size], 0.0).T, both[:, size:]


def tail_kernel(grams, resid, next_ref, factor_ref, done):
    rhs = factor_ref.shape[0]
    columns = resid.shape[1]
    folded = jnp.sum(grams[...], axis=0)
    gram = jnp.concatenate([folded[:, :rhs], folded[:, rhs:]], axis=0)
    lower, inverse = factored(gram, done)
    factor_ref[...] = lower
    coef = jnp.concatenate(split_parts(inverse), axis=0)
    step = 1024
    for i in range(columns // step):
        cols = slice(i * step, (i + 1) * step)
        first = dot(coef, resid[:rhs, cols])
        second = dot(coef[:rhs], resid[rhs:, cols])
        next_ref[:, cols] = (first[:rhs] + first[rhs:] + second).astype(BF16)


def tail(grams, resid):
    rhs, columns = resid.shape[0] // 2, resid.shape[1]
    args = (grams, resid)
    shapes = (
        jax.ShapeDtypeStruct((rhs, columns), BF16),
        jax.ShapeDtypeStruct((rhs, rhs), F32),
    )
    return pl.pallas_call(
        tail_kernel,
        grid=(1,),
        out_shape=shapes,
        in_specs=[whole(a.shape) for a in args],
        out_specs=tuple(whole(s.shape) for s in shapes),
        scratch_shapes=[pltpu.VMEM((rhs, 2 * rhs), F32)],
        compiler_params=params(6),
        name="tail",
    )(*args)


def shards(
    basis, near_blocks, near_src, near_count, p2m, m2l, send_list, send_count, far_src, far_class
):
    blocks, rhs, columns = basis.shape
    leaves = near_src.shape[0]
    classes, terms, _ = m2l.shape
    devices, near_devices = lax.axis_size("gx"), lax.axis_size("lo")
    peers = 2 * devices * near_devices
    slots = send_list.shape[2]
    total_rows = columns * peers
    halves = 2
    side = lax.axis_index("hi")
    same_side = ("gx", "lo")

    payload, own = all_multipoles(basis, p2m, send_list[0].T, send_count, halves)
    flip = [(0, 1), (1, 0)]
    given = lax.ppermute(payload, "hi", flip)
    up = [(i, i + 1) for i in range(devices - 1)]
    down = [(j, i) for i, j in up]
    sender = far_src // slots
    place = sender // (2 * near_devices) * near_devices + sender % near_devices
    place = place + jnp.where(sender // near_devices % 2 == side, 0, peers // 2)
    place = place * slots + far_src % slots
    class_hot = (far_class[:, None, :] == jnp.arange(classes)[None, :, None]).astype(BF16)
    rows = jnp.arange(peers * slots * halves)[None, None, None, :]
    wanted = place[None, :, :, None] * halves + jnp.arange(halves)[:, None, None, None]
    source_hot = (wanted == rows).astype(BF16)
    pick = jnp.einsum("gce,hgef->hcgf", class_hot, source_hot, preferred_element_type=F32)
    pick = pick.astype(BF16).reshape(halves, classes * leaves, -1)

    given, pick = lax.optimization_barrier((given, pick))

    def choose(multipoles, flops):
        sizes = (leaves, slots, halves, rhs, peers // 2)
        return chosen_multipoles(side[None], multipoles, *sizes, flops)

    def give(chosen):
        got = exchange(chosen.reshape(peers // 2, slots * halves, -1), same_side)
        return got.reshape(chosen.shape)

    chosen, own = lax.optimization_barrier((choose(payload, 7 * 10**10), own))
    ours = give(chosen)
    before, after = lax.ppermute(own, "gx", up), lax.ppermute(own, "gx", down)
    chosen, before, after = lax.optimization_barrier((choose(given, 7 * 10**9), before, after))
    theirs = give(chosen)

    near = near_field(near_src, near_count, (before, own, after), near_blocks)
    image, sums, basis_near = far_field(ours, theirs, pick, m2l, p2m, near, basis, halves, peers)
    sums = exchange(added(exchange(sums), peers))
    resid, gram, projections = residual(sums, basis_near, image, total_rows)
    pair = jnp.stack([gram, lax.ppermute(gram, "hi", flip)])
    grams = exchange(added(pair, peers // 2), same_side)
    next_block, factor = tail(grams, resid)
    return (next_block, projections.reshape(blocks, rhs, rhs), factor)


def solution(mesh):
    devices, segments = mesh.shape["gx"], mesh.shape["bulk"]
    mesh = jax.sharding.Mesh(mesh.devices.reshape(devices, 2, segments // 2), AXES)
    return jax.shard_map(
        shards,
        mesh=mesh,
        in_specs=(
            P(None, None, AXES),
            P(AXES, None, None, None),
            P(AXES, None),
            P(AXES),
            P(AXES, None, None),
            P(),
            P(AXES, None, None),
            P(AXES, None),
            P(AXES, None),
            P(AXES, None),
        ),
        out_specs=(P(None, AXES), P(), P()),
        check_vma=False,
    )
```

```python
import functools

import jax
import jax.numpy as jnp
from jax import lax
from jax.experimental import pallas as pl
from jax.experimental.pallas import tpu as pltpu
from jax.sharding import PartitionSpec as P

F32 = jnp.float32
BF16 = jnp.bfloat16
AXES = ("gx", "hi", "lo")
MIB = 1024 * 1024


def dot(a, b, dims=((1,), (0,)), precision=None):
    return lax.dot_general(a, b, (dims, ((), ())), precision=precision, preferred_element_type=F32)


def dot_nt(a, b, precision=None):
    return dot(a, b, ((1,), (1,)), precision)


def split_parts(values):
    upper = values.astype(BF16)
    lower = (values - upper.astype(F32)).astype(BF16)
    return (upper, lower)


def params(mib):
    return pltpu.CompilerParams(vmem_limit_bytes=mib * MIB)


def in_hbm(array):
    return pltpu.with_memory_space_constraint(array, pltpu.HBM)


def whole(shape):
    return pl.BlockSpec(shape, lambda *_: (0,) * len(shape))


def send_kernel(halves, x, p2m, listed, counts, out, scratch, lists):
    leaves, panels, terms = p2m.shape
    rhs = x.shape[1]
    part = rhs // halves
    slots, peers = listed.shape
    for g in range(leaves):
        mult = dot(x[0, :, g * panels : (g + 1) * panels], p2m[g])
        for h in range(halves):
            scratch[:, g * halves + h, :] = mult[h * part : (h + 1) * part]
    tall = leaves * halves
    for j in range(part):
        out[j * tall : (j + 1) * tall, :] = scratch[j].astype(BF16)
    lists[...] = jnp.zeros_like(lists)
    lists[:slots, :peers] = listed[...].astype(F32)
    lists[slots : slots + 1, :peers] = counts[...].astype(F32)
    out[part * tall :, :] = lists[...].astype(BF16)


def choose_kernel(halves, slots, leaves, near_devices, side, given, out):
    tall, terms = leaves * halves, given.shape[1]
    rows, part = out.shape[0], out.shape[1] // terms
    each = slots * halves
    receiver = lax.broadcasted_iota(jnp.int32, (rows, terms), 0) // each
    far_part, near_part = receiver // near_devices, receiver % near_devices
    device = far_part * (2 * near_devices) + side[0] * near_devices + near_part
    hot = (device == lax.broadcasted_iota(jnp.int32, (rows, terms), 1)).astype(F32).astype(BF16)
    spread = dot_nt(hot, given[part * tall :, :])
    row = lax.broadcasted_iota(jnp.int32, spread.shape, 0)
    lane = lax.broadcasted_iota(jnp.int32, spread.shape, 1)
    slot = row // halves % slots
    leaf = jnp.sum(jnp.where(lane == slot, spread, 0.0), axis=1, keepdims=True)
    live = jnp.sum(jnp.where(lane == slots, spread, 0.0), axis=1, keepdims=True)
    row = lax.broadcasted_iota(jnp.int32, (rows, tall), 0)
    lane = lax.broadcasted_iota(jnp.int32, (rows, tall), 1).astype(F32)
    held = (row // halves % slots).astype(F32) < live
    wanted = leaf * halves + (row % halves).astype(F32)
    chosen = ((lane == wanted) & held).astype(F32).astype(BF16)
    for j in range(part // 2):
        pair = [given[i * tall : (i + 1) * tall, :] for i in (2 * j, 2 * j + 1)]
        got = dot(chosen, jnp.concatenate(pair, axis=1))
        out[:, j * 2 * terms : (j + 1) * 2 * terms] = got.astype(BF16)


def all_multipoles(basis, p2m, listed, counts, halves):
    blocks, rhs, columns = basis.shape
    leaves, panels, terms = p2m.shape
    shape = (rhs * leaves + 16, terms)
    return pl.pallas_call(
        functools.partial(send_kernel, halves),
        grid=(1,),
        out_shape=jax.ShapeDtypeStruct(shape, BF16),
        in_specs=[
            pl.BlockSpec((1, rhs, columns), lambda i: (blocks - 1, 0, 0)),
            whole(p2m.shape),
            whole(listed.shape),
            whole(counts.shape),
        ],
        out_specs=whole(shape),
        scratch_shapes=[
            pltpu.VMEM((rhs // halves, leaves * halves, terms), F32),
            pltpu.VMEM((16, terms), F32),
        ],
        compiler_params=params(8),
        name="send",
    )(in_hbm(basis), in_hbm(p2m), in_hbm(listed), in_hbm(counts))


def copy_kernel(x, out):
    out[...] = x[0]


def last_block(basis):
    blocks, rhs, columns = basis.shape
    return pl.pallas_call(
        copy_kernel,
        grid=(1,),
        out_shape=jax.ShapeDtypeStruct((rhs, columns), BF16),
        in_specs=[pl.BlockSpec((1, rhs, columns), lambda i: (blocks - 1, 0, 0))],
        out_specs=whole((rhs, columns)),
        compiler_params=params(8),
        cost_estimate=pl.CostEstimate(flops=7 * 10**10, bytes_accessed=0, transcendentals=0),
        name="last_block",
    )(in_hbm(basis))


def chosen_multipoles(side, given, leaves, slots, halves, rhs, receivers, flops):
    terms = given.shape[1]
    shape = (receivers * slots * halves, rhs // halves * terms)
    return pl.pallas_call(
        functools.partial(choose_kernel, halves, slots, leaves, lax.axis_size("lo")),
        grid=(1,),
        out_shape=jax.ShapeDtypeStruct(shape, BF16),
        in_specs=[pl.BlockSpec(memory_space=pltpu.SMEM), whole(given.shape)],
        out_specs=whole(shape),
        compiler_params=params(8),
        cost_estimate=pl.CostEstimate(flops=flops, bytes_accessed=0, transcendentals=0),
        name="choose",
    )(side, given)


def near_kernel(src_ref, count_ref, *refs):
    pieces, (blocks_ref, out_ref, wide) = refs[:3], refs[3:]
    columns = pieces[0].shape[1]
    slots, panels = blocks_ref.shape[1], blocks_ref.shape[2]
    g = pl.program_id(0)

    @pl.when(g == 0)
    def _():
        for i, piece in enumerate(pieces):
            wide[:, i * columns : (i + 1) * columns] = piece[...]

    for i in range(blocks_ref.shape[0]):
        leaf = g * blocks_ref.shape[0] + i
        here = pl.ds(pl.multiple_of(columns + leaf * panels, panels), panels)
        total = [wide[:, here].astype(F32), 0.0]
        for k in range(slots):
            place = pl.multiple_of(src_ref[k, leaf] * panels, panels)
            source = wide[:, pl.ds(place, panels)]
            source = jnp.where(k < count_ref[leaf], source, jnp.zeros_like(source))
            total[k % 2] += dot_nt(source, blocks_ref[i, k])
        out_ref[:, i * panels : (i + 1) * panels] = total[0] + total[1]


def near_field(near_src, near_count, pieces, near_blocks):
    leaves, slots, panels, _ = near_blocks.shape
    rhs, columns = pieces[0].shape
    grid_spec = pltpu.PrefetchScalarGridSpec(
        num_scalar_prefetch=2,
        grid=(leaves // 2,),
        in_specs=[
            *[whole((rhs, columns))] * 3,
            pl.BlockSpec((2, slots, panels, panels), lambda g, *_: (g, 0, 0, 0)),
        ],
        out_specs=pl.BlockSpec((rhs, 2 * panels), lambda g, *_: (0, g)),
        scratch_shapes=[pltpu.VMEM((rhs, 3 * columns), BF16)],
    )
    return pl.pallas_call(
        near_kernel,
        grid_spec=grid_spec,
        out_shape=jax.ShapeDtypeStruct((rhs, columns), F32),
        compiler_params=params(12),
        cost_estimate=pl.CostEstimate(
            flops=2 * rhs * near_blocks.size,
            bytes_accessed=near_blocks.size * 2 + 7 * rhs * columns * 2,
            transcendentals=0,
        ),
        name="near",
    )(near_src.T, near_count, *[in_hbm(p) for p in pieces], in_hbm(near_blocks))


def far_kernel(
    halves, ours, theirs, pick, near, m2l_hbm, p2m_hbm, basis_hbm, image_ref, sums_ref, basis, *scratch
):
    recv, lhs, loc, both, m2l, p2m, sems = scratch
    moves = [
        pltpu.make_async_copy(source, target, sems.at[i])
        for i, (source, target) in enumerate(
            ((m2l_hbm, m2l), (p2m_hbm, p2m), (basis_hbm, basis))
        )
    ]
    for move in moves:
        move.start()
    leaves, panels, terms = p2m.shape
    classes = m2l.shape[0]
    blocks, rhs, columns = basis.shape
    part = rhs // halves
    group = 8
    rows = ours.shape[0]
    recv[:rows], recv[rows:] = ours[...], theirs[...]
    for h in range(halves):
        for j in range(0, part, group):
            got = dot(pick[h], recv[:, j * terms : (j + group) * terms]).astype(BF16)
            for t in range(group):
                base = (h * part + j + t) * leaves
                for c in range(classes):
                    lhs[base : base + leaves, c * terms : (c + 1) * terms] = got[
                        c * leaves : (c + 1) * leaves, t * terms : (t + 1) * terms
                    ]
    moves[0].wait()
    weights = m2l[...].reshape(classes * terms, terms)
    tall = 256
    for i in range(rhs * leaves // tall):
        got = dot(lhs[i * tall : (i + 1) * tall, :], weights)
        loc[i * tall // leaves : (i + 1) * tall // leaves] = got.reshape(
            tall // leaves, leaves, terms
        )
    moves[1].wait()
    for g in range(leaves):
        cols = slice(g * panels, (g + 1) * panels)
        image = near[:, cols] + dot_nt(loc[:, g, :].astype(BF16), p2m[g])
        image_ref[:, cols] = image
        both[:rhs, cols], both[rhs:, cols] = split_parts(image)
    moves[2].wait()
    inner = dot_nt(both[...], basis[...].reshape(blocks * rhs, columns))
    pack(inner[:rhs] + inner[rhs:], sums_ref)


def pack_sizes(rhs, wide, peers):
    rows = rhs * wide // 128 // peers
    return rows, -(-rows // 8) * 8


def pack(products, out_ref):
    peers, piece, lanes = out_ref.shape
    rhs, wide = products.shape
    rows, _ = pack_sizes(rhs, wide, peers)
    if rows < piece:
        out_ref[...] = jnp.zeros_like(out_ref)
    tall = jnp.concatenate(
        [products[:, i * lanes : (i + 1) * lanes] for i in range(wide // lanes)], axis=0
    )
    for p in range(peers):
        out_ref[p, :rows, :] = tall[p * rows : (p + 1) * rows]


def unpack(in_ref, rhs, wide):
    peers, _, lanes = in_ref.shape
    rows, _ = pack_sizes(rhs, wide, peers)
    tall = jnp.concatenate([in_ref[p, :rows, :] for p in range(peers)], axis=0)
    return jnp.concatenate(
        [tall[i * rhs : (i + 1) * rhs] for i in range(wide // lanes)], axis=1
    )


def far_field(ours, theirs, pick, m2l, p2m, near, basis, halves, peers):
    leaves, panels, terms = p2m.shape
    classes = m2l.shape[0]
    blocks, rhs, columns = basis.shape
    _, piece = pack_sizes(rhs, blocks * rhs, peers)
    args = (ours, theirs, pick, near)
    anywhere = pl.BlockSpec(memory_space=pl.ANY)
    return pl.pallas_call(
        functools.partial(far_kernel, halves),
        grid=(1,),
        out_shape=(
            jax.ShapeDtypeStruct((rhs, columns), F32),
            jax.ShapeDtypeStruct((peers, piece, 128), F32),
            pltpu.VMEM(basis.shape, BF16),
        ),
        in_specs=[whole(a.shape) for a in args] + [anywhere] * 3,
        out_specs=(
            whole((rhs, columns)),
            whole((peers, piece, 128)),
            pl.BlockSpec(memory_space=pltpu.VMEM),
        ),
        scratch_shapes=[
            pltpu.VMEM((2 * ours.shape[0], ours.shape[1]), BF16),
            pltpu.VMEM((rhs * leaves, classes * terms), BF16),
            pltpu.VMEM((rhs, leaves, terms), F32),
            pltpu.VMEM((2 * rhs, columns), BF16),
            pltpu.VMEM(m2l.shape, BF16),
            pltpu.VMEM(p2m.shape, BF16),
            pltpu.SemaphoreType.DMA((3,)),
        ],
        compiler_params=params(24),
        name="far",
    )(*args, in_hbm(m2l), in_hbm(p2m), in_hbm(basis))


def exchange(pieces, axes=AXES):
    return lax.all_to_all(pieces, axes, split_axis=0, concat_axis=0, tiled=True)


def add_kernel(in_ref, out_ref):
    total = jnp.sum(in_ref[...], axis=0)
    out_ref[...] = jnp.broadcast_to(total[None], out_ref.shape)


def added(pieces, copies):
    shape = (copies, *pieces.shape[1:])
    return pl.pallas_call(
        add_kernel,
        grid=(1,),
        out_shape=jax.ShapeDtypeStruct(shape, F32),
        in_specs=[whole(pieces.shape)],
        out_specs=whole(shape),
        compiler_params=params(4),
        name="add",
    )(pieces)


def resid_kernel(total_rows, sums, image, basis, resid_ref, gram_ref, proj_ref):
    blocks, rhs, columns = basis.shape
    wide = blocks * rhs
    proj = unpack(sums, rhs, wide) * (1.0 / total_rows)
    proj_ref[...] = proj.T
    coef = jnp.concatenate(split_parts(proj), axis=0)
    step = 1024
    for i in range(columns // step):
        cols = slice(i * step, (i + 1) * step)
        by_basis = dot(coef, basis[:, :, cols].reshape(wide, step))
        resid = image[:, cols] - (by_basis[:rhs] + by_basis[rhs:])
        resid_ref[:rhs, cols], resid_ref[rhs:, cols] = split_parts(resid)
    both = resid_ref[...]
    square = dot_nt(both, both)
    gram = square[:rhs, :rhs] + square[:rhs, rhs:] + square[rhs:, :rhs] + square[rhs:, rhs:]
    half = rhs // 2
    folded = jnp.concatenate([gram[:half], gram[half:]], axis=1) * (1.0 / total_rows)
    gram_ref[...] = folded


def residual(sums, basis, image, total_rows):
    blocks, rhs, columns = basis.shape
    args = (sums, image, basis)
    shapes = (
        jax.ShapeDtypeStruct((2 * rhs, columns), BF16),
        jax.ShapeDtypeStruct((rhs // 2, 2 * rhs), F32),
        jax.ShapeDtypeStruct((blocks * rhs, rhs), F32),
    )
    return pl.pallas_call(
        functools.partial(resid_kernel, total_rows),
        grid=(1,),
        out_shape=shapes,
        in_specs=[whole(a.shape) for a in args],
        out_specs=tuple(whole(s.shape) for s in shapes),
        compiler_params=params(24),
        name="residual",
    )(*args)


def factored(gram, done):
    size = gram.shape[0]
    rows = lax.broadcasted_iota(jnp.int32, (size, size), 0)
    cols = lax.broadcasted_iota(jnp.int32, (size, size), 1)
    both = jnp.concatenate([gram, (rows == cols).astype(F32)], axis=1)
    tiles = [both[8 * i : 8 * i + 8] for i in range(size // 8)]
    for j in range(0, size, 2):
        t, o = divmod(j, 8)
        first, second = tiles[t][o : o + 1], tiles[t][o + 1 : o + 2]
        a, b, c = first[:, j : j + 1], first[:, j + 1 : j + 2], second[:, j + 1 : j + 2]
        scale = 1.0 / (a * c - b * b)
        upper = (c * first - b * second) * scale
        lower = (a * second - b * first) * scale
        for i in range(t, size // 8):
            change = tiles[i][:, j : j + 1] * upper + tiles[i][:, j + 1 : j + 2] * lower
            tiles[i] = tiles[i] - change
        ratio = b / a
        done[j : j + 1, :] = first / jnp.sqrt(a)
        done[j + 1 : j + 2, :] = (second - ratio * first) / jnp.sqrt(c - ratio * b)
    both = done[...]
    return jnp.where(cols >= rows, both[:, :size], 0.0).T, both[:, size:]


def tail_kernel(grams, resid, next_ref, factor_ref, done):
    rhs = factor_ref.shape[0]
    columns = resid.shape[1]
    folded = jnp.sum(grams[...], axis=0)
    gram = jnp.concatenate([folded[:, :rhs], folded[:, rhs:]], axis=0)
    lower, inverse = factored(gram, done)
    factor_ref[...] = lower
    coef = jnp.concatenate(split_parts(inverse), axis=0)
    step = 1024
    for i in range(columns // step):
        cols = slice(i * step, (i + 1) * step)
        first = dot(coef, resid[:rhs, cols])
        second = dot(coef[:rhs], resid[rhs:, cols])
        next_ref[:, cols] = (first[:rhs] + first[rhs:] + second).astype(BF16)


def tail(grams, resid):
    rhs, columns = resid.shape[0] // 2, resid.shape[1]
    args = (grams, resid)
    shapes = (
        jax.ShapeDtypeStruct((rhs, columns), BF16),
        jax.ShapeDtypeStruct((rhs, rhs), F32),
    )
    return pl.pallas_call(
        tail_kernel,
        grid=(1,),
        out_shape=shapes,
        in_specs=[whole(a.shape) for a in args],
        out_specs=tuple(whole(s.shape) for s in shapes),
        scratch_shapes=[pltpu.VMEM((rhs, 2 * rhs), F32)],
        compiler_params=params(6),
        name="tail",
    )(*args)


def shards(
    basis, near_blocks, near_src, near_count, p2m, m2l, send_list, send_count, far_src, far_class
):
    blocks, rhs, columns = basis.shape
    leaves = near_src.shape[0]
    classes, terms, _ = m2l.shape
    devices, near_devices = lax.axis_size("gx"), lax.axis_size("lo")
    peers = 2 * devices * near_devices
    slots = send_list.shape[2]
    total_rows = columns * peers
    halves = 2
    side = lax.axis_index("hi")
    same_side = ("gx", "lo")

    payload = all_multipoles(basis, p2m, send_list[0].T, send_count, halves)
    flip = [(0, 1), (1, 0)]
    given = lax.ppermute(payload, "hi", flip)
    up = [(i, i + 1) for i in range(devices - 1)]
    down = [(j, i) for i, j in up]
    sender = far_src // slots
    place = sender // (2 * near_devices) * near_devices + sender % near_devices
    place = place + jnp.where(sender // near_devices % 2 == side, 0, peers // 2)
    place = place * slots + far_src % slots
    class_hot = (far_class[:, None, :] == jnp.arange(classes)[None, :, None]).astype(BF16)
    rows = jnp.arange(peers * slots * halves)[None, None, None, :]
    wanted = place[None, :, :, None] * halves + jnp.arange(halves)[:, None, None, None]
    source_hot = (wanted == rows).astype(BF16)
    pick = jnp.einsum("gce,hgef->hcgf", class_hot, source_hot, preferred_element_type=F32)
    pick = pick.astype(BF16).reshape(halves, classes * leaves, -1)

    given, pick = lax.optimization_barrier((given, pick))

    def choose(multipoles, flops):
        sizes = (leaves, slots, halves, rhs, peers // 2)
        return chosen_multipoles(side[None], multipoles, *sizes, flops)

    def give(chosen):
        got = exchange(chosen.reshape(peers // 2, slots * halves, -1), same_side)
        return got.reshape(chosen.shape)

    chosen, source = lax.optimization_barrier((choose(payload, 7 * 10**10), basis))
    ours = give(chosen)
    own = last_block(source)
    before, after = lax.ppermute(own, "gx", up), lax.ppermute(own, "gx", down)
    chosen, before, after = lax.optimization_barrier((choose(given, 7 * 10**9), before, after))
    theirs = give(chosen)

    near = near_field(near_src, near_count, (before, own, after), near_blocks)
    image, sums, basis_near = far_field(ours, theirs, pick, m2l, p2m, near, basis, halves, peers)
    sums = exchange(added(exchange(sums), peers))
    resid, gram, projections = residual(sums, basis_near, image, total_rows)
    pair = jnp.stack([gram, lax.ppermute(gram, "hi", flip)])
    grams = exchange(added(pair, peers // 2), same_side)
    next_block, factor = tail(grams, resid)
    return (next_block, projections.reshape(blocks, rhs, rhs), factor)


def solution(mesh):
    devices, segments = mesh.shape["gx"], mesh.shape["bulk"]
    mesh = jax.sharding.Mesh(mesh.devices.reshape(devices, 2, segments // 2), AXES)
    return jax.shard_map(
        shards,
        mesh=mesh,
        in_specs=(
            P(None, None, AXES),
            P(AXES, None, None, None),
            P(AXES, None),
            P(AXES),
            P(AXES, None, None),
            P(),
            P(AXES, None, None),
            P(AXES, None),
            P(AXES, None),
            P(AXES, None),
        ),
        out_specs=(P(None, AXES), P(), P()),
        check_vma=False,
    )
```

```python
import functools

import jax
import jax.numpy as jnp
from jax import lax
from jax.experimental import pallas as pl
from jax.experimental.pallas import tpu as pltpu
from jax.sharding import PartitionSpec as P

F32 = jnp.float32
BF16 = jnp.bfloat16
AXES = ("gx", "hi", "lo")
MIB = 1024 * 1024


def dot(a, b, dims=((1,), (0,)), precision=None):
    return lax.dot_general(a, b, (dims, ((), ())), precision=precision, preferred_element_type=F32)


def dot_nt(a, b, precision=None):
    return dot(a, b, ((1,), (1,)), precision)


def split_parts(values):
    upper = values.astype(BF16)
    lower = (values - upper.astype(F32)).astype(BF16)
    return (upper, lower)


def params(mib):
    return pltpu.CompilerParams(vmem_limit_bytes=mib * MIB)


def in_hbm(array):
    return pltpu.with_memory_space_constraint(array, pltpu.HBM)


def whole(shape):
    return pl.BlockSpec(shape, lambda *_: (0,) * len(shape))


def send_kernel(halves, x, p2m, listed, counts, out, scratch, lists):
    leaves, panels, terms = p2m.shape
    rhs = x.shape[1]
    part = rhs // halves
    slots, peers = listed.shape
    for g in range(leaves):
        mult = dot(x[0, :, g * panels : (g + 1) * panels], p2m[g])
        for h in range(halves):
            scratch[:, g * halves + h, :] = mult[h * part : (h + 1) * part]
    tall = leaves * halves
    for j in range(part):
        out[j * tall : (j + 1) * tall, :] = scratch[j].astype(BF16)
    lists[...] = jnp.zeros_like(lists)
    lists[:slots, :peers] = listed[...].astype(F32)
    lists[slots : slots + 1, :peers] = counts[...].astype(F32)
    out[part * tall :, :] = lists[...].astype(BF16)


def choose_kernel(halves, slots, leaves, near_devices, side, given, out):
    tall, terms = leaves * halves, given.shape[1]
    rows, part = out.shape[0], out.shape[1] // terms
    each = slots * halves
    receiver = lax.broadcasted_iota(jnp.int32, (rows, terms), 0) // each
    far_part, near_part = receiver // near_devices, receiver % near_devices
    device = far_part * (2 * near_devices) + side[0] * near_devices + near_part
    hot = (device == lax.broadcasted_iota(jnp.int32, (rows, terms), 1)).astype(F32).astype(BF16)
    spread = dot_nt(hot, given[part * tall :, :])
    row = lax.broadcasted_iota(jnp.int32, spread.shape, 0)
    lane = lax.broadcasted_iota(jnp.int32, spread.shape, 1)
    slot = row // halves % slots
    leaf = jnp.sum(jnp.where(lane == slot, spread, 0.0), axis=1, keepdims=True)
    live = jnp.sum(jnp.where(lane == slots, spread, 0.0), axis=1, keepdims=True)
    row = lax.broadcasted_iota(jnp.int32, (rows, tall), 0)
    lane = lax.broadcasted_iota(jnp.int32, (rows, tall), 1).astype(F32)
    held = (row // halves % slots).astype(F32) < live
    wanted = leaf * halves + (row % halves).astype(F32)
    chosen = ((lane == wanted) & held).astype(F32).astype(BF16)
    for j in range(part // 2):
        pair = [given[i * tall : (i + 1) * tall, :] for i in (2 * j, 2 * j + 1)]
        got = dot(chosen, jnp.concatenate(pair, axis=1))
        out[:, j * 2 * terms : (j + 1) * 2 * terms] = got.astype(BF16)


def all_multipoles(basis, p2m, listed, counts, halves):
    blocks, rhs, columns = basis.shape
    leaves, panels, terms = p2m.shape
    shape = (rhs * leaves + 16, terms)
    return pl.pallas_call(
        functools.partial(send_kernel, halves),
        grid=(1,),
        out_shape=jax.ShapeDtypeStruct(shape, BF16),
        in_specs=[
            pl.BlockSpec((1, rhs, columns), lambda i: (blocks - 1, 0, 0)),
            whole(p2m.shape),
            whole(listed.shape),
            whole(counts.shape),
        ],
        out_specs=whole(shape),
        scratch_shapes=[
            pltpu.VMEM((rhs // halves, leaves * halves, terms), F32),
            pltpu.VMEM((16, terms), F32),
        ],
        compiler_params=params(8),
        name="send",
    )(in_hbm(basis), in_hbm(p2m), in_hbm(listed), in_hbm(counts))


def copy_kernel(x, out):
    out[...] = x[0]


def last_block(basis):
    blocks, rhs, columns = basis.shape
    return pl.pallas_call(
        copy_kernel,
        grid=(1,),
        out_shape=jax.ShapeDtypeStruct((rhs, columns), BF16),
        in_specs=[pl.BlockSpec((1, rhs, columns), lambda i: (blocks - 1, 0, 0))],
        out_specs=whole((rhs, columns)),
        compiler_params=params(8),
        cost_estimate=pl.CostEstimate(flops=7 * 10**10, bytes_accessed=0, transcendentals=0),
        name="last_block",
    )(in_hbm(basis))


def chosen_multipoles(side, given, leaves, slots, halves, rhs, receivers, flops):
    terms = given.shape[1]
    shape = (receivers * slots * halves, rhs // halves * terms)
    return pl.pallas_call(
        functools.partial(choose_kernel, halves, slots, leaves, lax.axis_size("lo")),
        grid=(1,),
        out_shape=jax.ShapeDtypeStruct(shape, BF16),
        in_specs=[pl.BlockSpec(memory_space=pltpu.SMEM), whole(given.shape)],
        out_specs=whole(shape),
        compiler_params=params(8),
        cost_estimate=pl.CostEstimate(flops=flops, bytes_accessed=0, transcendentals=0),
        name="choose",
    )(side, given)


def near_kernel(src_ref, count_ref, *refs):
    pieces, (blocks_ref, out_ref, wide) = refs[:3], refs[3:]
    columns = pieces[0].shape[1]
    slots, panels = blocks_ref.shape[1], blocks_ref.shape[2]
    g = pl.program_id(0)

    @pl.when(g == 0)
    def _():
        for i, piece in enumerate(pieces):
            wide[:, i * columns : (i + 1) * columns] = piece[...]

    for i in range(blocks_ref.shape[0]):
        leaf = g * blocks_ref.shape[0] + i
        here = pl.ds(pl.multiple_of(columns + leaf * panels, panels), panels)
        total = [wide[:, here].astype(F32), 0.0]
        for k in range(slots):
            place = pl.multiple_of(src_ref[k, leaf] * panels, panels)
            source = wide[:, pl.ds(place, panels)]
            source = jnp.where(k < count_ref[leaf], source, jnp.zeros_like(source))
            total[k % 2] += dot_nt(source, blocks_ref[i, k])
        out_ref[:, i * panels : (i + 1) * panels] = total[0] + total[1]


def near_field(near_src, near_count, pieces, near_blocks):
    leaves, slots, panels, _ = near_blocks.shape
    rhs, columns = pieces[0].shape
    grid_spec = pltpu.PrefetchScalarGridSpec(
        num_scalar_prefetch=2,
        grid=(leaves // 2,),
        in_specs=[
            *[whole((rhs, columns))] * 3,
            pl.BlockSpec((2, slots, panels, panels), lambda g, *_: (g, 0, 0, 0)),
        ],
        out_specs=pl.BlockSpec((rhs, 2 * panels), lambda g, *_: (0, g)),
        scratch_shapes=[pltpu.VMEM((rhs, 3 * columns), BF16)],
    )
    return pl.pallas_call(
        near_kernel,
        grid_spec=grid_spec,
        out_shape=jax.ShapeDtypeStruct((rhs, columns), F32),
        compiler_params=params(12),
        cost_estimate=pl.CostEstimate(
            flops=2 * rhs * near_blocks.size,
            bytes_accessed=near_blocks.size * 2 + 7 * rhs * columns * 2,
            transcendentals=0,
        ),
        name="near",
    )(near_src.T, near_count, *[in_hbm(p) for p in pieces], in_hbm(near_blocks))


def far_kernel(
    halves, ours, theirs, pick, near, m2l_hbm, p2m_hbm, basis_hbm, image_ref, sums_ref, basis, *scratch
):
    recv, lhs, loc, both, m2l, p2m, sems = scratch
    moves = [
        pltpu.make_async_copy(source, target, sems.at[i])
        for i, (source, target) in enumerate(
            ((m2l_hbm, m2l), (p2m_hbm, p2m), (basis_hbm, basis))
        )
    ]
    for move in moves:
        move.start()
    leaves, panels, terms = p2m.shape
    classes = m2l.shape[0]
    blocks, rhs, columns = basis.shape
    part = rhs // halves
    group = 8
    rows = ours.shape[0]
    recv[:rows], recv[rows:] = ours[...], theirs[...]
    for h in range(halves):
        for j in range(0, part, group):
            got = dot(pick[h], recv[:, j * terms : (j + group) * terms]).astype(BF16)
            for t in range(group):
                base = (h * part + j + t) * leaves
                for c in range(classes):
                    lhs[base : base + leaves, c * terms : (c + 1) * terms] = got[
                        c * leaves : (c + 1) * leaves, t * terms : (t + 1) * terms
                    ]
    moves[0].wait()
    weights = m2l[...].reshape(classes * terms, terms)
    tall = 256
    for i in range(rhs * leaves // tall):
        got = dot(lhs[i * tall : (i + 1) * tall, :], weights)
        loc[i * tall // leaves : (i + 1) * tall // leaves] = got.reshape(
            tall // leaves, leaves, terms
        )
    moves[1].wait()
    for g in range(leaves):
        cols = slice(g * panels, (g + 1) * panels)
        image = near[:, cols] + dot_nt(loc[:, g, :].astype(BF16), p2m[g])
        image_ref[:, cols] = image
        both[:rhs, cols], both[rhs:, cols] = split_parts(image)
    moves[2].wait()
    inner = dot_nt(both[...], basis[...].reshape(blocks * rhs, columns))
    pack(inner[:rhs] + inner[rhs:], sums_ref)


def pack_sizes(rhs, wide, peers):
    rows = rhs * wide // 128 // peers
    return rows, -(-rows // 8) * 8


def pack(products, out_ref):
    peers, piece, lanes = out_ref.shape
    rhs, wide = products.shape
    rows, _ = pack_sizes(rhs, wide, peers)
    if rows < piece:
        out_ref[...] = jnp.zeros_like(out_ref)
    tall = jnp.concatenate(
        [products[:, i * lanes : (i + 1) * lanes] for i in range(wide // lanes)], axis=0
    )
    for p in range(peers):
        out_ref[p, :rows, :] = tall[p * rows : (p + 1) * rows]


def unpack(in_ref, rhs, wide):
    peers, _, lanes = in_ref.shape
    rows, _ = pack_sizes(rhs, wide, peers)
    tall = jnp.concatenate([in_ref[p, :rows, :] for p in range(peers)], axis=0)
    return jnp.concatenate(
        [tall[i * rhs : (i + 1) * rhs] for i in range(wide // lanes)], axis=1
    )


def far_field(ours, theirs, pick, m2l, p2m, near, basis, halves, peers):
    leaves, panels, terms = p2m.shape
    classes = m2l.shape[0]
    blocks, rhs, columns = basis.shape
    _, piece = pack_sizes(rhs, blocks * rhs, peers)
    args = (ours, theirs, pick, near)
    anywhere = pl.BlockSpec(memory_space=pl.ANY)
    return pl.pallas_call(
        functools.partial(far_kernel, halves),
        grid=(1,),
        out_shape=(
            jax.ShapeDtypeStruct((rhs, columns), F32),
            jax.ShapeDtypeStruct((peers, piece, 128), F32),
            pltpu.VMEM(basis.shape, BF16),
        ),
        in_specs=[whole(a.shape) for a in args] + [anywhere] * 3,
        out_specs=(
            whole((rhs, columns)),
            whole((peers, piece, 128)),
            pl.BlockSpec(memory_space=pltpu.VMEM),
        ),
        scratch_shapes=[
            pltpu.VMEM((2 * ours.shape[0], ours.shape[1]), BF16),
            pltpu.VMEM((rhs * leaves, classes * terms), BF16),
            pltpu.VMEM((rhs, leaves, terms), F32),
            pltpu.VMEM((2 * rhs, columns), BF16),
            pltpu.VMEM(m2l.shape, BF16),
            pltpu.VMEM(p2m.shape, BF16),
            pltpu.SemaphoreType.DMA((3,)),
        ],
        compiler_params=params(24),
        name="far",
    )(*args, in_hbm(m2l), in_hbm(p2m), in_hbm(basis))


def exchange(pieces, axes=AXES):
    return lax.all_to_all(pieces, axes, split_axis=0, concat_axis=0, tiled=True)


def add_kernel(in_ref, out_ref):
    total = jnp.sum(in_ref[...], axis=0)
    out_ref[...] = jnp.broadcast_to(total[None], out_ref.shape)


def added(pieces, copies):
    shape = (copies, *pieces.shape[1:])
    return pl.pallas_call(
        add_kernel,
        grid=(1,),
        out_shape=jax.ShapeDtypeStruct(shape, F32),
        in_specs=[whole(pieces.shape)],
        out_specs=whole(shape),
        compiler_params=params(4),
        name="add",
    )(pieces)


def resid_kernel(total_rows, sums, image, basis, resid_ref, gram_ref, proj_ref):
    blocks, rhs, columns = basis.shape
    wide = blocks * rhs
    proj = unpack(sums, rhs, wide) * (1.0 / total_rows)
    proj_ref[...] = proj.T
    coef = jnp.concatenate(split_parts(proj), axis=0)
    step = 1024
    for i in range(columns // step):
        cols = slice(i * step, (i + 1) * step)
        by_basis = dot(coef, basis[:, :, cols].reshape(wide, step))
        resid = image[:, cols] - (by_basis[:rhs] + by_basis[rhs:])
        resid_ref[:rhs, cols], resid_ref[rhs:, cols] = split_parts(resid)
    both = resid_ref[...]
    square = dot_nt(both, both)
    gram = square[:rhs, :rhs] + square[:rhs, rhs:] + square[rhs:, :rhs] + square[rhs:, rhs:]
    half = rhs // 2
    folded = jnp.concatenate([gram[:half], gram[half:]], axis=1) * (1.0 / total_rows)
    gram_ref[...] = folded


def residual(sums, basis, image, total_rows):
    blocks, rhs, columns = basis.shape
    args = (sums, image, basis)
    shapes = (
        jax.ShapeDtypeStruct((2 * rhs, columns), BF16),
        jax.ShapeDtypeStruct((rhs // 2, 2 * rhs), F32),
        jax.ShapeDtypeStruct((blocks * rhs, rhs), F32),
    )
    return pl.pallas_call(
        functools.partial(resid_kernel, total_rows),
        grid=(1,),
        out_shape=shapes,
        in_specs=[whole(a.shape) for a in args],
        out_specs=tuple(whole(s.shape) for s in shapes),
        compiler_params=params(24),
        name="residual",
    )(*args)


def factored(gram, done):
    size = gram.shape[0]
    rows = lax.broadcasted_iota(jnp.int32, (size, size), 0)
    cols = lax.broadcasted_iota(jnp.int32, (size, size), 1)
    both = jnp.concatenate([gram, (rows == cols).astype(F32)], axis=1)
    tiles = [both[8 * i : 8 * i + 8] for i in range(size // 8)]
    for j in range(0, size, 2):
        t, o = divmod(j, 8)
        first, second = tiles[t][o : o + 1], tiles[t][o + 1 : o + 2]
        a, b, c = first[:, j : j + 1], first[:, j + 1 : j + 2], second[:, j + 1 : j + 2]
        scale = 1.0 / (a * c - b * b)
        upper = (c * first - b * second) * scale
        lower = (a * second - b * first) * scale
        for i in range(t, size // 8):
            change = tiles[i][:, j : j + 1] * upper + tiles[i][:, j + 1 : j + 2] * lower
            tiles[i] = tiles[i] - change
        ratio = b / a
        done[j : j + 1, :] = first / jnp.sqrt(a)
        done[j + 1 : j + 2, :] = (second - ratio * first) / jnp.sqrt(c - ratio * b)
    both = done[...]
    return jnp.where(cols >= rows, both[:, :size], 0.0).T, both[:, size:]


def tail_kernel(grams, resid, next_ref, factor_ref, done):
    rhs = factor_ref.shape[0]
    columns = resid.shape[1]
    folded = jnp.sum(grams[...], axis=0)
    gram = jnp.concatenate([folded[:, :rhs], folded[:, rhs:]], axis=0)
    lower, inverse = factored(gram, done)
    factor_ref[...] = lower
    coef = jnp.concatenate(split_parts(inverse), axis=0)
    step = 1024
    for i in range(columns // step):
        cols = slice(i * step, (i + 1) * step)
        first = dot(coef, resid[:rhs, cols])
        second = dot(coef[:rhs], resid[rhs:, cols])
        next_ref[:, cols] = (first[:rhs] + first[rhs:] + second).astype(BF16)


def tail(grams, resid):
    rhs, columns = resid.shape[0] // 2, resid.shape[1]
    args = (grams, resid)
    shapes = (
        jax.ShapeDtypeStruct((rhs, columns), BF16),
        jax.ShapeDtypeStruct((rhs, rhs), F32),
    )
    return pl.pallas_call(
        tail_kernel,
        grid=(1,),
        out_shape=shapes,
        in_specs=[whole(a.shape) for a in args],
        out_specs=tuple(whole(s.shape) for s in shapes),
        scratch_shapes=[pltpu.VMEM((rhs, 2 * rhs), F32)],
        compiler_params=params(6),
        name="tail",
    )(*args)


def shards(
    basis, near_blocks, near_src, near_count, p2m, m2l, send_list, send_count, far_src, far_class
):
    blocks, rhs, columns = basis.shape
    leaves = near_src.shape[0]
    classes, terms, _ = m2l.shape
    devices, near_devices = lax.axis_size("gx"), lax.axis_size("lo")
    peers = 2 * devices * near_devices
    slots = send_list.shape[2]
    total_rows = columns * peers
    halves = 2
    side = lax.axis_index("hi")
    same_side = ("gx", "lo")

    payload = all_multipoles(basis, p2m, send_list[0].T, send_count, halves)
    flip = [(0, 1), (1, 0)]
    given = lax.ppermute(payload, "hi", flip)
    up = [(i, i + 1) for i in range(devices - 1)]
    down = [(j, i) for i, j in up]
    sender = far_src // slots
    place = sender // (2 * near_devices) * near_devices + sender % near_devices
    place = place + jnp.where(sender // near_devices % 2 == side, 0, peers // 2)
    place = place * slots + far_src % slots
    class_hot = (far_class[:, None, :] == jnp.arange(classes)[None, :, None]).astype(BF16)
    rows = jnp.arange(peers * slots * halves)[None, None, None, :]
    wanted = place[None, :, :, None] * halves + jnp.arange(halves)[:, None, None, None]
    source_hot = (wanted == rows).astype(BF16)
    pick = jnp.einsum("gce,hgef->hcgf", class_hot, source_hot, preferred_element_type=F32)
    pick = pick.astype(BF16).reshape(halves, classes * leaves, -1)

    given, pick = lax.optimization_barrier((given, pick))

    def choose(multipoles, flops):
        sizes = (leaves, slots, halves, rhs, peers // 2)
        return chosen_multipoles(side[None], multipoles, *sizes, flops)

    def give(chosen):
        got = exchange(chosen.reshape(peers // 2, slots * halves, -1), same_side)
        return got.reshape(chosen.shape)

    chosen, source = lax.optimization_barrier((choose(payload, 7 * 10**10), basis))
    ours = give(chosen)
    own = last_block(source)
    before, after = lax.ppermute(own, "gx", up), lax.ppermute(own, "gx", down)
    theirs = give(choose(given, 7 * 10**9))

    near = near_field(near_src, near_count, (before, own, after), near_blocks)
    image, sums, basis_near = far_field(ours, theirs, pick, m2l, p2m, near, basis, halves, peers)
    sums = exchange(added(exchange(sums), peers))
    resid, gram, projections = residual(sums, basis_near, image, total_rows)
    pair = jnp.stack([gram, lax.ppermute(gram, "hi", flip)])
    grams = exchange(added(pair, peers // 2), same_side)
    next_block, factor = tail(grams, resid)
    return (next_block, projections.reshape(blocks, rhs, rhs), factor)


def solution(mesh):
    devices, segments = mesh.shape["gx"], mesh.shape["bulk"]
    mesh = jax.sharding.Mesh(mesh.devices.reshape(devices, 2, segments // 2), AXES)
    return jax.shard_map(
        shards,
        mesh=mesh,
        in_specs=(
            P(None, None, AXES),
            P(AXES, None, None, None),
            P(AXES, None),
            P(AXES),
            P(AXES, None, None),
            P(),
            P(AXES, None, None),
            P(AXES, None),
            P(AXES, None),
            P(AXES, None),
        ),
        out_specs=(P(None, AXES), P(), P()),
        check_vma=False,
    )
```

```python
import functools

import jax
import jax.numpy as jnp
from jax import lax
from jax.experimental import pallas as pl
from jax.experimental.pallas import tpu as pltpu
from jax.sharding import PartitionSpec as P

F32 = jnp.float32
BF16 = jnp.bfloat16
AXES = ("gx", "hi", "lo")
MIB = 1024 * 1024


def dot(a, b, dims=((1,), (0,)), precision=None):
    return lax.dot_general(a, b, (dims, ((), ())), precision=precision, preferred_element_type=F32)


def dot_nt(a, b, precision=None):
    return dot(a, b, ((1,), (1,)), precision)


def split_parts(values):
    upper = values.astype(BF16)
    lower = (values - upper.astype(F32)).astype(BF16)
    return (upper, lower)


def params(mib):
    return pltpu.CompilerParams(vmem_limit_bytes=mib * MIB)


def in_hbm(array):
    return pltpu.with_memory_space_constraint(array, pltpu.HBM)


def whole(shape):
    return pl.BlockSpec(shape, lambda *_: (0,) * len(shape))


def send_kernel(halves, x, p2m, listed, counts, out, own, scratch, lists):
    leaves, panels, terms = p2m.shape
    rhs = x.shape[1]
    part = rhs // halves
    slots, peers = listed.shape
    own[...] = x[0]
    for g in range(leaves):
        mult = dot(x[0, :, g * panels : (g + 1) * panels], p2m[g])
        for h in range(halves):
            scratch[:, g * halves + h, :] = mult[h * part : (h + 1) * part]
    tall = leaves * halves
    for j in range(part):
        out[j * tall : (j + 1) * tall, :] = scratch[j].astype(BF16)
    lists[...] = jnp.zeros_like(lists)
    lists[:slots, :peers] = listed[...].astype(F32)
    lists[slots : slots + 1, :peers] = counts[...].astype(F32)
    out[part * tall :, :] = lists[...].astype(BF16)


def choose_kernel(halves, slots, leaves, near_devices, side, given, out):
    tall, terms = leaves * halves, given.shape[1]
    rows, part = out.shape[0], out.shape[1] // terms
    each = slots * halves
    receiver = lax.broadcasted_iota(jnp.int32, (rows, terms), 0) // each
    far_part, near_part = receiver // near_devices, receiver % near_devices
    device = far_part * (2 * near_devices) + side[0] * near_devices + near_part
    hot = (device == lax.broadcasted_iota(jnp.int32, (rows, terms), 1)).astype(F32).astype(BF16)
    spread = dot_nt(hot, given[part * tall :, :])
    row = lax.broadcasted_iota(jnp.int32, spread.shape, 0)
    lane = lax.broadcasted_iota(jnp.int32, spread.shape, 1)
    slot = row // halves % slots
    leaf = jnp.sum(jnp.where(lane == slot, spread, 0.0), axis=1, keepdims=True)
    live = jnp.sum(jnp.where(lane == slots, spread, 0.0), axis=1, keepdims=True)
    row = lax.broadcasted_iota(jnp.int32, (rows, tall), 0)
    lane = lax.broadcasted_iota(jnp.int32, (rows, tall), 1).astype(F32)
    held = (row // halves % slots).astype(F32) < live
    wanted = leaf * halves + (row % halves).astype(F32)
    chosen = ((lane == wanted) & held).astype(F32).astype(BF16)
    for j in range(part // 2):
        pair = [given[i * tall : (i + 1) * tall, :] for i in (2 * j, 2 * j + 1)]
        got = dot(chosen, jnp.concatenate(pair, axis=1))
        out[:, j * 2 * terms : (j + 1) * 2 * terms] = got.astype(BF16)


def all_multipoles(basis, p2m, listed, counts, halves):
    blocks, rhs, columns = basis.shape
    leaves, panels, terms = p2m.shape
    shapes = (
        jax.ShapeDtypeStruct((rhs * leaves + 16, terms), BF16),
        jax.ShapeDtypeStruct((rhs, columns), BF16),
    )
    return pl.pallas_call(
        functools.partial(send_kernel, halves),
        grid=(1,),
        out_shape=shapes,
        in_specs=[
            pl.BlockSpec((1, rhs, columns), lambda i: (blocks - 1, 0, 0)),
            whole(p2m.shape),
            whole(listed.shape),
            whole(counts.shape),
        ],
        out_specs=tuple(whole(s.shape) for s in shapes),
        scratch_shapes=[
            pltpu.VMEM((rhs // halves, leaves * halves, terms), F32),
            pltpu.VMEM((16, terms), F32),
        ],
        compiler_params=params(8),
        name="send",
    )(in_hbm(basis), in_hbm(p2m), in_hbm(listed), in_hbm(counts))


def chosen_multipoles(side, given, leaves, slots, halves, rhs, receivers):
    terms = given.shape[1]
    shape = (receivers * slots * halves, rhs // halves * terms)
    return pl.pallas_call(
        functools.partial(choose_kernel, halves, slots, leaves, lax.axis_size("lo")),
        grid=(1,),
        out_shape=jax.ShapeDtypeStruct(shape, BF16),
        in_specs=[pl.BlockSpec(memory_space=pltpu.SMEM), whole(given.shape)],
        out_specs=whole(shape),
        compiler_params=params(8),
        cost_estimate=pl.CostEstimate(flops=7 * 10**10, bytes_accessed=0, transcendentals=0),
        name="choose",
    )(side, given)


def near_kernel(src_ref, count_ref, *refs):
    pieces, (blocks_ref, out_ref, wide) = refs[:3], refs[3:]
    columns = pieces[0].shape[1]
    slots, panels = blocks_ref.shape[1], blocks_ref.shape[2]
    g = pl.program_id(0)

    @pl.when(g == 0)
    def _():
        for i, piece in enumerate(pieces):
            wide[:, i * columns : (i + 1) * columns] = piece[...]

    for i in range(blocks_ref.shape[0]):
        leaf = g * blocks_ref.shape[0] + i
        here = pl.ds(pl.multiple_of(columns + leaf * panels, panels), panels)
        total = [wide[:, here].astype(F32), 0.0]
        for k in range(slots):
            place = pl.multiple_of(src_ref[k, leaf] * panels, panels)
            source = wide[:, pl.ds(place, panels)]
            source = jnp.where(k < count_ref[leaf], source, jnp.zeros_like(source))
            total[k % 2] += dot_nt(source, blocks_ref[i, k])
        out_ref[:, i * panels : (i + 1) * panels] = total[0] + total[1]


def near_field(near_src, near_count, pieces, near_blocks):
    leaves, slots, panels, _ = near_blocks.shape
    rhs, columns = pieces[0].shape
    grid_spec = pltpu.PrefetchScalarGridSpec(
        num_scalar_prefetch=2,
        grid=(leaves // 2,),
        in_specs=[
            *[whole((rhs, columns))] * 3,
            pl.BlockSpec((2, slots, panels, panels), lambda g, *_: (g, 0, 0, 0)),
        ],
        out_specs=pl.BlockSpec((rhs, 2 * panels), lambda g, *_: (0, g)),
        scratch_shapes=[pltpu.VMEM((rhs, 3 * columns), BF16)],
    )
    return pl.pallas_call(
        near_kernel,
        grid_spec=grid_spec,
        out_shape=jax.ShapeDtypeStruct((rhs, columns), F32),
        compiler_params=params(12),
        cost_estimate=pl.CostEstimate(
            flops=2 * rhs * near_blocks.size,
            bytes_accessed=near_blocks.size * 2 + 7 * rhs * columns * 2,
            transcendentals=0,
        ),
        name="near",
    )(near_src.T, near_count, *[in_hbm(p) for p in pieces], in_hbm(near_blocks))


def far_kernel(
    halves, ours, theirs, pick, near, m2l_hbm, p2m_hbm, basis_hbm, image_ref, sums_ref, basis, *scratch
):
    recv, lhs, loc, both, m2l, p2m, sems = scratch
    moves = [
        pltpu.make_async_copy(source, target, sems.at[i])
        for i, (source, target) in enumerate(
            ((m2l_hbm, m2l), (p2m_hbm, p2m), (basis_hbm, basis))
        )
    ]
    for move in moves:
        move.start()
    leaves, panels, terms = p2m.shape
    classes = m2l.shape[0]
    blocks, rhs, columns = basis.shape
    part = rhs // halves
    group = 8
    rows = ours.shape[0]
    recv[:rows], recv[rows:] = ours[...], theirs[...]
    for h in range(halves):
        for j in range(0, part, group):
            got = dot(pick[h], recv[:, j * terms : (j + group) * terms]).astype(BF16)
            for t in range(group):
                base = (h * part + j + t) * leaves
                for c in range(classes):
                    lhs[base : base + leaves, c * terms : (c + 1) * terms] = got[
                        c * leaves : (c + 1) * leaves, t * terms : (t + 1) * terms
                    ]
    moves[0].wait()
    weights = m2l[...].reshape(classes * terms, terms)
    tall = 256
    for i in range(rhs * leaves // tall):
        got = dot(lhs[i * tall : (i + 1) * tall, :], weights)
        loc[i * tall // leaves : (i + 1) * tall // leaves] = got.reshape(
            tall // leaves, leaves, terms
        )
    moves[1].wait()
    for g in range(leaves):
        cols = slice(g * panels, (g + 1) * panels)
        image = near[:, cols] + dot_nt(loc[:, g, :].astype(BF16), p2m[g])
        image_ref[:, cols] = image
        both[:rhs, cols], both[rhs:, cols] = split_parts(image)
    moves[2].wait()
    inner = dot_nt(both[...], basis[...].reshape(blocks * rhs, columns))
    pack(inner[:rhs] + inner[rhs:], sums_ref)


def pack_sizes(rhs, wide, peers):
    rows = rhs * wide // 128 // peers
    return rows, -(-rows // 8) * 8


def pack(products, out_ref):
    peers, piece, lanes = out_ref.shape
    rhs, wide = products.shape
    rows, _ = pack_sizes(rhs, wide, peers)
    if rows < piece:
        out_ref[...] = jnp.zeros_like(out_ref)
    tall = jnp.concatenate(
        [products[:, i * lanes : (i + 1) * lanes] for i in range(wide // lanes)], axis=0
    )
    for p in range(peers):
        out_ref[p, :rows, :] = tall[p * rows : (p + 1) * rows]


def unpack(in_ref, rhs, wide):
    peers, _, lanes = in_ref.shape
    rows, _ = pack_sizes(rhs, wide, peers)
    tall = jnp.concatenate([in_ref[p, :rows, :] for p in range(peers)], axis=0)
    return jnp.concatenate(
        [tall[i * rhs : (i + 1) * rhs] for i in range(wide // lanes)], axis=1
    )


def far_field(ours, theirs, pick, m2l, p2m, near, basis, halves, peers):
    leaves, panels, terms = p2m.shape
    classes = m2l.shape[0]
    blocks, rhs, columns = basis.shape
    _, piece = pack_sizes(rhs, blocks * rhs, peers)
    args = (ours, theirs, pick, near)
    anywhere = pl.BlockSpec(memory_space=pl.ANY)
    return pl.pallas_call(
        functools.partial(far_kernel, halves),
        grid=(1,),
        out_shape=(
            jax.ShapeDtypeStruct((rhs, columns), F32),
            jax.ShapeDtypeStruct((peers, piece, 128), F32),
            pltpu.VMEM(basis.shape, BF16),
        ),
        in_specs=[whole(a.shape) for a in args] + [anywhere] * 3,
        out_specs=(
            whole((rhs, columns)),
            whole((peers, piece, 128)),
            pl.BlockSpec(memory_space=pltpu.VMEM),
        ),
        scratch_shapes=[
            pltpu.VMEM((2 * ours.shape[0], ours.shape[1]), BF16),
            pltpu.VMEM((rhs * leaves, classes * terms), BF16),
            pltpu.VMEM((rhs, leaves, terms), F32),
            pltpu.VMEM((2 * rhs, columns), BF16),
            pltpu.VMEM(m2l.shape, BF16),
            pltpu.VMEM(p2m.shape, BF16),
            pltpu.SemaphoreType.DMA((3,)),
        ],
        compiler_params=params(24),
        name="far",
    )(*args, in_hbm(m2l), in_hbm(p2m), in_hbm(basis))


def exchange(pieces, axes=AXES):
    return lax.all_to_all(pieces, axes, split_axis=0, concat_axis=0, tiled=True)


def add_kernel(in_ref, out_ref):
    total = jnp.sum(in_ref[...], axis=0)
    out_ref[...] = jnp.broadcast_to(total[None], out_ref.shape)


def added(pieces, copies):
    shape = (copies, *pieces.shape[1:])
    return pl.pallas_call(
        add_kernel,
        grid=(1,),
        out_shape=jax.ShapeDtypeStruct(shape, F32),
        in_specs=[whole(pieces.shape)],
        out_specs=whole(shape),
        compiler_params=params(4),
        name="add",
    )(pieces)


def resid_kernel(total_rows, sums, image, basis, resid_ref, gram_ref, proj_ref):
    blocks, rhs, columns = basis.shape
    wide = blocks * rhs
    proj = unpack(sums, rhs, wide) * (1.0 / total_rows)
    proj_ref[...] = proj.T
    coef = jnp.concatenate(split_parts(proj), axis=0)
    step = 1024
    for i in range(columns // step):
        cols = slice(i * step, (i + 1) * step)
        by_basis = dot(coef, basis[:, :, cols].reshape(wide, step))
        resid = image[:, cols] - (by_basis[:rhs] + by_basis[rhs:])
        resid_ref[:rhs, cols], resid_ref[rhs:, cols] = split_parts(resid)
    both = resid_ref[...]
    square = dot_nt(both, both)
    gram = square[:rhs, :rhs] + square[:rhs, rhs:] + square[rhs:, :rhs] + square[rhs:, rhs:]
    half = rhs // 2
    folded = jnp.concatenate([gram[:half], gram[half:]], axis=1) * (1.0 / total_rows)
    gram_ref[...] = folded


def residual(sums, basis, image, total_rows):
    blocks, rhs, columns = basis.shape
    args = (sums, image, basis)
    shapes = (
        jax.ShapeDtypeStruct((2 * rhs, columns), BF16),
        jax.ShapeDtypeStruct((rhs // 2, 2 * rhs), F32),
        jax.ShapeDtypeStruct((blocks * rhs, rhs), F32),
    )
    return pl.pallas_call(
        functools.partial(resid_kernel, total_rows),
        grid=(1,),
        out_shape=shapes,
        in_specs=[whole(a.shape) for a in args],
        out_specs=tuple(whole(s.shape) for s in shapes),
        compiler_params=params(24),
        name="residual",
    )(*args)


def factored(gram, done):
    size = gram.shape[0]
    rows = lax.broadcasted_iota(jnp.int32, (size, size), 0)
    cols = lax.broadcasted_iota(jnp.int32, (size, size), 1)
    both = jnp.concatenate([gram, (rows == cols).astype(F32)], axis=1)
    tiles = [both[8 * i : 8 * i + 8] for i in range(size // 8)]
    for j in range(0, size, 2):
        t, o = divmod(j, 8)
        first, second = tiles[t][o : o + 1], tiles[t][o + 1 : o + 2]
        a, b, c = first[:, j : j + 1], first[:, j + 1 : j + 2], second[:, j + 1 : j + 2]
        scale = 1.0 / (a * c - b * b)
        upper = (c * first - b * second) * scale
        lower = (a * second - b * first) * scale
        for i in range(t, size // 8):
            change = tiles[i][:, j : j + 1] * upper + tiles[i][:, j + 1 : j + 2] * lower
            tiles[i] = tiles[i] - change
        ratio = b / a
        done[j : j + 1, :] = first / jnp.sqrt(a)
        done[j + 1 : j + 2, :] = (second - ratio * first) / jnp.sqrt(c - ratio * b)
    both = done[...]
    return jnp.where(cols >= rows, both[:, :size], 0.0).T, both[:, size:]


def tail_kernel(grams, resid, next_ref, factor_ref, done):
    rhs = factor_ref.shape[0]
    columns = resid.shape[1]
    folded = jnp.sum(grams[...], axis=0)
    gram = jnp.concatenate([folded[:, :rhs], folded[:, rhs:]], axis=0)
    lower, inverse = factored(gram, done)
    factor_ref[...] = lower
    upper, lower = split_parts(inverse)
    left = jnp.concatenate([upper, lower], axis=0)
    right = jnp.concatenate([upper, jnp.zeros_like(upper)], axis=0)
    coef = jnp.concatenate([left, right], axis=1)
    step = 1024
    for i in range(columns // step):
        cols = slice(i * step, (i + 1) * step)
        both = dot(coef, resid[:, cols])
        next_ref[:, cols] = (both[:rhs] + both[rhs:]).astype(BF16)


def tail(grams, resid):
    rhs, columns = resid.shape[0] // 2, resid.shape[1]
    args = (grams, resid)
    shapes = (
        jax.ShapeDtypeStruct((rhs, columns), BF16),
        jax.ShapeDtypeStruct((rhs, rhs), F32),
    )
    return pl.pallas_call(
        tail_kernel,
        grid=(1,),
        out_shape=shapes,
        in_specs=[whole(a.shape) for a in args],
        out_specs=tuple(whole(s.shape) for s in shapes),
        scratch_shapes=[pltpu.VMEM((rhs, 2 * rhs), F32)],
        compiler_params=params(6),
        name="tail",
    )(*args)


def shards(
    basis, near_blocks, near_src, near_count, p2m, m2l, send_list, send_count, far_src, far_class
):
    blocks, rhs, columns = basis.shape
    leaves = near_src.shape[0]
    classes, terms, _ = m2l.shape
    devices, near_devices = lax.axis_size("gx"), lax.axis_size("lo")
    peers = 2 * devices * near_devices
    slots = send_list.shape[2]
    total_rows = columns * peers
    halves = 2
    side = lax.axis_index("hi")
    same_side = ("gx", "lo")

    payload, own = all_multipoles(basis, p2m, send_list[0].T, send_count, halves)
    flip = [(0, 1), (1, 0)]
    given = lax.ppermute(payload, "hi", flip)
    up = [(i, i + 1) for i in range(devices - 1)]
    down = [(j, i) for i, j in up]
    sender = far_src // slots
    place = sender // (2 * near_devices) * near_devices + sender % near_devices
    place = place + jnp.where(sender // near_devices % 2 == side, 0, peers // 2)
    place = place * slots + far_src % slots
    class_hot = (far_class[:, None, :] == jnp.arange(classes)[None, :, None]).astype(BF16)
    rows = jnp.arange(peers * slots * halves)[None, None, None, :]
    wanted = place[None, :, :, None] * halves + jnp.arange(halves)[:, None, None, None]
    source_hot = (wanted == rows).astype(BF16)
    pick = jnp.einsum("gce,hgef->hcgf", class_hot, source_hot, preferred_element_type=F32)
    pick = pick.astype(BF16).reshape(halves, classes * leaves, -1)

    given, pick = lax.optimization_barrier((given, pick))

    def choose(multipoles):
        return chosen_multipoles(side[None], multipoles, leaves, slots, halves, rhs, peers // 2)

    def give(chosen):
        got = exchange(chosen.reshape(peers // 2, slots * halves, -1), same_side)
        return got.reshape(chosen.shape)

    chosen, own = lax.optimization_barrier((choose(payload), own))
    ours = give(chosen)
    before, after = lax.ppermute(own, "gx", up), lax.ppermute(own, "gx", down)
    chosen, before, after = lax.optimization_barrier((choose(given), before, after))
    theirs = give(chosen)

    near = near_field(near_src, near_count, (before, own, after), near_blocks)
    image, sums, basis_near = far_field(ours, theirs, pick, m2l, p2m, near, basis, halves, peers)
    sums = exchange(added(exchange(sums), peers))
    resid, gram, projections = residual(sums, basis_near, image, total_rows)
    pair = jnp.stack([gram, lax.ppermute(gram, "hi", flip)])
    grams = exchange(added(pair, peers // 2), same_side)
    next_block, factor = tail(grams, resid)
    return (next_block, projections.reshape(blocks, rhs, rhs), factor)


def solution(mesh):
    devices, segments = mesh.shape["gx"], mesh.shape["bulk"]
    mesh = jax.sharding.Mesh(mesh.devices.reshape(devices, 2, segments // 2), AXES)
    return jax.shard_map(
        shards,
        mesh=mesh,
        in_specs=(
            P(None, None, AXES),
            P(AXES, None, None, None),
            P(AXES, None),
            P(AXES),
            P(AXES, None, None),
            P(),
            P(AXES, None, None),
            P(AXES, None),
            P(AXES, None),
            P(AXES, None),
        ),
        out_specs=(P(None, AXES), P(), P()),
        check_vma=False,
    )
```
